512 devices in a mesh: energy: 64 (over y, z), slab: 8 (over x, core).
Axes of the slice: x: 4, y: 4, z: 16, core: 2. Of those that a mesh axis runs over, the one named last changes fastest.
Arguments:
- energies: float32 [64], P('energy'), may hold values from -1 to 1
- onsite: float32 [8, 256], P('slab'), may hold values from -1.5 to 1.5
- hopping: float32 [2, 8, 256, 256], P(None, 'slab'), may hold values from -0.09375 to 0.09375
- coupling: float32 [2, 8, 64, 64], P(None, 'slab'), may hold values from -0.1875 to 0.1875
- injection: float32 [64, 8, 256], P('energy', 'slab'), may hold values from 0.004 to 0.04
- kernels: float32 [2, 2, 127], replicated, may hold values from -0.75 to 0.75
Outputs:
- sigma_retarded: float32 [2, 8, 64, 256, 256], P(None, 'slab', None, 'energy')
- sigma_lesser: float32 [2, 8, 64, 256, 256], P(None, 'slab', None, 'energy')
The draws below stay inside these ranges and needn't reach their ends.
All inputs are finite; a program needn't handle non-finite values.
Results may differ from the reference program's by a relative error of at most 0.0003.
Values sent between devices are 32-bit elements; how exact they have to be, the bound alone decides.
No kernel may reach another device: no remote copies, remote signals or barrier semaphores. Data moves between devices by JAX's collectives and lax.ppermute only.
A program may use at most 64 MiB of HBM per device.

```python
import math
import jax
import jax.numpy as jnp
from jax import lax

N = 256
W = 64
NE = 64
NS = 8
KLEN = 127


def block_scale(own_key, shape, cuts, smallest, largest):
    def one(dim, blocks):
        draws = jax.random.uniform(jax.random.fold_in(jax.random.fold_in(own_key, 6), dim), (blocks,), jnp.float32, smallest / len(cuts), largest / len(cuts))
        return jnp.repeat(jnp.exp(draws), shape[dim] // blocks).reshape((-1,) + (1,) * (len(shape) - dim - 1))

    level = one(*cuts[0])
    for cut in cuts[1:]:
        level = level * one(*cut)
    return level


def centred(key, dims, deviation, most, pieces=(), kind=jnp.bfloat16):
    level = block_scale(key, dims, pieces, -0.22, 0.18) if pieces else 1.0
    result = jax.random.normal(key, dims, jnp.float32) * deviation * level
    return jnp.minimum(jnp.maximum(result, -most), most).astype(kind)


def setup_inputs(seed: int = 0) -> dict:
    keys = jax.random.split(jax.random.key(seed), 7)
    return {
        "energies": jnp.clip(jax.random.uniform(keys[0], (NE,), jnp.float32, -1.0, 1.0) * block_scale(keys[0], (NE,), ((0, 64),), -0.4, 0.0), -1.0, 1.0),
        "onsite": jnp.clip(jax.random.uniform(keys[1], (NS, N), jnp.float32, -1.5, 1.5) * block_scale(keys[1], (NS, N), ((0, 8),), -0.4, 0.0), -1.5, 1.5),
        "hopping": centred(keys[2], (2, NS, N, N), (16 * N) ** -0.5, 0.09375, ((1, 8),), jnp.float32),
        "coupling": centred(keys[3], (2, NS, W, W), (16 * W) ** -0.5, 0.1875, ((1, 8),), jnp.float32),
        "injection": jnp.clip(jnp.exp(math.log(0.04) - 2.30258502 * jax.random.uniform(keys[4], (NE, NS, N), jnp.float32) ** block_scale(keys[4], (NE, NS, N), ((0, 64), (1, 8)), -0.2, 0.2)), 0.004, 0.04),
        "kernels": centred(keys[5], (2, 2, KLEN), NE ** -0.5, 0.75, (), jnp.float32),
    }


highest = lax.Precision.HIGHEST
damping = 0.02

def matmul_high(first_arg, second_arg):
    return jnp.matmul(first_arg, second_arg, precision=highest)

def complex_dot(first_pair, second_pair):
    real_part = matmul_high(first_pair[0], second_pair[0]) - matmul_high(first_pair[1], second_pair[1])
    imag_part = matmul_high(first_pair[0], second_pair[1]) + matmul_high(first_pair[1], second_pair[0])
    return (real_part, imag_part)

def adjoint(matrix_pair):
    return (jnp.swapaxes(matrix_pair[0], -1, -2), -jnp.swapaxes(matrix_pair[1], -1, -2))

def invert_block(system):
    orbitals = system[0].shape[-1]
    real_form = jnp.concatenate([jnp.concatenate([system[0], -system[1]], axis=-1), jnp.concatenate([system[1], system[0]], axis=-1)], axis=-2)
    identity = jnp.eye(orbitals, dtype=jnp.float32)
    stacked = jnp.concatenate([identity, jnp.zeros((orbitals, orbitals), jnp.float32)], axis=0)
    right_block = jnp.broadcast_to(stacked, real_form.shape[:-1] + (orbitals,))
    solved = jnp.linalg.solve(real_form, right_block)
    return (solved[..., :orbitals, :], solved[..., orbitals:, :])

def forward_slab(energy, onsite_row, hermit, couple, inject, prev_green, prev_lesser):
    orbitals = onsite_row.shape[-1]
    boundary = couple[0].shape[-1]
    sigma_ret = complex_dot(complex_dot(couple, prev_green), adjoint(couple))
    sigma_less = complex_dot(complex_dot(couple, prev_lesser), adjoint(couple))
    detune = energy[:, None] - onsite_row[None, :]
    identity = jnp.eye(orbitals, dtype=jnp.float32)
    padding = ((0, 0), (0, orbitals - boundary), (0, orbitals - boundary))
    system = (identity * detune[:, None, :] - hermit[0] - jnp.pad(sigma_ret[0], padding), identity * damping - hermit[1] - jnp.pad(sigma_ret[1], padding))
    green_block = invert_block(system)
    front_term = complex_dot((green_block[0][:, :, :boundary], green_block[1][:, :, :boundary]), sigma_less)
    widening = ((0, 0), (0, 0), (0, orbitals - boundary))
    scaled = (jnp.pad(front_term[0], widening) - green_block[1] * inject[:, None, :], jnp.pad(front_term[1], widening) + green_block[0] * inject[:, None, :])
    lesser = complex_dot(scaled, adjoint(green_block))
    return (green_block, lesser)

def backward_slab(green_block, lesser, m_ret, m_less):
    boundary = m_ret[0].shape[-1]
    back_col = (green_block[0][:, :, -boundary:], green_block[1][:, :, -boundary:])
    back_row = (green_block[0][:, -boundary:, :], green_block[1][:, -boundary:, :])
    less_row = (lesser[0][:, -boundary:, :], lesser[1][:, -boundary:, :])
    less_col = (lesser[0][:, :, -boundary:], lesser[1][:, :, -boundary:])
    through = complex_dot(back_col, m_ret)
    back_adj = adjoint(back_col)
    gain_term = complex_dot(through, back_row)
    full_green = (green_block[0] + gain_term[0], green_block[1] + gain_term[1])
    inflow = complex_dot(complex_dot(back_col, m_less), back_adj)
    mixed_one = complex_dot(through, less_row)
    mixed_two = complex_dot(complex_dot(less_col, adjoint(m_ret)), back_adj)
    full_lesser = (lesser[0] + inflow[0] - mixed_one[0] - mixed_two[0], lesser[1] + inflow[1] - mixed_one[1] - mixed_two[1])
    return (full_green, full_lesser)

def front_block(matrix_pair, couple):
    boundary = couple[0].shape[-1]
    corner = (matrix_pair[0][..., :boundary, :boundary], matrix_pair[1][..., :boundary, :boundary])
    return complex_dot(complex_dot(adjoint(couple), corner), couple)

def toeplitz_tables(kernels):
    total_count = (kernels.shape[-1] + 1) // 2
    offsets = jnp.arange(total_count)[:, None] - jnp.arange(total_count)[None, :] + total_count - 1
    return kernels[:, :, offsets]

def convolve_energy(table, piece):
    total_count = piece.shape[1]
    flat_piece = piece.reshape(2, total_count, -1)
    real_part = matmul_high(table[0], flat_piece[0]) - matmul_high(table[1], flat_piece[1])
    imag_part = matmul_high(table[0], flat_piece[1]) + matmul_high(table[1], flat_piece[0])
    return jnp.stack([real_part, imag_part]).reshape(piece.shape)

def reference(energies, onsite, hopping, coupling, injection, kernels):
    hermits = [((hopping[0, slab_index] + hopping[0, slab_index].T) * 0.5, (hopping[1, slab_index] - hopping[1, slab_index].T) * 0.5) for slab_index in range(NS)]
    identity_edge = jnp.eye(W, dtype=jnp.float32)[None]
    zeros_edge = jnp.zeros((1, W, W), jnp.float32)

    def one_energy(energy_item):
        energy, inject = energy_item
        energy_row = energy[None]
        prev_green = (zeros_edge, -identity_edge)
        prev_lesser = (zeros_edge, identity_edge)
        greens = []
        lessers = []
        for slab_index in range(NS):
            couple = (coupling[0, slab_index], coupling[1, slab_index])
            green_block, lesser = forward_slab(energy_row, onsite[slab_index], hermits[slab_index], couple, inject[slab_index][None], prev_green, prev_lesser)
            greens.append(green_block)
            lessers.append(lesser)
            prev_green = (green_block[0][:, -W:, -W:], green_block[1][:, -W:, -W:])
            prev_lesser = (lesser[0][:, -W:, -W:], lesser[1][:, -W:, -W:])
        m_ret = (zeros_edge, zeros_edge)
        m_less = (zeros_edge, zeros_edge)
        out_green = [None] * NS
        out_lesser = [None] * NS
        for slab_index in reversed(range(NS)):
            full_green, full_lesser = backward_slab(greens[slab_index], lessers[slab_index], m_ret, m_less)
            couple = (coupling[0, slab_index], coupling[1, slab_index])
            m_ret = front_block(full_green, couple)
            m_less = front_block(full_lesser, couple)
            out_green[slab_index] = jnp.stack(full_green)[:, 0]
            out_lesser[slab_index] = jnp.stack(full_lesser)[:, 0]
        return (jnp.stack(out_green, axis=1), jnp.stack(out_lesser, axis=1))
    all_green, all_lesser = lax.map(one_energy, (energies, injection))
    tables = toeplitz_tables(kernels)
    sigma_retarded = jnp.stack([convolve_energy(tables[0], jnp.transpose(all_green[:, :, slab_index], (1, 0, 2, 3))) for slab_index in range(NS)], axis=1)
    sigma_lesser = jnp.stack([convolve_energy(tables[1], jnp.transpose(all_lesser[:, :, slab_index], (1, 0, 2, 3))) for slab_index in range(NS)], axis=1)
    return (sigma_retarded, sigma_lesser)
```

```python
import functools

import jax
import jax.numpy as jnp
from jax import lax
from jax.experimental import pallas as pl
from jax.experimental.pallas import tpu as pltpu
from jax.sharding import PartitionSpec as P

ETA = 0.02
F32 = jnp.float32
BF16 = jnp.bfloat16
NN = (((1,), (0,)), ((), ()))
NT = (((1,), (1,)), ((), ()))


def mm(a, b, dims=NN):
    return lax.dot_general(a, b, dims, precision=lax.Precision.HIGHEST, preferred_element_type=F32)


def halves(x):
    high = x.astype(BF16)
    return high, (x - high.astype(F32)).astype(BF16)


def mm3(a, b):
    def one(x, y):
        return lax.dot_general(x, y, NN, preferred_element_type=F32)

    return one(a[0], b[0]) + (one(a[0], b[1]) + one(a[1], b[0]))


def cat(parts, axis):
    return jnp.concatenate(parts, axis=axis)


def blk(r, i):
    return cat([cat([r, -i], 1), cat([i, r], 1)], 0)


def pair(z):
    n = z.shape[1] // 2
    return z[:n, :n], -z[:n, n:]


def full(top):
    n = top.shape[0]
    return cat([top, cat([-top[:, n:], top[:, :n]], 1)], 0)


def eye(n):
    return (lax.broadcasted_iota(jnp.int32, (n, n), 0) == lax.broadcasted_iota(jnp.int32, (n, n), 1)).astype(F32)


def imag_eye(n):
    return blk(jnp.zeros((n, n), F32), eye(n))


def times_i(z):
    n = z.shape[0] // 2
    return cat([-z[n:], z[:n]], 0)


def inverses(mats):
    eyes = [eye(z.shape[0]) for z in mats]
    parts = [halves(z) for z in mats]
    scales, lows, guesses = [], [], []
    for z, zp, one in zip(mats, parts, eyes):
        zt = z.T
        w = mm3(zp, halves(zt))
        u = jnp.max(jnp.sum(jnp.abs(w), axis=1, keepdims=True))
        inv_u = 1.0 / u
        low = (ETA * ETA) * inv_u
        gain = 4.0 / ((1.0 + low) * (1.0 + low))
        r = (1.0 + low) * one - w * inv_u
        guesses.append((gain * inv_u) * mm3(halves(zt), halves(r)))
        lows.append(low * gain)

    def smallest(values):
        return functools.reduce(jnp.minimum, values)

    def cond(state):
        lows, _ = state
        return smallest(lows) < 0.999

    def step(state):
        lows, guesses = state
        new_lows, new_guesses = [], []
        for zp, one, low, x in zip(parts, eyes, lows, guesses):
            gain = 4.0 / ((1.0 + low) * (1.0 + low))
            xp = halves(x)
            r = (1.0 + low) * one - mm3(zp, xp)
            new_guesses.append(gain * mm3(xp, halves(r)))
            new_lows.append(low * gain)
        return tuple(new_lows), tuple(new_guesses)

    _, guesses = lax.while_loop(cond, step, (tuple(lows), tuple(guesses)))

    def polish(guesses):
        out, sizes = [], []
        for z, one, x in zip(mats, eyes, guesses):
            r = one - mm(z, x)
            out.append(x + mm3(halves(x), halves(r)))
            sizes.append(jnp.max(jnp.sum(jnp.abs(r), axis=1, keepdims=True)))
        return functools.reduce(jnp.maximum, sizes), tuple(out)

    size, guesses = polish(guesses)

    def again(state):
        count, size, _ = state
        return (size > 3e-3) & (count < 8)

    def more(state):
        count, _, guesses = state
        size, guesses = polish(guesses)
        return count + 1, size, guesses

    _, _, guesses = lax.while_loop(again, more, (jnp.int32(0), size, guesses))
    return guesses


def rolled(x, axis):
    n = x.shape[axis]
    if axis == 0:
        return cat([x[n - 64 :], x[: n - 64]], 0)
    return cat([x[:, n - 64 :], x[:, : n - 64]], 1)


def unrolled(x, axis):
    if axis == 0:
        return cat([x[64:], x[:64]], 0)
    return cat([x[:, 64:], x[:, :64]], 1)


def eliminate_body(energy, onsite, hop):
    h0 = rolled(rolled(hop[0], 0), 1)
    h1 = rolled(rolled(hop[1], 0), 1)
    on = rolled(onsite, 1)
    one = eye(256)
    ar = one * (energy - on) - (h0 + h0.T) * 0.5
    ai = one * ETA - (h1 - h1.T) * 0.5

    def part(rows, cols):
        return blk(ar[rows, cols], ai[rows, cols])

    b, i = slice(0, 128), slice(128, 256)
    (inner,) = inverses([part(i, i)])
    abi = part(b, i)
    y = mm(abi, inner)
    z = mm(inner, part(i, b))
    s = part(b, b) - mm(abi, z)
    return s, inner[:128], y, z[:128]


def corners(s):
    r, i = pair(s)
    lo, hi = slice(0, 64), slice(64, 128)
    return [[blk(r[p, q], i[p, q]) for q in (lo, hi)] for p in (lo, hi)]


def maps_body(slab, s, couple, couple_next):
    (bb, bf), (fb, ff) = corners(s)
    c = blk(couple[0], couple[1])
    cn = blk(couple_next[0], couple_next[1])
    ib, if_ = inverses([bb, ff])
    b = -mm(ib, bf)
    d = -mm(fb, ib)
    phi = ff + mm(d, bf)
    br = -mm(if_, fb)
    dr = -mm(bf, if_)
    psi = bb + mm(dr, fb)
    ie = imag_eye(64)
    ct = c.T
    cnt = cn.T
    left = [mm(mm(cn, ib), cnt), mm(cn, b), mm(d, cnt), phi]
    right = [mm(mm(ct, if_), c), mm(ct, br), mm(dr, c), psi]
    lead = [-mm(times_i(cn)[:], cnt), 0.0 * b, 0.0 * d, ie]
    last = slab == 7
    first = slab == 0
    left = [jnp.where(last, v, u) for u, v in zip(left, lead)]
    right = [jnp.where(first, v, u) for u, v in zip(right, [0.0 * b, 0.0 * b, 0.0 * d, ie])]
    raw = [ib, b, d, phi]
    return [u[:64] for u in left], [u[:64] for u in right], [u[:64] for u in raw]


def compose(outer, inner, phi_inv):
    a2, b2, d2, _ = outer
    a1, b1, d1, phi1 = inner
    pq = mm(phi_inv, cat([b1, d2], 1))
    quad = mm(cat([b2, d1], 0), pq)
    n = a1.shape[0]
    return [a2 + quad[:n, n:], quad[:n, :n], quad[n:, n:], phi1 - quad[n:, :n]]


def compose_body(lo, li, ro, ri):
    lo, li, ro, ri = [[full(u) for u in m] for m in (lo, li, ro, ri)]
    pl_, pr_ = inverses([lo[3] - li[0], ro[3] - ri[0]])
    left = compose(lo, li, pl_)
    right = compose(ro, ri, pr_)
    return [u[:64] for u in left], [u[:64] for u in right]


def close_body(lo, la, ro, ra, s, inner, y, z, raw):
    lo, ro = [[full(u) for u in m] for m in (lo, ro)]
    la, ra = full(la), full(ra)
    pl_, pr_ = inverses([lo[3] - la, ro[3] - ra])
    sig_l = lo[0] + mm(mm(lo[1], pl_), lo[2])
    sig_r = ro[0] + mm(mm(ro[1], pr_), ro[2])
    ib, b, d, phi = [full(u) for u in raw]
    lr, li = pair(sig_l)
    rr, ri = pair(sig_r)
    zero = jnp.zeros((64, 64), F32)

    def spread(x, w):
        return cat([cat([x, zero], 1), cat([zero, w], 1)], 0)

    closed = s - blk(spread(rr, lr), spread(ri, li))
    e_inv, big = inverses([phi - sig_l, closed])
    be = mm(b, e_inv)
    gfb = mm(e_inv, d)
    gbb = ib + mm(be, d)

    def joined(k):
        return cat([cat([pair(gbb)[k], pair(be)[k]], 1), cat([pair(gfb)[k], pair(e_inv)[k]], 1)], 0)

    small = cat([joined(0), -joined(1)], 1)
    return restore(big[:128], inner, y, z), small


def restore(top, inner, y, z):
    ty = mm(top, y)
    zt = mm(z, full(top))
    zty = mm(zt, y)
    low = inner + zty
    r = cat([cat([top[:, :128], -ty[:, :128]], 1), cat([-zt[:, :128], low[:, :128]], 1)], 0)
    i = cat([cat([-top[:, 128:], ty[:, 128:]], 1), cat([zt[:, 128:], -low[:, 128:]], 1)], 0)
    return r, i


def for_rows(r, i):
    r, i = [unrolled(unrolled(x, 0), 1).reshape(32, 8, 256) for x in (r, i)]
    upper = lax.broadcasted_iota(jnp.int32, (32, 8, 256), 1) < 4

    def swapped(x):
        return cat([x[:, 4:], x[:, :4]], 1)

    even = jnp.where(upper, r, swapped(i))
    odd = jnp.where(upper, swapped(r), i)
    return even, odd


def right_adj(lr, li, gr, gi):
    n = lr.shape[0]
    rows = cat([cat([lr, li], 1), cat([li, -lr], 1)], 0)
    out = mm(rows, cat([gr, gi], 1), NT)
    return out[:n], out[n:]


def lesser_parts_body(slab, fr, fi, small, inner, y, z, inject, couple, couple_next):
    gr, gi = restore(small, inner, y, z)
    hr, hi = 1.5 * gr - fr, 1.5 * gi - fi
    d = rolled(inject, 1)
    lr = cat([gr[:64], hr[64:128]], 0) * d
    li = cat([gi[:64], hi[64:128]], 0) * d
    mr, mi = right_adj(lr, li, gr[:128], gi[:128])
    c = blk(couple[0], couple[1])
    cn = blk(couple_next[0], couple_next[1])
    ct, cnt = c.T, cn.T
    w = mm(mm(cn, blk(-mi[:64, :64], mr[:64, :64])), cnt)
    w = jnp.where(slab == 7, mm(times_i(cn), cnt), w)
    q = mm(mm(ct, blk(-mi[64:, 64:], mr[64:, 64:])), c)
    q = q - q.T
    beta = mm(cn, blk(gr[:64, 64:128], gi[:64, 64:128]))
    left = mm(
        ct,
        cat(
            [
                blk(gr[64:128, 64:128], gi[64:128, 64:128]),
                blk(hr[64:128, 64:128], hi[64:128, 64:128]),
                blk(gr[64:128, :64], gi[64:128, :64]),
            ],
            1,
        ),
    )
    u, v, zz = left[:, :128], left[:, 128:256], left[:, 256:]
    return (gr, gi), [m[:64] for m in (w, q, beta, u, v, zz)]


def lesser_body(slab, parts, gr, gi, fr, fi, inject):
    sig = full(parts(7, 0))
    mine = sig
    sources = {}
    for t in range(8):
        if t:
            beta = full(parts(t - 1, 2))
            sig = full(parts(t - 1, 0)) + mm(mm(beta, sig), beta, NT)
            mine = jnp.where(slab == t, sig, mine)
            c = mm(mm(full(parts(t, 4)), sig), full(parts(t, 3)), NT)
            sources[t] = full(parts(t, 1)) + c - c.T
    back = jnp.zeros_like(sig)
    my_back = back
    for t in range(7, 0, -1):
        zz = full(parts(t, 5))
        back = sources[t] + mm(mm(zz, back), zz, NT)
        my_back = jnp.where(slab == t - 1, back, my_back)
    hr, hi = 1.5 * gr - fr, 1.5 * gi - fi
    d = rolled(inject, 1)
    right_r, right_i = pair(mine)
    back_r, back_i = pair(0.5 * my_back)

    def cols(xr, xi, m):
        out = mm(cat([xr, xi], 1), m)
        return out

    fm = cat([cat([right_r, right_i], 1), cat([-right_i, right_r], 1)], 0)
    bm = cat([cat([back_r, back_i], 1), cat([-back_i, back_r], 1)], 0)
    on_f = cols(hr[:, 64:128], hi[:, 64:128], fm)
    on_b = cols(gr[:, :64], gi[:, :64], bm)
    add_r = cat([on_b[:, :64], on_f[:, :64]], 1)
    add_i = cat([on_b[:, 64:], on_f[:, 64:]], 1)
    lr, li = -hi * d, hr * d
    lr = cat([lr[:, :128] + add_r, lr[:, 128:]], 1)
    li = cat([li[:, :128] + add_i, li[:, 128:]], 1)
    nr, ni = right_adj(lr, li, gr, gi)
    return nr - nr.T, ni + ni.T


VM = pl.BlockSpec(memory_space=pltpu.VMEM)
SM = pl.BlockSpec(memory_space=pltpu.SMEM)


def call(kernel, outs, specs, micros):
    return pl.pallas_call(
        kernel,
        out_shape=[jax.ShapeDtypeStruct(o, F32) for o in outs],
        in_specs=specs,
        out_specs=[VM] * len(outs),
        compiler_params=pltpu.CompilerParams(vmem_limit_bytes=40 * 2**20),
        cost_estimate=pl.CostEstimate(flops=int(micros * 1.1e9), bytes_accessed=1 << 20, transcendentals=0),
    )


def eliminate_kernel(energy, onsite, hop, s, inner, y, z):
    s[...], inner[...], y[...], z[...] = eliminate_body(energy[0], onsite[...], (hop[0, 0], hop[1, 0]))


def put(ref, values):
    for k, v in enumerate(values):
        ref[k] = v


def got(ref):
    return [ref[k] for k in range(4)]


def maps_kernel(slab, s, couple, couple_next, left, right, raw):
    l, r, w = maps_body(slab[0], s[...], (couple[0, 0], couple[1, 0]), (couple_next[0, 0], couple_next[1, 0]))
    put(left, l)
    put(right, r)
    put(raw, w)


def compose_kernel(lo, li, ro, ri, left, right):
    l, r = compose_body(got(lo), got(li), got(ro), got(ri))
    put(left, l)
    put(right, r)


def put_rows(ref, r, i):
    even, odd = for_rows(r, i)
    ref[:, 0] = even
    ref[:, 1] = odd


def close_kernel(lo, la, ro, ra, s, inner, y, z, raw, rows, whole, small):
    (r, i), sm = close_body(got(lo), la[...], got(ro), ra[...], s[...], inner[...], y[...], z[...], got(raw))
    put_rows(rows, r, i)
    whole[0] = r
    whole[1] = i
    small[...] = sm


def lesser_parts_kernel(slab, whole, small, inner, y, z, inject, couple, couple_next, g, parts):
    pair_, p = lesser_parts_body(
        slab[0],
        whole[0],
        whole[1],
        small[...],
        inner[...],
        y[...],
        z[...],
        inject[:, 0],
        (couple[0, 0], couple[1, 0]),
        (couple_next[0, 0], couple_next[1, 0]),
    )
    g[0] = pair_[0]
    g[1] = pair_[1]
    put(parts, p)


def lesser_kernel(slab, parts, g, whole, inject, rows):
    r, i = lesser_body(slab[0], lambda t, k: parts[t, k], g[0], g[1], whole[0], whole[1], inject[:, 0])
    put_rows(rows, r, i)


def convolve_kernel(table, piece, out):
    for j in range(4):
        x = cat([piece[:, j], piece[:, 4 + j]], 0)
        o = mm(table[...], x)
        out[0, 0, :, j] = o[:64]
        out[1, 0, :, j] = o[64:]


def tables_kernel(kern, out):
    for k in range(2):
        t = []
        for c in range(2):
            x = jnp.broadcast_to(kern[k, c : c + 1, :], (64, 128))
            t.append(pltpu.roll(x, 65, 1, stride=1, stride_axis=0)[:, :64])
        out[k] = blk(t[0], t[1])


def per_device(energies, onsite, hopping, coupling, injection, kernels):
    slab = lax.axis_index("slab").astype(jnp.int32).reshape(1)

    def shifted(x, k):
        return lax.ppermute(x, "slab", [(s, (s + k) % 8) for s in range(8)])

    couple_next = shifted(coupling, -1)
    reversed_kernels = jnp.pad(kernels[:, :, ::-1], ((0, 0), (0, 0), (0, 1)))
    (tables,) = call(tables_kernel, [(2, 128, 128)], [VM], 1)(reversed_kernels)
    m256, half = (256, 256), (128, 256)
    s, inner, y, z = call(eliminate_kernel, [m256, half, m256, half], [SM, VM, VM], 8)(energies, onsite, hopping)
    port = (4, 64, 128)
    left, right, raw = call(maps_kernel, [port] * 3, [SM] + [VM] * 3, 6)(slab, s, coupling, couple_next)
    pairs = call(compose_kernel, [port] * 2, [VM] * 4, 5)
    left2, right2 = pairs(shifted(left, 1), shifted(left, 2), shifted(right, -1), shifted(right, -2))
    left4, right4 = pairs(left2, shifted(left2, 2), right2, shifted(right2, -2))
    sent = (64, 8, 256)
    rows, whole, small = call(close_kernel, [(32, 2, 8, 256), (2, 256, 256), half], [VM] * 9, 12)(
        left4, shifted(left4[0], 4), right4, shifted(right4[0], -4), s, inner, y, z, raw
    )

    def to_rows(x):
        return lax.all_to_all(x.reshape(sent), "energy", split_axis=0, concat_axis=0, tiled=True)

    got_r = to_rows(rows)
    g, parts = call(lesser_parts_kernel, [(2, 256, 256), (6, 64, 128)], [SM] + [VM] * 8, 5)(
        slab, whole, small, inner, y, z, injection, coupling, couple_next
    )
    all_parts = lax.all_gather(parts, "slab")
    (rows_l,) = call(lesser_kernel, [(32, 2, 8, 256)], [SM] + [VM] * 4, 8)(slab, all_parts, g, whole, injection)
    got_l = to_rows(rows_l)
    conv = call(convolve_kernel, [(2, 1, 64, 4, 256)], [VM] * 2, 2)
    return conv(tables[0], got_r)[0], conv(tables[1], got_l)[0]


def solution(mesh):
    in_specs = (
        P("energy"),
        P("slab", None),
        P(None, "slab", None, None),
        P(None, "slab", None, None),
        P("energy", "slab", None),
        P(),
    )
    out_specs = (P(None, "slab", None, "energy", None), P(None, "slab", None, "energy", None))
    return jax.shard_map(per_device, mesh=mesh, in_specs=in_specs, out_specs=out_specs, check_vma=False)
```

```python
import functools

import jax
import jax.numpy as jnp
from jax import lax
from jax.experimental import pallas as pl
from jax.experimental.pallas import tpu as pltpu
from jax.sharding import PartitionSpec as P

ETA = 0.02
F32 = jnp.float32
BF16 = jnp.bfloat16
NN = (((1,), (0,)), ((), ()))
NT = (((1,), (1,)), ((), ()))


def mmh(a, b, dims=NN):
    return lax.dot_general(a, b, dims, precision=lax.Precision.HIGHEST, preferred_element_type=F32)


def halves(x):
    high = x.astype(BF16)
    return high, (x - high.astype(F32)).astype(BF16)


def mm1(a, b, dims=NN):
    return lax.dot_general(a, b, dims, preferred_element_type=F32)


def mm3(a, b, dims=NN):
    return mm1(a[0], b[0], dims) + (mm1(a[0], b[1], dims) + mm1(a[1], b[0], dims))


def mm(a, b, dims=NN):
    return mm3(halves(a), halves(b), dims)


def cat(parts, axis):
    return jnp.concatenate(parts, axis=axis)


def blk(r, i):
    return cat([cat([r, -i], 1), cat([i, r], 1)], 0)


def pair(z):
    n = z.shape[1] // 2
    return z[:n, :n], -z[:n, n:]


def full(top):
    n = top.shape[0]
    return cat([top, cat([-top[:, n:], top[:, :n]], 1)], 0)


def eye(n):
    return (lax.broadcasted_iota(jnp.int32, (n, n), 0) == lax.broadcasted_iota(jnp.int32, (n, n), 1)).astype(F32)


def imag_eye(n):
    return blk(jnp.zeros((n, n), F32), eye(n))


def times_i(z):
    n = z.shape[0] // 2
    return cat([-z[n:], z[:n]], 0)


def lowest(values):
    return functools.reduce(jnp.minimum, values)


def raised(low):
    return 4.0 / ((1.0 + low) * (1.0 + low))


def spread_of(residues):
    return functools.reduce(jnp.maximum, [jnp.sum(r * r) for r in residues])


def inverses(mats):
    n = len(mats)
    eyes = [eye(z.shape[0]) for z in mats]
    rounded = [z.astype(BF16) for z in mats]
    flipped = [z.T for z in mats]
    lows, scales, guesses = [], [], []
    for z, zt, one in zip(rounded, flipped, eyes):
        zt = zt.astype(BF16)
        w = mm1(z, zt)
        u = jnp.max(jnp.sum(jnp.abs(w), axis=1, keepdims=True)) * 1.01
        inv_u = 1.0 / u
        low = (ETA * ETA) * inv_u
        gain = raised(low)
        r = (1.0 + low) * one - w * inv_u
        guesses.append(((gain * inv_u) * mm1(zt, r.astype(BF16))).astype(BF16))
        lows.append(low * gain)
        scales.append(inv_u)

    def step(state):
        lows, guesses = state
        rs = [((1.0 + lows[k]) * eyes[k] - mm1(rounded[k], guesses[k])).astype(BF16) for k in range(n)]
        new = [(raised(lows[k]) * mm1(guesses[k], rs[k])).astype(BF16) for k in range(n)]
        return tuple(low * raised(low) for low in lows), tuple(new)

    _, guesses = lax.while_loop(lambda state: lowest(state[0]) < 0.95, step, (tuple(lows), tuple(guesses)))

    parts = [halves(z) for z in mats]
    better = []
    for k in range(n):
        x = guesses[k]
        r = eyes[k] - (mm1(parts[k][0], x) + mm1(parts[k][1], x))
        rh, rl = halves(r)
        better.append(x.astype(F32) + (mm1(x, rh) + mm1(x, rl)))

    def polish(xs):
        rs = [eyes[k] - mmh(mats[k], xs[k]) for k in range(n)]
        return spread_of(rs), tuple(xs[k] + mm1(xs[k].astype(BF16), rs[k].astype(BF16)) for k in range(n))

    size, better = polish(better)
    enough = 2.5e-5

    def restart():
        def careful(state):
            lows, xs = state
            new = []
            for k in range(n):
                xp = halves(xs[k])
                r = (1.0 + lows[k]) * eyes[k] - mm3(parts[k], xp)
                new.append(raised(lows[k]) * mm3(xp, halves(r)))
            return tuple(low * raised(low) for low in lows), tuple(new)

        start = tuple((ETA * ETA) * s for s in scales), tuple(zt * s for zt, s in zip(flipped, scales))
        _, xs = lax.while_loop(lambda state: lowest(state[0]) < 0.999, careful, start)

        def again(state):
            count, size, _ = state
            return (count < 8) & jnp.logical_not(size <= enough)

        def more(state):
            count, _, xs = state
            size, xs = polish(xs)
            return count + 1, size, xs

        size, xs = polish(xs)
        return lax.while_loop(again, more, (jnp.int32(0), size, xs))[2]

    return lax.cond(size <= enough, lambda: better, restart)


def rolled(x, axis):
    n = x.shape[axis]
    if axis == 0:
        return cat([x[n - 64 :], x[: n - 64]], 0)
    return cat([x[:, n - 64 :], x[:, : n - 64]], 1)


def unrolled(x, axis):
    if axis == 0:
        return cat([x[64:], x[:64]], 0)
    return cat([x[:, 64:], x[:, :64]], 1)


def eliminate_body(energy, onsite, hop):
    h0 = rolled(rolled(hop[0], 0), 1)
    h1 = rolled(rolled(hop[1], 0), 1)
    on = rolled(onsite, 1)
    one = eye(256)
    ar = one * (energy - on) - (h0 + h0.T) * 0.5
    ai = one * ETA - (h1 - h1.T) * 0.5

    def part(rows, cols):
        return blk(ar[rows, cols], ai[rows, cols])

    b, i = slice(0, 128), slice(128, 256)
    (inner,) = inverses([part(i, i)])
    abi = part(b, i)
    y = mm(abi, inner)
    z = mm(inner, part(i, b))
    s = part(b, b) - mm(abi, z)
    return s, inner[:128], y, z[:128]


def corners(s):
    r, i = pair(s)
    lo, hi = slice(0, 64), slice(64, 128)
    return [[blk(r[p, q], i[p, q]) for q in (lo, hi)] for p in (lo, hi)]


def maps_body(s, couple, next_top):
    (bb, bf), (fb, ff) = corners(s)
    c = blk(couple[0], couple[1])
    cn = full(next_top)
    ib, if_ = inverses([bb, ff])
    b = -mm(ib, bf)
    d = -mm(fb, ib)
    phi = ff + mm(d, bf)
    br = -mm(if_, fb)
    dr = -mm(bf, if_)
    psi = bb + mm(dr, fb)
    ct = c.T
    cnt = cn.T
    left = [mm(mm(cn, ib), cnt), mm(cn, b), mm(d, cnt), phi]
    right = [mm(mm(ct, if_), c), mm(ct, br), mm(dr, c), psi]
    raw = [ib, b, d, phi]
    return [u[:64] for u in left], [u[:64] for u in right], [u[:64] for u in raw]


def compose(outer, inner, phi_inv):
    a2, b2, d2, _ = outer
    a1, b1, d1, phi1 = inner
    pq = mm(phi_inv, cat([b1, d2], 1))
    quad = mm(cat([b2, d1], 0), pq)
    n = a1.shape[0]
    return [a2 + quad[:n, n:], quad[:n, :n], quad[n:, n:], phi1 - quad[n:, :n]]


def level(slots):
    phis = inverses([outer[3] - inner[0] for outer, inner in slots])
    return [[u[:64] for u in compose(o, i, p)] for (o, i), p in zip(slots, phis)]


def constant_map(value):
    zero = jnp.zeros_like(value)
    return [value, zero, zero, imag_eye(64)]


def choose(cond, one, other):
    return [jnp.where(cond, x, y) for x, y in zip(one, other)]


def tree_body(slab, lead_top, sent, put, get):
    none = constant_map(jnp.zeros((128, 128), F32))
    lead = full(lead_top)
    lead = constant_map(-times_i(mm(lead, lead, NT)))

    def wide(tops):
        return [full(u) for u in tops]

    lefts = (slab + 2) // 2

    def fetch(is_left, place):
        source = jnp.where(is_left, slab - 1 - place, slab + 1 + place)
        there = (source >= 0) & (source < 8)
        found = wide(sent(jnp.clip(source, 0, 7)))
        return choose(there, found, choose(source == -1, lead, none))

    slots = []
    for k in range(5):
        is_left = k < lefts
        place = 2 * jnp.where(is_left, k, k - lefts)
        slots.append((fetch(is_left, place), fetch(is_left, place + 1)))
    for k, m in enumerate(level(slots)):
        put(k, m)

    twos = (lefts + 1) // 2
    slots = []
    for k in range(3):
        is_left = k < twos
        outer = jnp.where(is_left, 2 * k, lefts + 2 * (k - twos))
        stop = jnp.where(is_left, lefts, 5)
        inner = choose(outer + 1 < stop, wide(get(jnp.minimum(outer + 1, 4))), none)
        slots.append((wide(get(outer)), inner))
    for k, m in enumerate(level(slots)):
        put(5 + k, m)

    slots = []
    for first, stop in ((0, twos), (twos, 3)):
        inner = choose(first + 1 < stop, wide(get(5 + jnp.minimum(first + 1, 2))), none)
        slots.append((wide(get(5 + first)), inner))
    phis = inverses([outer[3] - inner[0] for outer, inner in slots])
    return [o[0] + mm(mm(o[1], p), o[2]) for (o, _), p in zip(slots, phis)]


def close_body(sig_l, sig_r, s, inner, y, z, raw):
    ib, b, d, phi = [full(u) for u in raw]
    lr, li = pair(sig_l)
    rr, ri = pair(sig_r)
    zero = jnp.zeros((64, 64), F32)

    def spread(x, w):
        return cat([cat([x, zero], 1), cat([zero, w], 1)], 0)

    closed = s - blk(spread(rr, lr), spread(ri, li))
    e_inv, big = inverses([phi - sig_l, closed])
    be = mm(b, e_inv)
    gfb = mm(e_inv, d)
    gbb = ib + mm(be, d)

    def joined(k):
        return cat([cat([pair(gbb)[k], pair(be)[k]], 1), cat([pair(gfb)[k], pair(e_inv)[k]], 1)], 0)

    small = cat([joined(0), -joined(1)], 1)
    return restore(big[:128], inner, y, z), small


def restore(top, inner, y, z):
    ty = mm(top, y)
    zt = mm(z, full(top))
    zty = mm(zt, y)
    low = inner + zty
    r = cat([cat([top[:, :128], -ty[:, :128]], 1), cat([-zt[:, :128], low[:, :128]], 1)], 0)
    i = cat([cat([-top[:, 128:], ty[:, 128:]], 1), cat([zt[:, 128:], -low[:, 128:]], 1)], 0)
    return r, i


def for_rows(r, i):
    r, i = [unrolled(unrolled(x, 0), 1).reshape(32, 8, 256) for x in (r, i)]
    upper = lax.broadcasted_iota(jnp.int32, (32, 8, 256), 1) < 4

    def swapped(x):
        return cat([x[:, 4:], x[:, :4]], 1)

    even = jnp.where(upper, r, swapped(i))
    odd = jnp.where(upper, swapped(r), i)
    return even, odd


def right_adj(lr, li, gr, gi):
    n = lr.shape[0]
    rows = cat([cat([lr, li], 1), cat([li, -lr], 1)], 0)
    out = mm(rows, cat([gr, gi], 1), NT)
    return out[:n], out[n:]


def lesser_parts_body(fr, fi, small, inner, y, z, inject, couple, next_top):
    gr, gi = restore(small, inner, y, z)
    hr, hi = 1.5 * gr - fr, 1.5 * gi - fi
    d = rolled(inject, 1)
    lr = cat([gr[:64], hr[64:128]], 0) * d
    li = cat([gi[:64], hi[64:128]], 0) * d
    mr, mi = right_adj(lr, li, gr[:128], gi[:128])
    c = blk(couple[0], couple[1])
    cn = full(next_top)
    ct, cnt = c.T, cn.T
    w = mm(mm(cn, blk(-mi[:64, :64], mr[:64, :64])), cnt)
    w = (w - w.T) * 0.5
    q = mm(mm(ct, blk(-mi[64:, 64:], mr[64:, 64:])), c)
    q = q - q.T
    beta = mm(cn, blk(gr[:64, 64:128], gi[:64, 64:128]))
    left = mm(
        ct,
        cat(
            [
                blk(gr[64:128, 64:128], gi[64:128, 64:128]),
                blk(hr[64:128, 64:128], hi[64:128, 64:128]),
                blk(gr[64:128, :64], gi[64:128, :64]),
            ],
            1,
        ),
    )
    u, v, zz = left[:, :128], left[:, 128:256], left[:, 256:]
    return (gr, gi), [m[:64] for m in (w + times_i(q), beta, u, v, zz)]


def lesser_body(slab, lead_top, parts, gr, gi, fr, fi, inject):
    lead = full(lead_top)
    sig = times_i(mm(lead, lead, NT))
    mine = sig
    sources = {}
    packed = [full(parts(t, 0)) for t in range(8)]
    for t in range(8):
        if t:
            beta = full(parts(t - 1, 1))
            both = packed[t - 1]
            sig = (both - both.T) * 0.5 + mm(mm(beta, sig), beta, NT)
            mine = jnp.where(slab == t, sig, mine)
            c = mm(mm(full(parts(t, 3)), sig), full(parts(t, 2)), NT)
            sources[t] = c - c.T - times_i((packed[t] + packed[t].T) * 0.5)
    back = jnp.zeros_like(sig)
    my_back = back
    for t in range(7, 0, -1):
        zz = full(parts(t, 4))
        back = sources[t] + mm(mm(zz, back), zz, NT)
        my_back = jnp.where(slab == t - 1, back, my_back)
    hr, hi = 1.5 * gr - fr, 1.5 * gi - fi
    d = rolled(inject, 1)
    right_r, right_i = pair(mine)
    back_r, back_i = pair(0.5 * my_back)

    def cols(xr, xi, m):
        out = mm(cat([xr, xi], 1), m)
        return out

    fm = cat([cat([right_r, right_i], 1), cat([-right_i, right_r], 1)], 0)
    bm = cat([cat([back_r, back_i], 1), cat([-back_i, back_r], 1)], 0)
    on_f = cols(hr[:, 64:128], hi[:, 64:128], fm)
    on_b = cols(gr[:, :64], gi[:, :64], bm)
    add_r = cat([on_b[:, :64], on_f[:, :64]], 1)
    add_i = cat([on_b[:, 64:], on_f[:, 64:]], 1)
    lr, li = -hi * d, hr * d
    lr = cat([lr[:, :128] + add_r, lr[:, 128:]], 1)
    li = cat([li[:, :128] + add_i, li[:, 128:]], 1)
    nr, ni = right_adj(lr, li, gr, gi)
    return nr - nr.T, ni + ni.T


VM = pl.BlockSpec(memory_space=pltpu.VMEM)
SM = pl.BlockSpec(memory_space=pltpu.SMEM)


def call(kernel, outs, specs, micros, scratch=()):
    return pl.pallas_call(
        kernel,
        out_shape=[jax.ShapeDtypeStruct(o, F32) for o in outs],
        in_specs=specs,
        out_specs=[VM] * len(outs),
        scratch_shapes=list(scratch),
        compiler_params=pltpu.CompilerParams(vmem_limit_bytes=40 * 2**20),
        cost_estimate=pl.CostEstimate(flops=int(micros * 1.1e9), bytes_accessed=1 << 20, transcendentals=0),
    )


def eliminate_kernel(energy, onsite, hop, s, inner, y, z):
    s[...], inner[...], y[...], z[...] = eliminate_body(energy[0], onsite[...], (hop[0, 0], hop[1, 0]))


def put(ref, values):
    for k, v in enumerate(values):
        ref[k] = v


def maps_kernel(slab, s, couple, tops, sends, raw):
    me = slab[0]
    left, right, own = maps_body(s[...], (couple[0, 0], couple[1, 0]), tops[lax.rem(me + 1, 8)])
    put(raw, own)
    for t in range(8):
        put(sends.at[t], choose(me < t, left, right))


def put_rows(ref, r, i):
    even, odd = for_rows(r, i)
    ref[:, 0] = even
    ref[:, 1] = odd


def close_kernel(slab, tops, sent, s, inner, y, z, raw, rows, whole, small, kept):
    def load(ref):
        return lambda t: [ref[t, k] for k in range(4)]

    sig_l, sig_r = tree_body(slab[0], tops[0], load(sent), lambda k, m: put(kept.at[k], m), load(kept))
    (r, i), sm = close_body(sig_l, sig_r, s[...], inner[...], y[...], z[...], [raw[k] for k in range(4)])
    put_rows(rows, r, i)
    whole[0] = r
    whole[1] = i
    small[...] = sm


def lesser_parts_kernel(slab, whole, small, inner, y, z, inject, couple, tops, g, parts):
    pair_, p = lesser_parts_body(
        whole[0],
        whole[1],
        small[...],
        inner[...],
        y[...],
        z[...],
        inject[:, 0],
        (couple[0, 0], couple[1, 0]),
        tops[lax.rem(slab[0] + 1, 8)],
    )
    g[0] = pair_[0]
    g[1] = pair_[1]
    for t in range(8):
        put(parts.at[t], p)


def lesser_kernel(slab, tops, parts, g, whole, inject, rows):
    r, i = lesser_body(
        slab[0], tops[0], lambda t, k: parts[t, k], g[0], g[1], whole[0], whole[1], inject[:, 0]
    )
    put_rows(rows, r, i)


def convolve_kernel(table, piece, out):
    for j in range(4):
        x = cat([piece[:, j], piece[:, 4 + j]], 0)
        o = mm(table[...], x)
        out[0, 0, :, j] = o[:64]
        out[1, 0, :, j] = o[64:]


def tables_kernel(kern, out):
    for k in range(2):
        t = []
        for c in range(2):
            x = jnp.broadcast_to(kern[k, c : c + 1, :], (64, 128))
            t.append(pltpu.roll(x, 65, 1, stride=1, stride_axis=0)[:, :64])
        out[k] = blk(t[0], t[1])


def per_device(energies, onsite, hopping, coupling, injection, kernels):
    slab = lax.axis_index("slab").astype(jnp.int32).reshape(1)

    def swapped_over(x, axis):
        return lax.all_to_all(x, axis, split_axis=0, concat_axis=0, tiled=True)

    top = jnp.concatenate([coupling[0, 0], -coupling[1, 0]], axis=1)
    tops = swapped_over(jnp.broadcast_to(top, (8, 64, 128)), "slab")
    reversed_kernels = jnp.pad(kernels[:, :, ::-1], ((0, 0), (0, 0), (0, 1)))
    (tables,) = call(tables_kernel, [(2, 128, 128)], [VM], 1)(reversed_kernels)
    m256, half = (256, 256), (128, 256)
    s, inner, y, z = call(eliminate_kernel, [m256, half, m256, half], [SM, VM, VM], 8)(energies, onsite, hopping)
    sends, raw = call(maps_kernel, [(8, 4, 64, 128), (4, 64, 128)], [SM] + [VM] * 3, 6)(slab, s, coupling, tops)
    sent = swapped_over(sends, "slab")
    rows, whole, small = call(
        close_kernel,
        [(32, 2, 8, 256), (2, 256, 256), half],
        [SM] + [VM] * 7,
        25,
        [pltpu.VMEM((8, 4, 64, 128), F32)],
    )(slab, tops, sent, s, inner, y, z, raw)

    def to_rows(x):
        return swapped_over(x.reshape(64, 8, 256), "energy")

    got_r = to_rows(rows)
    g, parts = call(lesser_parts_kernel, [(2, 256, 256), (8, 5, 64, 128)], [SM] + [VM] * 8, 5)(
        slab, whole, small, inner, y, z, injection, coupling, tops
    )
    all_parts = swapped_over(parts, "slab")
    (rows_l,) = call(lesser_kernel, [(32, 2, 8, 256)], [SM] + [VM] * 5, 8)(
        slab, tops, all_parts, g, whole, injection
    )
    got_l = to_rows(rows_l)
    conv = call(convolve_kernel, [(2, 1, 64, 4, 256)], [VM] * 2, 2)
    return conv(tables[0], got_r)[0], conv(tables[1], got_l)[0]


def solution(mesh):
    in_specs = (
        P("energy"),
        P("slab", None),
        P(None, "slab", None, None),
        P(None, "slab", None, None),
        P("energy", "slab", None),
        P(),
    )
    out_specs = (P(None, "slab", None, "energy", None), P(None, "slab", None, "energy", None))
    return jax.shard_map(per_device, mesh=mesh, in_specs=in_specs, out_specs=out_specs, check_vma=False)
```

```python
import functools

import jax
import jax.numpy as jnp
from jax import lax
from jax.experimental import pallas as pl
from jax.experimental.pallas import tpu as pltpu
from jax.sharding import PartitionSpec as P

ETA = 0.02
F32 = jnp.float32
BF16 = jnp.bfloat16
NN = (((1,), (0,)), ((), ()))
NT = (((1,), (1,)), ((), ()))


def mmh(a, b, dims=NN):
    return lax.dot_general(a, b, dims, precision=lax.Precision.HIGHEST, preferred_element_type=F32)


def halves(x):
    high = x.astype(BF16)
    return high, (x - high.astype(F32)).astype(BF16)


def mm1(a, b, dims=NN):
    return lax.dot_general(a, b, dims, preferred_element_type=F32)


def mm3(a, b, dims=NN):
    return mm1(a[0], b[0], dims) + (mm1(a[0], b[1], dims) + mm1(a[1], b[0], dims))


def mm(a, b, dims=NN):
    return mm3(halves(a), halves(b), dims)


def cat(parts, axis):
    return jnp.concatenate(parts, axis=axis)


def blk(r, i):
    return cat([cat([r, -i], 1), cat([i, r], 1)], 0)


def pair(z):
    n = z.shape[1] // 2
    return z[:n, :n], -z[:n, n:]


def full(top):
    n = top.shape[0]
    return cat([top, cat([-top[:, n:], top[:, :n]], 1)], 0)


def eye(n):
    return (lax.broadcasted_iota(jnp.int32, (n, n), 0) == lax.broadcasted_iota(jnp.int32, (n, n), 1)).astype(F32)


def imag_eye(n):
    return blk(jnp.zeros((n, n), F32), eye(n))


def times_i(z):
    n = z.shape[0] // 2
    return cat([-z[n:], z[:n]], 0)


def lowest(values):
    return functools.reduce(jnp.minimum, values)


def scaled(low, floor):
    base = jnp.maximum(low, floor)
    shift = 1.0 + base
    gain = 4.0 / (shift * shift)
    return shift, gain, jnp.minimum(gain * low * (shift - low), gain * base)


def spread_of(residues):
    return functools.reduce(jnp.maximum, [jnp.sum(r * r) for r in residues])


def inverses(mats):
    n = len(mats)
    eyes = [eye(z.shape[0]) for z in mats]
    rounded = [z.astype(BF16) for z in mats]
    flipped = [z.T for z in mats]
    lows, scales, guesses = [], [], []
    for z, zt, one in zip(rounded, flipped, eyes):
        zt = zt.astype(BF16)
        w = mm1(z, zt)
        u = jnp.max(jnp.sum(jnp.abs(w), axis=1, keepdims=True)) * 1.01
        inv_u = 1.0 / u
        shift, gain, low = scaled((ETA * ETA) * inv_u, 0.05)
        r = shift * one - w * inv_u
        guesses.append(((gain * inv_u) * mm1(zt, r.astype(BF16))).astype(BF16))
        lows.append(low)
        scales.append(inv_u)

    def step(state):
        lows, guesses = state
        plans = [scaled(low, 0.05) for low in lows]
        rs = [(plans[k][0] * eyes[k] - mm1(rounded[k], guesses[k])).astype(BF16) for k in range(n)]
        new = [(plans[k][1] * mm1(guesses[k], rs[k])).astype(BF16) for k in range(n)]
        return tuple(p[2] for p in plans), tuple(new)

    _, guesses = lax.while_loop(lambda state: lowest(state[0]) < 0.98, step, (tuple(lows), tuple(guesses)))

    parts = [halves(z) for z in mats]
    better = []
    for k in range(n):
        x = guesses[k]
        r = eyes[k] - (mm1(parts[k][0], x) + mm1(parts[k][1], x))
        rh, rl = halves(r)
        better.append(x.astype(F32) + (mm1(x, rh) + mm1(x, rl)))

    def polish(xs):
        rs = [eyes[k] - mmh(mats[k], xs[k]) for k in range(n)]
        return spread_of(rs), tuple(xs[k] + mm1(xs[k].astype(BF16), rs[k].astype(BF16)) for k in range(n))

    size, better = polish(better)
    enough = 1e-4

    def repaired():
        near = size < 0.25

        def careful(state):
            lows, xs = state
            plans = [scaled(low, 1e-3) for low in lows]
            new = []
            for k in range(n):
                xp = halves(xs[k])
                r = plans[k][0] * eyes[k] - mm3(parts[k], xp)
                new.append(plans[k][1] * mm3(xp, halves(r)))
            return tuple(p[2] for p in plans), tuple(new)

        lows = tuple(jnp.where(near, 1.0, (ETA * ETA) * s) for s in scales)
        xs = tuple(jnp.where(near, x, zt * s) for x, zt, s in zip(better, flipped, scales))
        _, xs = lax.while_loop(lambda state: lowest(state[0]) < 0.999, careful, (lows, xs))

        def again(state):
            count, size, _ = state
            return (count < 8) & jnp.logical_not(size <= enough)

        def more(state):
            count, _, xs = state
            size, xs = polish(xs)
            return count + 1, size, xs

        first, xs = polish(xs)
        return lax.while_loop(again, more, (jnp.int32(0), first, xs))[2]

    return lax.cond(size <= enough, lambda: better, repaired)


def rolled(x, axis):
    n = x.shape[axis]
    if axis == 0:
        return cat([x[n - 64 :], x[: n - 64]], 0)
    return cat([x[:, n - 64 :], x[:, : n - 64]], 1)


def unrolled(x, axis):
    if axis == 0:
        return cat([x[64:], x[:64]], 0)
    return cat([x[:, 64:], x[:, :64]], 1)


def eliminate_body(energy, onsite, hop):
    h0 = rolled(rolled(hop[0], 0), 1)
    h1 = rolled(rolled(hop[1], 0), 1)
    on = rolled(onsite, 1)
    one = eye(256)
    ar = one * (energy - on) - (h0 + h0.T) * 0.5
    ai = one * ETA - (h1 - h1.T) * 0.5

    def part(rows, cols):
        return blk(ar[rows, cols], ai[rows, cols])

    b, i = slice(0, 128), slice(128, 256)
    (inner,) = inverses([part(i, i)])
    abi = part(b, i)
    y = mm(abi, inner)
    z = mm(inner, part(i, b))
    s = part(b, b) - mm(abi, z)
    return s, inner[:128], y, z[:128]


def corners(s):
    r, i = pair(s)
    lo, hi = slice(0, 64), slice(64, 128)
    return [[blk(r[p, q], i[p, q]) for q in (lo, hi)] for p in (lo, hi)]


def maps_body(s, couple, next_top):
    (bb, bf), (fb, ff) = corners(s)
    c = blk(couple[0], couple[1])
    cn = full(next_top)
    ib, if_ = inverses([bb, ff])
    b = -mm(ib, bf)
    d = -mm(fb, ib)
    phi = ff + mm(d, bf)
    br = -mm(if_, fb)
    dr = -mm(bf, if_)
    psi = bb + mm(dr, fb)
    ct = c.T
    cnt = cn.T
    left = [mm(mm(cn, ib), cnt), mm(cn, b), mm(d, cnt), phi]
    right = [mm(mm(ct, if_), c), mm(ct, br), mm(dr, c), psi]
    raw = [ib, b, d, phi]
    return [u[:64] for u in left], [u[:64] for u in right], [u[:64] for u in raw]


def compose(outer, inner, phi_inv):
    a2, b2, d2, _ = outer
    a1, b1, d1, phi1 = inner
    pq = mm(phi_inv, cat([b1, d2], 1))
    quad = mm(cat([b2, d1], 0), pq)
    n = a1.shape[0]
    return [a2 + quad[:n, n:], quad[:n, :n], quad[n:, n:], phi1 - quad[n:, :n]]


def level(slots):
    phis = inverses([outer[3] - inner[0] for outer, inner in slots])
    return [[u[:64] for u in compose(o, i, p)] for (o, i), p in zip(slots, phis)]


def constant_map(value):
    zero = jnp.zeros_like(value)
    return [value, zero, zero, imag_eye(64)]


def choose(cond, one, other):
    return [jnp.where(cond, x, y) for x, y in zip(one, other)]


def tree_body(slab, lead_top, sent, put, get):
    none = constant_map(jnp.zeros((128, 128), F32))
    lead = full(lead_top)
    lead = constant_map(-times_i(mm(lead, lead, NT)))

    def wide(tops):
        return [full(u) for u in tops]

    lefts = (slab + 2) // 2

    def fetch(is_left, place):
        source = jnp.where(is_left, slab - 1 - place, slab + 1 + place)
        there = (source >= 0) & (source < 8)
        found = wide(sent(jnp.clip(source, 0, 7)))
        return choose(there, found, choose(source == -1, lead, none))

    slots = []
    for k in range(5):
        is_left = k < lefts
        place = 2 * jnp.where(is_left, k, k - lefts)
        slots.append((fetch(is_left, place), fetch(is_left, place + 1)))
    for k, m in enumerate(level(slots)):
        put(k, m)

    twos = (lefts + 1) // 2
    slots = []
    for k in range(3):
        is_left = k < twos
        outer = jnp.where(is_left, 2 * k, lefts + 2 * (k - twos))
        stop = jnp.where(is_left, lefts, 5)
        inner = choose(outer + 1 < stop, wide(get(jnp.minimum(outer + 1, 4))), none)
        slots.append((wide(get(outer)), inner))
    for k, m in enumerate(level(slots)):
        put(5 + k, m)

    slots = []
    for first, stop in ((0, twos), (twos, 3)):
        inner = choose(first + 1 < stop, wide(get(5 + jnp.minimum(first + 1, 2))), none)
        slots.append((wide(get(5 + first)), inner))
    phis = inverses([outer[3] - inner[0] for outer, inner in slots])
    return [o[0] + mm(mm(o[1], p), o[2]) for (o, _), p in zip(slots, phis)]


def close_body(sig_l, sig_r, s, inner, y, z, raw):
    ib, b, d, phi = [full(u) for u in raw]
    lr, li = pair(sig_l)
    rr, ri = pair(sig_r)
    zero = jnp.zeros((64, 64), F32)

    def spread(x, w):
        return cat([cat([x, zero], 1), cat([zero, w], 1)], 0)

    closed = s - blk(spread(rr, lr), spread(ri, li))
    e_inv, big = inverses([phi - sig_l, closed])
    be = mm(b, e_inv)
    gfb = mm(e_inv, d)
    gbb = ib + mm(be, d)

    def joined(k):
        return cat([cat([pair(gbb)[k], pair(be)[k]], 1), cat([pair(gfb)[k], pair(e_inv)[k]], 1)], 0)

    small = cat([joined(0), -joined(1)], 1)
    return restore(big[:128], inner, y, z), small


def restore(top, inner, y, z):
    ty = mm(top, y)
    zt = mm(z, full(top))
    zty = mm(zt, y)
    low = inner + zty
    r = cat([cat([top[:, :128], -ty[:, :128]], 1), cat([-zt[:, :128], low[:, :128]], 1)], 0)
    i = cat([cat([-top[:, 128:], ty[:, 128:]], 1), cat([zt[:, 128:], -low[:, 128:]], 1)], 0)
    return r, i


def for_rows(r, i):
    r, i = [unrolled(unrolled(x, 0), 1).reshape(32, 8, 256) for x in (r, i)]
    upper = lax.broadcasted_iota(jnp.int32, (32, 8, 256), 1) < 4

    def swapped(x):
        return cat([x[:, 4:], x[:, :4]], 1)

    even = jnp.where(upper, r, swapped(i))
    odd = jnp.where(upper, swapped(r), i)
    return even, odd


def right_adj(lr, li, gr, gi):
    n = lr.shape[0]
    rows = cat([cat([lr, li], 1), cat([li, -lr], 1)], 0)
    out = mm(rows, cat([gr, gi], 1), NT)
    return out[:n], out[n:]


def lesser_parts_body(fr, fi, small, inner, y, z, inject, couple, next_top):
    gr, gi = restore(small, inner, y, z)
    hr, hi = 1.5 * gr - fr, 1.5 * gi - fi
    d = rolled(inject, 1)
    lr = cat([gr[:64], hr[64:128]], 0) * d
    li = cat([gi[:64], hi[64:128]], 0) * d
    mr, mi = right_adj(lr, li, gr[:128], gi[:128])
    c = blk(couple[0], couple[1])
    cn = full(next_top)
    ct, cnt = c.T, cn.T
    w = mm(mm(cn, blk(-mi[:64, :64], mr[:64, :64])), cnt)
    w = (w - w.T) * 0.5
    q = mm(mm(ct, blk(-mi[64:, 64:], mr[64:, 64:])), c)
    q = q - q.T
    beta = mm(cn, blk(gr[:64, 64:128], gi[:64, 64:128]))
    left = mm(
        ct,
        cat(
            [
                blk(gr[64:128, 64:128], gi[64:128, 64:128]),
                blk(hr[64:128, 64:128], hi[64:128, 64:128]),
                blk(gr[64:128, :64], gi[64:128, :64]),
            ],
            1,
        ),
    )
    u, v, zz = left[:, :128], left[:, 128:256], left[:, 256:]
    return (gr, gi), [m[:64] for m in (w + times_i(q), beta, u, v, zz)]


def lesser_body(slab, lead_top, parts, gr, gi, fr, fi, inject):
    lead = full(lead_top)
    sig = times_i(mm(lead, lead, NT))
    mine = sig
    sources = {}
    packed = [full(parts(t, 0)) for t in range(8)]
    for t in range(8):
        if t:
            beta = full(parts(t - 1, 1))
            both = packed[t - 1]
            sig = (both - both.T) * 0.5 + mm(mm(beta, sig), beta, NT)
            mine = jnp.where(slab == t, sig, mine)
            c = mm(mm(full(parts(t, 3)), sig), full(parts(t, 2)), NT)
            sources[t] = c - c.T - times_i((packed[t] + packed[t].T) * 0.5)
    back = jnp.zeros_like(sig)
    my_back = back
    for t in range(7, 0, -1):
        zz = full(parts(t, 4))
        back = sources[t] + mm(mm(zz, back), zz, NT)
        my_back = jnp.where(slab == t - 1, back, my_back)
    hr, hi = 1.5 * gr - fr, 1.5 * gi - fi
    d = rolled(inject, 1)
    right_r, right_i = pair(mine)
    back_r, back_i = pair(0.5 * my_back)

    def cols(xr, xi, m):
        out = mm(cat([xr, xi], 1), m)
        return out

    fm = cat([cat([right_r, right_i], 1), cat([-right_i, right_r], 1)], 0)
    bm = cat([cat([back_r, back_i], 1), cat([-back_i, back_r], 1)], 0)
    on_f = cols(hr[:, 64:128], hi[:, 64:128], fm)
    on_b = cols(gr[:, :64], gi[:, :64], bm)
    add_r = cat([on_b[:, :64], on_f[:, :64]], 1)
    add_i = cat([on_b[:, 64:], on_f[:, 64:]], 1)
    lr, li = -hi * d, hr * d
    lr = cat([lr[:, :128] + add_r, lr[:, 128:]], 1)
    li = cat([li[:, :128] + add_i, li[:, 128:]], 1)
    nr, ni = right_adj(lr, li, gr, gi)
    return nr - nr.T, ni + ni.T


VM = pl.BlockSpec(memory_space=pltpu.VMEM)
SM = pl.BlockSpec(memory_space=pltpu.SMEM)


def call(kernel, outs, specs, micros, scratch=()):
    return pl.pallas_call(
        kernel,
        out_shape=[jax.ShapeDtypeStruct(o, F32) for o in outs],
        in_specs=specs,
        out_specs=[VM] * len(outs),
        scratch_shapes=list(scratch),
        compiler_params=pltpu.CompilerParams(vmem_limit_bytes=40 * 2**20),
        cost_estimate=pl.CostEstimate(flops=int(micros * 1.1e9), bytes_accessed=1 << 20, transcendentals=0),
    )


def eliminate_kernel(energy, onsite, hop, s, inner, y, z):
    s[...], inner[...], y[...], z[...] = eliminate_body(energy[0], onsite[...], (hop[0, 0], hop[1, 0]))


def put(ref, values):
    for k, v in enumerate(values):
        ref[k] = v


def maps_kernel(slab, s, couple, tops, sends, raw):
    me = slab[0]
    left, right, own = maps_body(s[...], (couple[0, 0], couple[1, 0]), tops[lax.rem(me + 1, 8)])
    put(raw, own)
    for t in range(8):
        put(sends.at[t], choose(me < t, left, right))


def put_rows(ref, r, i):
    even, odd = for_rows(r, i)
    ref[:, 0] = even
    ref[:, 1] = odd


def put_rows_by_z(ref, r, i):
    for k, x in enumerate(for_rows(r, i)):
        x = x.reshape(4, 8, 8, 256)
        for y in range(4):
            ref[:, k, y] = x[y]


def close_kernel(slab, tops, sent, s, inner, y, z, raw, rows, whole, small, kept):
    def load(ref):
        return lambda t: [ref[t, k] for k in range(4)]

    sig_l, sig_r = tree_body(slab[0], tops[0], load(sent), lambda k, m: put(kept.at[k], m), load(kept))
    (r, i), sm = close_body(sig_l, sig_r, s[...], inner[...], y[...], z[...], [raw[k] for k in range(4)])
    put_rows(rows, r, i)
    whole[0] = r
    whole[1] = i
    small[...] = sm


def lesser_parts_kernel(slab, whole, small, inner, y, z, inject, couple, tops, g, parts):
    pair_, p = lesser_parts_body(
        whole[0],
        whole[1],
        small[...],
        inner[...],
        y[...],
        z[...],
        inject[:, 0],
        (couple[0, 0], couple[1, 0]),
        tops[lax.rem(slab[0] + 1, 8)],
    )
    g[0] = pair_[0]
    g[1] = pair_[1]
    put(parts, p)


def lesser_kernel(slab, tops, parts, g, whole, inject, rows):
    r, i = lesser_body(
        slab[0], tops[0], lambda t, k: parts[t, k], g[0], g[1], whole[0], whole[1], inject[:, 0]
    )
    put_rows_by_z(rows, r, i)


def convolve_kernel(table, piece, out):
    for j in range(4):
        x = cat([piece[:, j], piece[:, 4 + j]], 0)
        o = mm(table[...], x)
        out[0, 0, :, j] = o[:64]
        out[1, 0, :, j] = o[64:]


def tables_kernel(kern, out):
    for k in range(2):
        t = []
        for c in range(2):
            x = jnp.broadcast_to(kern[k, c : c + 1, :], (64, 128))
            t.append(pltpu.roll(x, 65, 1, stride=1, stride_axis=0)[:, :64])
        out[k] = blk(t[0], t[1])


def per_device(energies, onsite, hopping, coupling, injection, kernels):
    slab = lax.axis_index("slab").astype(jnp.int32).reshape(1)

    def swapped_over(x, axis, groups=None):
        return lax.all_to_all(x, axis, split_axis=0, concat_axis=0, tiled=True, axis_index_groups=groups)

    def to_rows_in_stages(x):
        along_z = [[16 * y + z for z in range(16)] for y in range(4)]
        along_y = [[16 * y + z for y in range(4)] for z in range(16)]
        x = swapped_over(x.reshape(16, 4 * 8, 256), "energy", along_z)
        x = jnp.swapaxes(x.reshape(16, 4, 8, 256), 0, 1)
        return swapped_over(x.reshape(4, 16 * 8, 256), "energy", along_y).reshape(64, 8, 256)

    top = jnp.concatenate([coupling[0, 0], -coupling[1, 0]], axis=1)
    tops = swapped_over(jnp.broadcast_to(top, (8, 64, 128)), "slab")
    reversed_kernels = jnp.pad(kernels[:, :, ::-1], ((0, 0), (0, 0), (0, 1)))
    (tables,) = call(tables_kernel, [(2, 128, 128)], [VM], 1)(reversed_kernels)
    m256, half = (256, 256), (128, 256)
    s, inner, y, z = call(eliminate_kernel, [m256, half, m256, half], [SM, VM, VM], 8)(energies, onsite, hopping)
    sends, raw = call(maps_kernel, [(8, 4, 64, 128), (4, 64, 128)], [SM] + [VM] * 3, 6)(slab, s, coupling, tops)
    sent = swapped_over(sends, "slab")
    rows, whole, small = call(
        close_kernel,
        [(32, 2, 8, 256), (2, 256, 256), half],
        [SM] + [VM] * 7,
        25,
        [pltpu.VMEM((8, 4, 64, 128), F32)],
    )(slab, tops, sent, s, inner, y, z, raw)

    def to_rows(x):
        return swapped_over(x.reshape(64, 8, 256), "energy")

    got_r = to_rows(rows)
    g, parts = call(lesser_parts_kernel, [(2, 256, 256), (5, 64, 128)], [SM] + [VM] * 8, 3)(
        slab, whole, small, inner, y, z, injection, coupling, tops
    )
    all_parts = lax.all_gather(parts, "slab")
    (rows_l,) = call(lesser_kernel, [(8, 2, 4, 8, 256)], [SM] + [VM] * 5, 8)(
        slab, tops, all_parts, g, whole, injection
    )
    got_l = to_rows_in_stages(rows_l)
    conv = call(convolve_kernel, [(2, 1, 64, 4, 256)], [VM] * 2, 2)
    return conv(tables[0], got_r)[0], conv(tables[1], got_l)[0]


def solution(mesh):
    in_specs = (
        P("energy"),
        P("slab", None),
        P(None, "slab", None, None),
        P(None, "slab", None, None),
        P("energy", "slab", None),
        P(),
    )
    out_specs = (P(None, "slab", None, "energy", None), P(None, "slab", None, "energy", None))
    return jax.shard_map(per_device, mesh=mesh, in_specs=in_specs, out_specs=out_specs, check_vma=False)
```

```python
import functools

import jax
import jax.numpy as jnp
from jax import lax
from jax.experimental import pallas as pl
from jax.experimental.pallas import tpu as pltpu
from jax.sharding import PartitionSpec as P

ETA = 0.02
F32 = jnp.float32
BF16 = jnp.bfloat16
NN = (((1,), (0,)), ((), ()))
NT = (((1,), (1,)), ((), ()))


def mmh(a, b, dims=NN):
    return lax.dot_general(a, b, dims, precision=lax.Precision.HIGHEST, preferred_element_type=F32)


def halves(x):
    high = x.astype(BF16)
    return high, (x - high.astype(F32)).astype(BF16)


def mm1(a, b, dims=NN):
    return lax.dot_general(a, b, dims, preferred_element_type=F32)


def mm3(a, b, dims=NN):
    return mm1(a[0], b[0], dims) + (mm1(a[0], b[1], dims) + mm1(a[1], b[0], dims))


def mm(a, b, dims=NN):
    return mm3(halves(a), halves(b), dims)


def cat(parts, axis):
    return jnp.concatenate(parts, axis=axis)


def blk(r, i):
    return cat([cat([r, -i], 1), cat([i, r], 1)], 0)


def pair(z):
    n = z.shape[1] // 2
    return z[:n, :n], -z[:n, n:]


def full(top):
    n = top.shape[0]
    return cat([top, cat([-top[:, n:], top[:, :n]], 1)], 0)


def eye(n):
    return (lax.broadcasted_iota(jnp.int32, (n, n), 0) == lax.broadcasted_iota(jnp.int32, (n, n), 1)).astype(F32)


def imag_eye(n):
    return blk(jnp.zeros((n, n), F32), eye(n))


def times_i(z):
    n = z.shape[0] // 2
    return cat([-z[n:], z[:n]], 0)


def lowest(values):
    return functools.reduce(jnp.minimum, values)


def scaled(low, floor):
    base = jnp.maximum(low, floor)
    shift = 1.0 + base
    gain = 4.0 / (shift * shift)
    return shift, gain, jnp.minimum(gain * low * (shift - low), gain * base)


def spread_of(residues):
    return functools.reduce(jnp.maximum, [jnp.sum(r * r) for r in residues])


def inverses(mats):
    n = len(mats)
    eyes = [eye(z.shape[0]) for z in mats]
    rounded = [z.astype(BF16) for z in mats]
    flipped = [z.T for z in mats]
    lows, scales, guesses = [], [], []
    for z, zt, one in zip(rounded, flipped, eyes):
        zt = zt.astype(BF16)
        w = mm1(z, zt)
        u = jnp.max(jnp.sum(jnp.abs(w), axis=1, keepdims=True)) * 1.01
        inv_u = 1.0 / u
        shift, gain, low = scaled((ETA * ETA) * inv_u, 0.05)
        r = shift * one - w * inv_u
        guesses.append(((gain * inv_u) * mm1(zt, r.astype(BF16))).astype(BF16))
        lows.append(low)
        scales.append(inv_u)

    def step(state):
        lows, guesses = state
        plans = [scaled(low, 0.05) for low in lows]
        rs = [(plans[k][0] * eyes[k] - mm1(rounded[k], guesses[k])).astype(BF16) for k in range(n)]
        new = [(plans[k][1] * mm1(guesses[k], rs[k])).astype(BF16) for k in range(n)]
        return tuple(p[2] for p in plans), tuple(new)

    _, guesses = lax.while_loop(lambda state: lowest(state[0]) < 0.98, step, (tuple(lows), tuple(guesses)))

    parts = [halves(z) for z in mats]
    better = []
    for k in range(n):
        x = guesses[k]
        r = eyes[k] - (mm1(parts[k][0], x) + mm1(parts[k][1], x))
        rh, rl = halves(r)
        better.append(x.astype(F32) + (mm1(x, rh) + mm1(x, rl)))

    def polish(xs):
        rs = [eyes[k] - mmh(mats[k], xs[k]) for k in range(n)]
        return spread_of(rs), tuple(xs[k] + mm1(xs[k].astype(BF16), rs[k].astype(BF16)) for k in range(n))

    size, better = polish(better)
    enough = 1e-4

    def repaired():
        near = size < 0.25

        def careful(state):
            lows, xs = state
            plans = [scaled(low, 1e-3) for low in lows]
            new = []
            for k in range(n):
                xp = halves(xs[k])
                r = plans[k][0] * eyes[k] - mm3(parts[k], xp)
                new.append(plans[k][1] * mm3(xp, halves(r)))
            return tuple(p[2] for p in plans), tuple(new)

        lows = tuple(jnp.where(near, 1.0, (ETA * ETA) * s) for s in scales)
        xs = tuple(jnp.where(near, x, zt * s) for x, zt, s in zip(better, flipped, scales))
        _, xs = lax.while_loop(lambda state: lowest(state[0]) < 0.999, careful, (lows, xs))

        def again(state):
            count, size, _ = state
            return (count < 8) & jnp.logical_not(size <= enough)

        def more(state):
            count, _, xs = state
            size, xs = polish(xs)
            return count + 1, size, xs

        first, xs = polish(xs)
        return lax.while_loop(again, more, (jnp.int32(0), first, xs))[2]

    return lax.cond(size <= enough, lambda: better, repaired)


def rolled(x, axis):
    n = x.shape[axis]
    if axis == 0:
        return cat([x[n - 64 :], x[: n - 64]], 0)
    return cat([x[:, n - 64 :], x[:, : n - 64]], 1)


def unrolled(x, axis):
    if axis == 0:
        return cat([x[64:], x[:64]], 0)
    return cat([x[:, 64:], x[:, :64]], 1)


def eliminate_body(energy, onsite, hop):
    h0 = rolled(rolled(hop[0], 0), 1)
    h1 = rolled(rolled(hop[1], 0), 1)
    on = rolled(onsite, 1)
    one = eye(256)
    ar = one * (energy - on) - (h0 + h0.T) * 0.5
    ai = one * ETA - (h1 - h1.T) * 0.5

    def part(rows, cols):
        return blk(ar[rows, cols], ai[rows, cols])

    b, i = slice(0, 128), slice(128, 256)
    (inner,) = inverses([part(i, i)])
    abi = part(b, i)
    y = mm(abi, inner)
    z = mm(inner, part(i, b))
    s = part(b, b) - mm(abi, z)
    return s, inner[:128], y, z[:128]


def corners(s):
    r, i = pair(s)
    lo, hi = slice(0, 64), slice(64, 128)
    return [[blk(r[p, q], i[p, q]) for q in (lo, hi)] for p in (lo, hi)]


def maps_body(s, couple, next_top):
    (bb, bf), (fb, ff) = corners(s)
    c = blk(couple[0], couple[1])
    cn = full(next_top)
    ib, if_ = inverses([bb, ff])
    b = -mm(ib, bf)
    d = -mm(fb, ib)
    phi = ff + mm(d, bf)
    br = -mm(if_, fb)
    dr = -mm(bf, if_)
    psi = bb + mm(dr, fb)
    ct = c.T
    cnt = cn.T
    left = [mm(mm(cn, ib), cnt), mm(cn, b), mm(d, cnt), phi]
    right = [mm(mm(ct, if_), c), mm(ct, br), mm(dr, c), psi]
    raw = [ib, b, d, phi]
    return [u[:64] for u in left], [u[:64] for u in right], [u[:64] for u in raw]


def compose(outer, inner, phi_inv):
    a2, b2, d2, _ = outer
    a1, b1, d1, phi1 = inner
    pq = mm(phi_inv, cat([b1, d2], 1))
    quad = mm(cat([b2, d1], 0), pq)
    n = a1.shape[0]
    return [a2 + quad[:n, n:], quad[:n, :n], quad[n:, n:], phi1 - quad[n:, :n]]


def level(slots):
    phis = inverses([outer[3] - inner[0] for outer, inner in slots])
    return [[u[:64] for u in compose(o, i, p)] for (o, i), p in zip(slots, phis)]


def constant_map(value):
    zero = jnp.zeros_like(value)
    return [value, zero, zero, imag_eye(64)]


def choose(cond, one, other):
    return [jnp.where(cond, x, y) for x, y in zip(one, other)]


def tree_body(slab, lead_top, sent, put, get):
    none = constant_map(jnp.zeros((128, 128), F32))
    lead = full(lead_top)
    lead = constant_map(-times_i(mm(lead, lead, NT)))

    def wide(tops):
        return [full(u) for u in tops]

    lefts = (slab + 2) // 2

    def fetch(is_left, place):
        source = jnp.where(is_left, slab - 1 - place, slab + 1 + place)
        there = (source >= 0) & (source < 8)
        found = wide(sent(jnp.clip(source, 0, 7)))
        return choose(there, found, choose(source == -1, lead, none))

    slots = []
    for k in range(5):
        is_left = k < lefts
        place = 2 * jnp.where(is_left, k, k - lefts)
        slots.append((fetch(is_left, place), fetch(is_left, place + 1)))
    for k, m in enumerate(level(slots)):
        put(k, m)

    twos = (lefts + 1) // 2
    slots = []
    for k in range(3):
        is_left = k < twos
        outer = jnp.where(is_left, 2 * k, lefts + 2 * (k - twos))
        stop = jnp.where(is_left, lefts, 5)
        inner = choose(outer + 1 < stop, wide(get(jnp.minimum(outer + 1, 4))), none)
        slots.append((wide(get(outer)), inner))
    for k, m in enumerate(level(slots)):
        put(5 + k, m)

    slots = []
    for first, stop in ((0, twos), (twos, 3)):
        inner = choose(first + 1 < stop, wide(get(5 + jnp.minimum(first + 1, 2))), none)
        slots.append((wide(get(5 + first)), inner))
    phis = inverses([outer[3] - inner[0] for outer, inner in slots])
    return [o[0] + mm(mm(o[1], p), o[2]) for (o, _), p in zip(slots, phis)]


def close_body(sig_l, sig_r, s, inner, y, z, raw):
    ib, b, d, phi = [full(u) for u in raw]
    lr, li = pair(sig_l)
    rr, ri = pair(sig_r)
    zero = jnp.zeros((64, 64), F32)

    def spread(x, w):
        return cat([cat([x, zero], 1), cat([zero, w], 1)], 0)

    closed = s - blk(spread(rr, lr), spread(ri, li))
    e_inv, big = inverses([phi - sig_l, closed])
    be = mm(b, e_inv)
    gfb = mm(e_inv, d)
    gbb = ib + mm(be, d)

    def joined(k):
        return cat([cat([pair(gbb)[k], pair(be)[k]], 1), cat([pair(gfb)[k], pair(e_inv)[k]], 1)], 0)

    small = cat([joined(0), -joined(1)], 1)
    return restore(big[:128], inner, y, z), small


def restore(top, inner, y, z):
    ty = mm(top, y)
    zt = mm(z, full(top))
    zty = mm(zt, y)
    low = inner + zty
    r = cat([cat([top[:, :128], -ty[:, :128]], 1), cat([-zt[:, :128], low[:, :128]], 1)], 0)
    i = cat([cat([-top[:, 128:], ty[:, 128:]], 1), cat([zt[:, 128:], -low[:, 128:]], 1)], 0)
    return r, i


def for_rows(r, i):
    r, i = [unrolled(unrolled(x, 0), 1).reshape(32, 8, 256) for x in (r, i)]
    upper = lax.broadcasted_iota(jnp.int32, (32, 8, 256), 1) < 4

    def swapped(x):
        return cat([x[:, 4:], x[:, :4]], 1)

    even = jnp.where(upper, r, swapped(i))
    odd = jnp.where(upper, swapped(r), i)
    return even, odd


def right_adj(lr, li, gr, gi):
    n = lr.shape[0]
    rows = cat([cat([lr, li], 1), cat([li, -lr], 1)], 0)
    out = mm(rows, cat([gr, gi], 1), NT)
    return out[:n], out[n:]


def lesser_parts_body(fr, fi, small, inner, y, z, inject, couple, next_top):
    gr, gi = restore(small, inner, y, z)
    hr, hi = 1.5 * gr - fr, 1.5 * gi - fi
    d = rolled(inject, 1)
    lr = cat([gr[:64], hr[64:128]], 0) * d
    li = cat([gi[:64], hi[64:128]], 0) * d
    mr, mi = right_adj(lr, li, gr[:128], gi[:128])
    c = blk(couple[0], couple[1])
    cn = full(next_top)
    ct, cnt = c.T, cn.T
    w = mm(mm(cn, blk(-mi[:64, :64], mr[:64, :64])), cnt)
    w = (w - w.T) * 0.5
    q = mm(mm(ct, blk(-mi[64:, 64:], mr[64:, 64:])), c)
    q = q - q.T
    beta = mm(cn, blk(gr[:64, 64:128], gi[:64, 64:128]))
    left = mm(
        ct,
        cat(
            [
                blk(gr[64:128, 64:128], gi[64:128, 64:128]),
                blk(hr[64:128, 64:128], hi[64:128, 64:128]),
                blk(gr[64:128, :64], gi[64:128, :64]),
            ],
            1,
        ),
    )
    u, v, zz = left[:, :128], left[:, 128:256], left[:, 256:]
    return (gr, gi), [m[:64] for m in (w + times_i(q), beta, u, v, zz)]


def lesser_body(slab, lead_top, parts, gr, gi, fr, fi, inject):
    lead = full(lead_top)
    sig = times_i(mm(lead, lead, NT))
    mine = sig
    sources = {}
    packed = [full(parts(t, 0)) for t in range(8)]
    for t in range(8):
        if t:
            beta = full(parts(t - 1, 1))
            both = packed[t - 1]
            sig = (both - both.T) * 0.5 + mm(mm(beta, sig), beta, NT)
            mine = jnp.where(slab == t, sig, mine)
            c = mm(mm(full(parts(t, 3)), sig), full(parts(t, 2)), NT)
            sources[t] = c - c.T - times_i((packed[t] + packed[t].T) * 0.5)
    back = jnp.zeros_like(sig)
    my_back = back
    for t in range(7, 0, -1):
        zz = full(parts(t, 4))
        back = sources[t] + mm(mm(zz, back), zz, NT)
        my_back = jnp.where(slab == t - 1, back, my_back)
    hr, hi = 1.5 * gr - fr, 1.5 * gi - fi
    d = rolled(inject, 1)
    right_r, right_i = pair(mine)
    back_r, back_i = pair(0.5 * my_back)

    def cols(xr, xi, m):
        out = mm(cat([xr, xi], 1), m)
        return out

    fm = cat([cat([right_r, right_i], 1), cat([-right_i, right_r], 1)], 0)
    bm = cat([cat([back_r, back_i], 1), cat([-back_i, back_r], 1)], 0)
    on_f = cols(hr[:, 64:128], hi[:, 64:128], fm)
    on_b = cols(gr[:, :64], gi[:, :64], bm)
    add_r = cat([on_b[:, :64], on_f[:, :64]], 1)
    add_i = cat([on_b[:, 64:], on_f[:, 64:]], 1)
    lr, li = -hi * d, hr * d
    lr = cat([lr[:, :128] + add_r, lr[:, 128:]], 1)
    li = cat([li[:, :128] + add_i, li[:, 128:]], 1)
    nr, ni = right_adj(lr, li, gr, gi)
    return nr - nr.T, ni + ni.T


VM = pl.BlockSpec(memory_space=pltpu.VMEM)
SM = pl.BlockSpec(memory_space=pltpu.SMEM)


def call(kernel, outs, specs, micros, scratch=()):
    return pl.pallas_call(
        kernel,
        out_shape=[jax.ShapeDtypeStruct(o, F32) for o in outs],
        in_specs=specs,
        out_specs=[VM] * len(outs),
        scratch_shapes=list(scratch),
        compiler_params=pltpu.CompilerParams(vmem_limit_bytes=40 * 2**20),
        cost_estimate=pl.CostEstimate(flops=int(micros * 1.1e9), bytes_accessed=1 << 20, transcendentals=0),
    )


def eliminate_kernel(energy, onsite, hop, s, inner, y, z):
    s[...], inner[...], y[...], z[...] = eliminate_body(energy[0], onsite[...], (hop[0, 0], hop[1, 0]))


def put(ref, values):
    for k, v in enumerate(values):
        ref[k] = v


def maps_kernel(slab, s, couple, next_top, sends, raw):
    me = slab[0]
    left, right, own = maps_body(s[...], (couple[0, 0], couple[1, 0]), next_top[...])
    put(raw, own)
    for t in range(8):
        put(sends.at[t], choose(me < t, left, right))


def put_rows(ref, r, i):
    even, odd = for_rows(r, i)
    ref[:, 0] = even
    ref[:, 1] = odd


def close_kernel(slab, tops, sent, s, inner, y, z, raw, rows, whole, small, kept):
    def load(ref):
        return lambda t: [ref[t, k] for k in range(4)]

    sig_l, sig_r = tree_body(slab[0], tops[0], load(sent), lambda k, m: put(kept.at[k], m), load(kept))
    (r, i), sm = close_body(sig_l, sig_r, s[...], inner[...], y[...], z[...], [raw[k] for k in range(4)])
    put_rows(rows, r, i)
    whole[0] = r
    whole[1] = i
    small[...] = sm


def lesser_parts_kernel(whole, small, inner, y, z, inject, couple, next_top, g, parts):
    pair_, p = lesser_parts_body(
        whole[0],
        whole[1],
        small[...],
        inner[...],
        y[...],
        z[...],
        inject[:, 0],
        (couple[0, 0], couple[1, 0]),
        next_top[...],
    )
    g[0] = pair_[0]
    g[1] = pair_[1]
    put(parts, p)


def lesser_kernel(slab, tops, parts, g, whole, inject, rows):
    r, i = lesser_body(
        slab[0], tops[0], lambda t, k: parts[t, k], g[0], g[1], whole[0], whole[1], inject[:, 0]
    )
    put_rows(rows, r, i)


def convolve_kernel(table, piece, out):
    for j in range(4):
        x = cat([piece[:, j], piece[:, 4 + j]], 0)
        o = mm(table[...], x)
        out[0, 0, :, j] = o[:64]
        out[1, 0, :, j] = o[64:]


def tables_kernel(kern, out):
    for k in range(2):
        t = []
        for c in range(2):
            x = jnp.broadcast_to(kern[k, c : c + 1, :], (64, 128))
            t.append(pltpu.roll(x, 65, 1, stride=1, stride_axis=0)[:, :64])
        out[k] = blk(t[0], t[1])


def per_device(energies, onsite, hopping, coupling, injection, kernels):
    slab = lax.axis_index("slab").astype(jnp.int32).reshape(1)

    def swapped_over(x, axis):
        return lax.all_to_all(x, axis, split_axis=0, concat_axis=0, tiled=True)

    top = jnp.concatenate([coupling[0, 0], -coupling[1, 0]], axis=1)
    next_top = lax.ppermute(top, "slab", [(t, (t + 7) % 8) for t in range(8)])
    tops = lax.all_gather(top, "slab")
    reversed_kernels = jnp.pad(kernels[:, :, ::-1], ((0, 0), (0, 0), (0, 1)))
    (tables,) = call(tables_kernel, [(2, 128, 128)], [VM], 1)(reversed_kernels)
    m256, half = (256, 256), (128, 256)
    s, inner, y, z = call(eliminate_kernel, [m256, half, m256, half], [SM, VM, VM], 8)(energies, onsite, hopping)
    sends, raw = call(maps_kernel, [(8, 4, 64, 128), (4, 64, 128)], [SM] + [VM] * 3, 6)(slab, s, coupling, next_top)
    sent = swapped_over(sends, "slab")
    rows, whole, small = call(
        close_kernel,
        [(32, 2, 8, 256), (2, 256, 256), half],
        [SM] + [VM] * 7,
        25,
        [pltpu.VMEM((8, 4, 64, 128), F32)],
    )(slab, tops, sent, s, inner, y, z, raw)

    def to_rows(x):
        return swapped_over(x.reshape(64, 8, 256), "energy")

    got_r = to_rows(rows)
    g, parts = call(lesser_parts_kernel, [(2, 256, 256), (5, 64, 128)], [VM] * 8, 3)(
        whole, small, inner, y, z, injection, coupling, next_top
    )
    all_parts = lax.all_gather(parts, "slab")
    (rows_l,) = call(lesser_kernel, [(32, 2, 8, 256)], [SM] + [VM] * 5, 8)(
        slab, tops, all_parts, g, whole, injection
    )
    got_l = to_rows(rows_l)
    conv = call(convolve_kernel, [(2, 1, 64, 4, 256)], [VM] * 2, 2)
    return conv(tables[0], got_r)[0], conv(tables[1], got_l)[0]


def solution(mesh):
    in_specs = (
        P("energy"),
        P("slab", None),
        P(None, "slab", None, None),
        P(None, "slab", None, None),
        P("energy", "slab", None),
        P(),
    )
    out_specs = (P(None, "slab", None, "energy", None), P(None, "slab", None, "energy", None))
    return jax.shard_map(per_device, mesh=mesh, in_specs=in_specs, out_specs=out_specs, check_vma=False)
```

```python
import functools

import jax
import jax.numpy as jnp
from jax import lax
from jax.experimental import pallas as pl
from jax.experimental.pallas import tpu as pltpu
from jax.sharding import PartitionSpec as P

ETA = 0.02
F32 = jnp.float32
BF16 = jnp.bfloat16
NN = (((1,), (0,)), ((), ()))
NT = (((1,), (1,)), ((), ()))


def mmh(a, b, dims=NN):
    return lax.dot_general(a, b, dims, precision=lax.Precision.HIGHEST, preferred_element_type=F32)


def halves(x):
    high = x.astype(BF16)
    return high, (x - high.astype(F32)).astype(BF16)


def mm1(a, b, dims=NN):
    return lax.dot_general(a, b, dims, preferred_element_type=F32)


def mm3(a, b, dims=NN):
    return mm1(a[0], b[0], dims) + (mm1(a[0], b[1], dims) + mm1(a[1], b[0], dims))


def mm(a, b, dims=NN):
    return mm3(halves(a), halves(b), dims)


def cat(parts, axis):
    return jnp.concatenate(parts, axis=axis)


def blk(r, i):
    return cat([cat([r, -i], 1), cat([i, r], 1)], 0)


def pair(z):
    n = z.shape[1] // 2
    return z[:n, :n], -z[:n, n:]


def full(top):
    n = top.shape[0]
    return cat([top, cat([-top[:, n:], top[:, :n]], 1)], 0)


def eye(n):
    return (lax.broadcasted_iota(jnp.int32, (n, n), 0) == lax.broadcasted_iota(jnp.int32, (n, n), 1)).astype(F32)


def imag_eye(n):
    return blk(jnp.zeros((n, n), F32), eye(n))


def times_i(z):
    n = z.shape[0] // 2
    return cat([-z[n:], z[:n]], 0)


def lowest(values):
    return functools.reduce(jnp.minimum, values)


def scaled(low, floor):
    base = jnp.maximum(low, floor)
    shift = 1.0 + base
    gain = 4.0 / (shift * shift)
    return shift, gain, jnp.minimum(gain * low * (shift - low), gain * base)


ENOUGH = 1e-4


def corrected(mats, xs):
    rs = [eye(z.shape[0]) - mmh(z, x) for z, x in zip(mats, xs)]
    size = functools.reduce(jnp.maximum, [jnp.sum(r * r) for r in rs])
    return size, tuple(x + mm1(x.astype(BF16), r.astype(BF16)) for x, r in zip(xs, rs))


def bound(z):
    zt = z.T
    w = mm1(z.astype(BF16), zt.astype(BF16))
    return 1.0 / (1.01 * jnp.max(jnp.sum(jnp.abs(w), axis=1, keepdims=True))), w, zt


def quick(sizes):
    def inverses(mats, factor=2.0):
        n = len(mats)
        eyes = [eye(z.shape[0]) for z in mats]
        parts = [halves(z) for z in mats]
        lows, guesses = [], []
        for z, one in zip(mats, eyes):
            inv_u, w, zt = bound(z)
            shift, gain, low = scaled((factor * ETA * ETA) * inv_u, 0.05)
            r = shift * one - w * inv_u
            guesses.append(((gain * inv_u) * mm1(zt.astype(BF16), r.astype(BF16))).astype(BF16))
            lows.append(low)

        def step(state):
            lows, guesses = state
            plans = [scaled(low, 0.05) for low in lows]
            rs = [(plans[k][0] * eyes[k] - mm1(parts[k][0], guesses[k])).astype(BF16) for k in range(n)]
            new = [(plans[k][1] * mm1(guesses[k], rs[k])).astype(BF16) for k in range(n)]
            return tuple(p[2] for p in plans), tuple(new)

        _, guesses = lax.while_loop(lambda state: lowest(state[0]) < 0.98, step, (tuple(lows), tuple(guesses)))
        better = []
        for (zh, zl), one, x in zip(parts, eyes, guesses):
            rh, rl = halves(one - (mm1(zh, x) + mm1(zl, x)))
            better.append(x.astype(F32) + (mm1(x, rh) + mm1(x, rl)))
        size, better = corrected(mats, better)
        sizes.append(size)
        return better

    return inverses


def careful(mats, factor=1.0):
    n = len(mats)
    eyes = [eye(z.shape[0]) for z in mats]
    parts = [halves(z) for z in mats]
    lows, xs = [], []
    for z in mats:
        inv_u, _, zt = bound(z)
        lows.append((ETA * ETA) * inv_u)
        xs.append(zt * inv_u)

    def step(state):
        lows, xs = state
        plans = [scaled(low, 1e-3) for low in lows]
        new = []
        for k in range(n):
            xp = halves(xs[k])
            r = plans[k][0] * eyes[k] - mm3(parts[k], xp)
            new.append(plans[k][1] * mm3(xp, halves(r)))
        return tuple(p[2] for p in plans), tuple(new)

    _, xs = lax.while_loop(lambda state: lowest(state[0]) < 0.999, step, (tuple(lows), tuple(xs)))

    def again(state):
        count, size, _ = state
        return (count < 8) & jnp.logical_not(size <= ENOUGH)

    def more(state):
        count, _, xs = state
        size, xs = corrected(mats, xs)
        return count + 1, size, xs

    size, xs = corrected(mats, xs)
    return lax.while_loop(again, more, (jnp.int32(0), size, xs))[2]


def guarded(run):
    sizes = []
    run(quick(sizes))

    @pl.when(jnp.logical_not(functools.reduce(jnp.maximum, sizes) <= ENOUGH))
    def _():
        run(careful)


def rolled(x, axis):
    n = x.shape[axis]
    if axis == 0:
        return cat([x[n - 64 :], x[: n - 64]], 0)
    return cat([x[:, n - 64 :], x[:, : n - 64]], 1)


def unrolled(x, axis):
    if axis == 0:
        return cat([x[64:], x[:64]], 0)
    return cat([x[:, 64:], x[:, :64]], 1)


def eliminate_body(inverses, energy, onsite, hop):
    h0 = rolled(rolled(hop[0], 0), 1)
    h1 = rolled(rolled(hop[1], 0), 1)
    on = rolled(onsite, 1)
    one = eye(256)
    ar = one * (energy - on) - (h0 + h0.T) * 0.5
    ai = one * ETA - (h1 - h1.T) * 0.5

    def part(rows, cols):
        return blk(ar[rows, cols], ai[rows, cols])

    b, i = slice(0, 128), slice(128, 256)
    (inner,) = inverses([part(i, i)], 1.0)
    abi = part(b, i)
    y = mm(abi, inner)
    z = mm(inner, part(i, b))
    s = part(b, b) - mm(abi, z)
    return s, inner[:128], y, z[:128]


def corners(s):
    r, i = pair(s)
    lo, hi = slice(0, 64), slice(64, 128)
    return [[blk(r[p, q], i[p, q]) for q in (lo, hi)] for p in (lo, hi)]


def lead_of(slab, c):
    return jnp.where(slab == 0, mm(c, c, NT), 0.0)


def maps_body(inverses, slab, s, couple, next_top):
    (bb, bf), (fb, ff) = corners(s)
    c = blk(couple[0], couple[1])
    cn = full(next_top)
    ff = ff + times_i(lead_of(slab, c))
    ib, if_ = inverses([bb, ff])
    b = -mm(ib, bf)
    d = -mm(fb, ib)
    phi = ff + mm(d, bf)
    br = -mm(if_, fb)
    dr = -mm(bf, if_)
    psi = bb + mm(dr, fb)
    ct = c.T
    cnt = cn.T
    left = [mm(mm(cn, ib), cnt), mm(cn, b), mm(d, cnt), phi]
    right = [mm(mm(ct, if_), c), mm(ct, br), mm(dr, c), psi]
    raw = [ib, b, d, phi]
    return [u[:64] for u in left], [u[:64] for u in right], [u[:64] for u in raw]


def compose(outer, inner, phi_inv):
    a2, b2, d2, _ = outer
    a1, b1, d1, phi1 = inner
    pq = mm(phi_inv, cat([b1, d2], 1))
    quad = mm(cat([b2, d1], 0), pq)
    n = a1.shape[0]
    return [a2 + quad[:n, n:], quad[:n, :n], quad[n:, n:], phi1 - quad[n:, :n]]


def level(inverses, slots):
    phis = inverses([outer[3] - inner[0] for outer, inner in slots])
    return [[u[:64] for u in compose(o, i, p)] for (o, i), p in zip(slots, phis)]


def constant_map(value):
    zero = jnp.zeros_like(value)
    return [value, zero, zero, imag_eye(64)]


def choose(cond, one, other):
    return [jnp.where(cond, x, y) for x, y in zip(one, other)]


def tree_body(inverses, slab, sent, put, get):
    none = constant_map(jnp.zeros((128, 128), F32))

    def wide(tops):
        return [full(u) for u in tops]

    lefts = (slab + 1) // 2

    def fetch(is_left, place):
        source = jnp.where(is_left, slab - 1 - place, slab + 1 + place)
        there = (source >= 0) & (source < 8)
        return choose(there, wide(sent(jnp.clip(source, 0, 7))), none)

    slots = []
    for k in range(4):
        is_left = k < lefts
        place = 2 * jnp.where(is_left, k, k - lefts)
        slots.append((fetch(is_left, place), fetch(is_left, place + 1)))
    for k, m in enumerate(level(inverses, slots)):
        put(k, m)

    twos = (lefts + 1) // 2
    slots = []
    for k in range(3):
        is_left = k < twos
        first = jnp.where(is_left, 2 * k, lefts + 2 * (k - twos))
        stop = jnp.where(is_left, lefts, 4)
        outer = choose(first < stop, wide(get(jnp.minimum(first, 3))), none)
        inner = choose(first + 1 < stop, wide(get(jnp.minimum(first + 1, 3))), none)
        slots.append((outer, inner))
    for k, m in enumerate(level(inverses, slots)):
        put(4 + k, m)

    slots = []
    for first, stop in ((0, twos), (twos, 3)):
        outer = choose(first < stop, wide(get(4 + jnp.minimum(first, 2))), none)
        inner = choose(first + 1 < stop, wide(get(4 + jnp.minimum(first + 1, 2))), none)
        slots.append((outer, inner))
    phis = inverses([outer[3] - inner[0] for outer, inner in slots])
    return [o[0] + mm(mm(o[1], p), o[2]) for (o, _), p in zip(slots, phis)]


def close_body(inverses, slab, couple, sig_l, sig_r, s, inner, y, z, raw):
    ib, b, d, phi = [full(u) for u in raw]
    lr, li = pair(sig_l - times_i(lead_of(slab, blk(couple[0], couple[1]))))
    rr, ri = pair(sig_r)
    zero = jnp.zeros((64, 64), F32)

    def spread(x, w):
        return cat([cat([x, zero], 1), cat([zero, w], 1)], 0)

    closed = s - blk(spread(rr, lr), spread(ri, li))
    e_inv, big = inverses([phi - sig_l, closed])
    be = mm(b, e_inv)
    gfb = mm(e_inv, d)
    gbb = ib + mm(be, d)

    def joined(k):
        return cat([cat([pair(gbb)[k], pair(be)[k]], 1), cat([pair(gfb)[k], pair(e_inv)[k]], 1)], 0)

    small = cat([joined(0), -joined(1)], 1)
    return restore(big[:128], inner, y, z), small


def restore(top, inner, y, z):
    ty = mm(top, y)
    zt = mm(z, full(top))
    zty = mm(zt, y)
    low = inner + zty
    r = cat([cat([top[:, :128], -ty[:, :128]], 1), cat([-zt[:, :128], low[:, :128]], 1)], 0)
    i = cat([cat([-top[:, 128:], ty[:, 128:]], 1), cat([zt[:, 128:], -low[:, 128:]], 1)], 0)
    return r, i


def for_rows(r, i):
    r, i = [unrolled(unrolled(x, 0), 1).reshape(32, 8, 256) for x in (r, i)]
    upper = lax.broadcasted_iota(jnp.int32, (32, 8, 256), 1) < 4

    def swapped(x):
        return cat([x[:, 4:], x[:, :4]], 1)

    even = jnp.where(upper, r, swapped(i))
    odd = jnp.where(upper, swapped(r), i)
    return even, odd


def right_adj(lr, li, gr, gi):
    n = lr.shape[0]
    rows = cat([cat([lr, li], 1), cat([li, -lr], 1)], 0)
    out = mm(rows, cat([gr, gi], 1), NT)
    return out[:n], out[n:]


def lesser_parts_body(slab, fr, fi, small, inner, y, z, inject, couple, next_top):
    gr, gi = restore(small, inner, y, z)
    hr, hi = 1.5 * gr - fr, 1.5 * gi - fi
    d = rolled(inject, 1)
    lr = cat([gr[:64], hr[64:128]], 0) * d
    li = cat([gi[:64], hi[64:128]], 0) * d
    mr, mi = right_adj(lr, li, gr[:128], gi[:128])
    c = blk(couple[0], couple[1])
    cn = full(next_top)
    ct, cnt = c.T, cn.T
    w = mm(mm(cn, blk(-mi[:64, :64], mr[:64, :64])), cnt)
    beta = mm(cn, blk(gr[:64, 64:128], gi[:64, 64:128]))
    w = w + mm(mm(beta, times_i(lead_of(slab, c))), beta, NT)
    w = (w - w.T) * 0.5
    q = mm(mm(ct, blk(-mi[64:, 64:], mr[64:, 64:])), c)
    q = q - q.T
    left = mm(
        ct,
        cat(
            [
                blk(gr[64:128, 64:128], gi[64:128, 64:128]),
                blk(hr[64:128, 64:128], hi[64:128, 64:128]),
                blk(gr[64:128, :64], gi[64:128, :64]),
            ],
            1,
        ),
    )
    u, v, zz = left[:, :128], left[:, 128:256], left[:, 256:]
    return (gr, gi), [m[:64] for m in (w + times_i(q), beta, u, v, zz)]


def lesser_body(slab, couple, parts, gr, gi, fr, fi, inject):
    mine = times_i(lead_of(slab, blk(couple[0], couple[1])))
    sources = {}
    packed = [full(parts(t, 0)) for t in range(8)]
    for t in range(8):
        if t:
            beta = full(parts(t - 1, 1))
            both = packed[t - 1]
            w = (both - both.T) * 0.5
            sig = w + mm(mm(beta, sig), beta, NT) if t > 1 else w
            mine = jnp.where(slab == t, sig, mine)
            c = mm(mm(full(parts(t, 3)), sig), full(parts(t, 2)), NT)
            sources[t] = c - c.T - times_i((packed[t] + packed[t].T) * 0.5)
    back = jnp.zeros_like(sig)
    my_back = back
    for t in range(7, 0, -1):
        zz = full(parts(t, 4))
        back = sources[t] + mm(mm(zz, back), zz, NT)
        my_back = jnp.where(slab == t - 1, back, my_back)
    hr, hi = 1.5 * gr - fr, 1.5 * gi - fi
    d = rolled(inject, 1)
    right_r, right_i = pair(mine)
    back_r, back_i = pair(0.5 * my_back)

    def cols(xr, xi, m):
        out = mm(cat([xr, xi], 1), m)
        return out

    fm = cat([cat([right_r, right_i], 1), cat([-right_i, right_r], 1)], 0)
    bm = cat([cat([back_r, back_i], 1), cat([-back_i, back_r], 1)], 0)
    on_f = cols(hr[:, 64:128], hi[:, 64:128], fm)
    on_b = cols(gr[:, :64], gi[:, :64], bm)
    add_r = cat([on_b[:, :64], on_f[:, :64]], 1)
    add_i = cat([on_b[:, 64:], on_f[:, 64:]], 1)
    lr, li = -hi * d, hr * d
    lr = cat([lr[:, :128] + add_r, lr[:, 128:]], 1)
    li = cat([li[:, :128] + add_i, li[:, 128:]], 1)
    nr, ni = right_adj(lr, li, gr, gi)
    return nr - nr.T, ni + ni.T


VM = pl.BlockSpec(memory_space=pltpu.VMEM)
SM = pl.BlockSpec(memory_space=pltpu.SMEM)


def call(kernel, outs, specs, micros, scratch=()):
    return pl.pallas_call(
        kernel,
        out_shape=[jax.ShapeDtypeStruct(o, F32) for o in outs],
        in_specs=specs,
        out_specs=[VM] * len(outs),
        scratch_shapes=list(scratch),
        compiler_params=pltpu.CompilerParams(vmem_limit_bytes=40 * 2**20),
        cost_estimate=pl.CostEstimate(flops=int(micros * 1.1e9), bytes_accessed=1 << 20, transcendentals=0),
    )


def eliminate_kernel(energy, onsite, hop, s, inner, y, z):
    def run(inverses):
        s[...], inner[...], y[...], z[...] = eliminate_body(inverses, energy[0], onsite[...], (hop[0, 0], hop[1, 0]))

    guarded(run)


def put(ref, values):
    for k, v in enumerate(values):
        ref[k] = v


def maps_kernel(slab, s, couple, next_top, sends, raw):
    me = slab[0]

    def run(inverses):
        left, right, own = maps_body(inverses, me, s[...], (couple[0, 0], couple[1, 0]), next_top[...])
        put(raw, own)
        for t in range(8):
            put(sends.at[t], choose(me < t, left, right))

    guarded(run)


def put_rows(ref, r, i):
    even, odd = for_rows(r, i)
    ref[:, 0] = even
    ref[:, 1] = odd


def close_kernel(slab, couple, sent, s, inner, y, z, raw, rows, whole, small, kept):
    def load(ref):
        return lambda t: [ref[t, k] for k in range(4)]

    def run(inverses):
        sig_l, sig_r = tree_body(inverses, slab[0], load(sent), lambda k, m: put(kept.at[k], m), load(kept))
        own = [raw[k] for k in range(4)]
        (r, i), sm = close_body(
            inverses, slab[0], (couple[0, 0], couple[1, 0]), sig_l, sig_r, s[...], inner[...], y[...], z[...], own
        )
        put_rows(rows, r, i)
        whole[0] = r
        whole[1] = i
        small[...] = sm

    guarded(run)


def lesser_parts_kernel(slab, whole, small, inner, y, z, inject, couple, next_top, g, parts):
    pair_, p = lesser_parts_body(
        slab[0],
        whole[0],
        whole[1],
        small[...],
        inner[...],
        y[...],
        z[...],
        inject[:, 0],
        (couple[0, 0], couple[1, 0]),
        next_top[...],
    )
    g[0] = pair_[0]
    g[1] = pair_[1]
    put(parts, p)


def lesser_kernel(slab, couple, parts, g, whole, inject, rows):
    r, i = lesser_body(
        slab[0],
        (couple[0, 0], couple[1, 0]),
        lambda t, k: parts[t, k],
        g[0],
        g[1],
        whole[0],
        whole[1],
        inject[:, 0],
    )
    put_rows(rows, r, i)


def convolve_kernel(table, piece, out):
    for j in range(4):
        x = cat([piece[:, j], piece[:, 4 + j]], 0)
        o = mm(table[...], x)
        out[0, 0, :, j] = o[:64]
        out[1, 0, :, j] = o[64:]


def tables_kernel(kern, out):
    for k in range(2):
        t = []
        for c in range(2):
            x = jnp.broadcast_to(kern[k, c : c + 1, :], (64, 128))
            t.append(pltpu.roll(x, 65, 1, stride=1, stride_axis=0)[:, :64])
        out[k] = blk(t[0], t[1])


def per_device(energies, onsite, hopping, coupling, injection, kernels):
    slab = lax.axis_index("slab").astype(jnp.int32).reshape(1)

    def swapped_over(x, axis):
        return lax.all_to_all(x, axis, split_axis=0, concat_axis=0, tiled=True)

    top = jnp.concatenate([coupling[0, 0], -coupling[1, 0]], axis=1)
    next_top = lax.ppermute(top, "slab", [(t, (t + 7) % 8) for t in range(8)])
    reversed_kernels = jnp.pad(kernels[:, :, ::-1], ((0, 0), (0, 0), (0, 1)))
    (tables,) = call(tables_kernel, [(2, 128, 128)], [VM], 1)(reversed_kernels)
    m256, half = (256, 256), (128, 256)
    s, inner, y, z = call(eliminate_kernel, [m256, half, m256, half], [SM, VM, VM], 8)(energies, onsite, hopping)
    sends, raw = call(maps_kernel, [(8, 4, 64, 128), (4, 64, 128)], [SM] + [VM] * 3, 6)(slab, s, coupling, next_top)
    sent = swapped_over(sends, "slab")
    rows, whole, small = call(
        close_kernel,
        [(32, 2, 8, 256), (2, 256, 256), half],
        [SM] + [VM] * 7,
        25,
        [pltpu.VMEM((7, 4, 64, 128), F32)],
    )(slab, coupling, sent, s, inner, y, z, raw)

    def to_rows(x):
        return swapped_over(x.reshape(64, 8, 256), "energy")

    got_r = to_rows(rows)
    g, parts = call(lesser_parts_kernel, [(2, 256, 256), (5, 64, 128)], [SM] + [VM] * 8, 3)(
        slab, whole, small, inner, y, z, injection, coupling, next_top
    )
    all_parts = lax.all_gather(parts, "slab")
    (rows_l,) = call(lesser_kernel, [(32, 2, 8, 256)], [SM] + [VM] * 5, 8)(
        slab, coupling, all_parts, g, whole, injection
    )
    got_l = to_rows(rows_l)
    conv = call(convolve_kernel, [(2, 1, 64, 4, 256)], [VM] * 2, 2)
    return conv(tables[0], got_r)[0], conv(tables[1], got_l)[0]


def solution(mesh):
    in_specs = (
        P("energy"),
        P("slab", None),
        P(None, "slab", None, None),
        P(None, "slab", None, None),
        P("energy", "slab", None),
        P(),
    )
    out_specs = (P(None, "slab", None, "energy", None), P(None, "slab", None, "energy", None))
    return jax.shard_map(per_device, mesh=mesh, in_specs=in_specs, out_specs=out_specs, check_vma=False)
```

```python
import functools

import jax
import jax.numpy as jnp
from jax import lax
from jax.experimental import pallas as pl
from jax.experimental.pallas import tpu as pltpu
from jax.sharding import PartitionSpec as P

ETA = 0.02
F32 = jnp.float32
BF16 = jnp.bfloat16
NN = (((1,), (0,)), ((), ()))
NT = (((1,), (1,)), ((), ()))


def mmh(a, b, dims=NN):
    return lax.dot_general(a, b, dims, precision=lax.Precision.HIGHEST, preferred_element_type=F32)


def halves(x):
    high = x.astype(BF16)
    return high, (x - high.astype(F32)).astype(BF16)


def mm1(a, b, dims=NN):
    return lax.dot_general(a, b, dims, preferred_element_type=F32)


def mm3(a, b, dims=NN):
    return mm1(a[0], b[0], dims) + (mm1(a[0], b[1], dims) + mm1(a[1], b[0], dims))


def mm(a, b, dims=NN):
    return mm3(halves(a), halves(b), dims)


def cat(parts, axis):
    return jnp.concatenate(parts, axis=axis)


def blk(r, i):
    return cat([cat([r, -i], 1), cat([i, r], 1)], 0)


def pair(z):
    n = z.shape[1] // 2
    return z[:n, :n], -z[:n, n:]


def full(top):
    n = top.shape[0]
    return cat([top, cat([-top[:, n:], top[:, :n]], 1)], 0)


def eye(n):
    return (lax.broadcasted_iota(jnp.int32, (n, n), 0) == lax.broadcasted_iota(jnp.int32, (n, n), 1)).astype(F32)


def imag_eye(n):
    return blk(jnp.zeros((n, n), F32), eye(n))


def times_i(z):
    n = z.shape[0] // 2
    return cat([-z[n:], z[:n]], 0)


def lowest(values):
    return functools.reduce(jnp.minimum, values)


def scaled(low, floor):
    base = jnp.maximum(low, floor)
    shift = 1.0 + base
    gain = 4.0 / (shift * shift)
    return shift, gain, jnp.minimum(gain * low * (shift - low), gain * base)


ENOUGH = 1e-4


def corrected(mats, xs):
    rs = [eye(z.shape[0]) - mmh(z, x) for z, x in zip(mats, xs)]
    size = functools.reduce(jnp.maximum, [jnp.sum(r * r) for r in rs])
    return size, tuple(x + mm1(x.astype(BF16), r.astype(BF16)) for x, r in zip(xs, rs))


def bound(z):
    zt = z.T
    w = mm1(z.astype(BF16), zt.astype(BF16))
    return 1.0 / (1.01 * jnp.max(jnp.sum(jnp.abs(w), axis=1, keepdims=True))), w, zt


FLOOR = 0.035


def last_steps():
    low = FLOOR
    for _ in range(4):
        shift = 1.0 + low
        gain = 4.0 / (shift * shift)
        yield shift, gain
        low *= gain


def quick(sizes):
    def inverses(mats, factor=2.0):
        eyes = [eye(z.shape[0]) for z in mats]
        parts = [halves(z) for z in mats]
        shift = 1.0 + FLOOR
        gain = 4.0 / (shift * shift)
        lows, guesses = [], []
        for z, one in zip(mats, eyes):
            inv_u, w, zt = bound(z)
            r = shift * one - w * inv_u
            guesses.append(((gain * inv_u) * mm1(zt.astype(BF16), r.astype(BF16))).astype(BF16))
            lows.append((factor * ETA * ETA) * inv_u)
        low = lowest(lows)
        rise = gain * (shift - FLOOR)
        count = sum((low < FLOOR * rise**-k).astype(jnp.int32) for k in range(1, 20))

        def step(shift, gain, guesses):
            rs = [(shift * one - mm1(p[0], x)).astype(BF16) for p, one, x in zip(parts, eyes, guesses)]
            return tuple((gain * mm1(x, r)).astype(BF16) for x, r in zip(guesses, rs))

        guesses = lax.fori_loop(0, count, lambda _, xs: step(shift, gain, xs), tuple(guesses))
        for late_shift, late_gain in last_steps():
            guesses = step(late_shift, late_gain, guesses)
        better = []
        for (zh, zl), one, x in zip(parts, eyes, guesses):
            rh, rl = halves(one - (mm1(zh, x) + mm1(zl, x)))
            better.append(x.astype(F32) + (mm1(x, rh) + mm1(x, rl)))
        size, better = corrected(mats, better)
        sizes.append(size)
        return better

    return inverses


def careful(mats, factor=1.0):
    n = len(mats)
    eyes = [eye(z.shape[0]) for z in mats]
    parts = [halves(z) for z in mats]
    lows, xs = [], []
    for z in mats:
        inv_u, _, zt = bound(z)
        lows.append((ETA * ETA) * inv_u)
        xs.append(zt * inv_u)

    def step(state):
        lows, xs = state
        plans = [scaled(low, 1e-3) for low in lows]
        new = []
        for k in range(n):
            xp = halves(xs[k])
            r = plans[k][0] * eyes[k] - mm3(parts[k], xp)
            new.append(plans[k][1] * mm3(xp, halves(r)))
        return tuple(p[2] for p in plans), tuple(new)

    _, xs = lax.while_loop(lambda state: lowest(state[0]) < 0.999, step, (tuple(lows), tuple(xs)))

    def again(state):
        count, size, _ = state
        return (count < 8) & jnp.logical_not(size <= ENOUGH)

    def more(state):
        count, _, xs = state
        size, xs = corrected(mats, xs)
        return count + 1, size, xs

    size, xs = corrected(mats, xs)
    return lax.while_loop(again, more, (jnp.int32(0), size, xs))[2]


def guarded(run):
    sizes = []
    run(quick(sizes))

    @pl.when(jnp.logical_not(functools.reduce(jnp.maximum, sizes) <= ENOUGH))
    def _():
        run(careful)


def rolled(x, axis):
    n = x.shape[axis]
    if axis == 0:
        return cat([x[n - 64 :], x[: n - 64]], 0)
    return cat([x[:, n - 64 :], x[:, : n - 64]], 1)


def unrolled(x, axis):
    if axis == 0:
        return cat([x[64:], x[:64]], 0)
    return cat([x[:, 64:], x[:, :64]], 1)


def eliminate_body(inverses, energy, onsite, hop):
    h0 = rolled(rolled(hop[0], 0), 1)
    h1 = rolled(rolled(hop[1], 0), 1)
    on = rolled(onsite, 1)
    one = eye(256)
    ar = one * (energy - on) - (h0 + h0.T) * 0.5
    ai = one * ETA - (h1 - h1.T) * 0.5

    def part(rows, cols):
        return blk(ar[rows, cols], ai[rows, cols])

    b, i = slice(0, 128), slice(128, 256)
    (inner,) = inverses([part(i, i)], 1.0)
    abi = part(b, i)
    y = mm(abi, inner)
    z = mm(inner, part(i, b))
    s = part(b, b) - mm(abi, z)
    return s, inner[:128], y, z[:128]


def corners(s):
    r, i = pair(s)
    lo, hi = slice(0, 64), slice(64, 128)
    return [[blk(r[p, q], i[p, q]) for q in (lo, hi)] for p in (lo, hi)]


def lead_of(slab, c):
    return jnp.where(slab == 0, mm(c, c, NT), 0.0)


def maps_body(inverses, slab, s, couple, next_top):
    (bb, bf), (fb, ff) = corners(s)
    c = blk(couple[0], couple[1])
    cn = full(next_top)
    ff = ff + times_i(lead_of(slab, c))
    ib, if_ = inverses([bb, ff])
    b = -mm(ib, bf)
    d = -mm(fb, ib)
    phi = ff + mm(d, bf)
    br = -mm(if_, fb)
    dr = -mm(bf, if_)
    psi = bb + mm(dr, fb)
    ct = c.T
    cnt = cn.T
    left = [mm(mm(cn, ib), cnt), mm(cn, b), mm(d, cnt), phi]
    right = [mm(mm(ct, if_), c), mm(ct, br), mm(dr, c), psi]
    raw = [ib, b, d, phi]
    return [u[:64] for u in left], [u[:64] for u in right], [u[:64] for u in raw]


def compose(outer, inner, phi_inv):
    a2, b2, d2, _ = outer
    a1, b1, d1, phi1 = inner
    pq = mm(phi_inv, cat([b1, d2], 1))
    quad = mm(cat([b2, d1], 0), pq)
    n = a1.shape[0]
    return [a2 + quad[:n, n:], quad[:n, :n], quad[n:, n:], phi1 - quad[n:, :n]]


def level(inverses, slots):
    phis = inverses([outer[3] - inner[0] for outer, inner in slots])
    return [[u[:64] for u in compose(o, i, p)] for (o, i), p in zip(slots, phis)]


def constant_map(value):
    zero = jnp.zeros_like(value)
    return [value, zero, zero, imag_eye(64)]


def choose(cond, one, other):
    return [jnp.where(cond, x, y) for x, y in zip(one, other)]


def tree_body(inverses, slab, sent, put, get):
    none = constant_map(jnp.zeros((128, 128), F32))

    def wide(tops):
        return [full(u) for u in tops]

    lefts = (slab + 1) // 2

    def fetch(is_left, place):
        source = jnp.where(is_left, slab - 1 - place, slab + 1 + place)
        there = (source >= 0) & (source < 8)
        return choose(there, wide(sent(jnp.clip(source, 0, 7))), none)

    slots = []
    for k in range(4):
        is_left = k < lefts
        place = 2 * jnp.where(is_left, k, k - lefts)
        slots.append((fetch(is_left, place), fetch(is_left, place + 1)))
    for k, m in enumerate(level(inverses, slots)):
        put(k, m)

    twos = (lefts + 1) // 2
    slots = []
    for k in range(3):
        is_left = k < twos
        first = jnp.where(is_left, 2 * k, lefts + 2 * (k - twos))
        stop = jnp.where(is_left, lefts, 4)
        outer = choose(first < stop, wide(get(jnp.minimum(first, 3))), none)
        inner = choose(first + 1 < stop, wide(get(jnp.minimum(first + 1, 3))), none)
        slots.append((outer, inner))
    for k, m in enumerate(level(inverses, slots)):
        put(4 + k, m)

    slots = []
    for first, stop in ((0, twos), (twos, 3)):
        outer = choose(first < stop, wide(get(4 + jnp.minimum(first, 2))), none)
        inner = choose(first + 1 < stop, wide(get(4 + jnp.minimum(first + 1, 2))), none)
        slots.append((outer, inner))
    phis = inverses([outer[3] - inner[0] for outer, inner in slots])
    return [o[0] + mm(mm(o[1], p), o[2]) for (o, _), p in zip(slots, phis)]


def close_body(inverses, slab, couple, sig_l, sig_r, s, inner, y, z, raw):
    ib, b, d, phi = [full(u) for u in raw]
    lr, li = pair(sig_l - times_i(lead_of(slab, blk(couple[0], couple[1]))))
    rr, ri = pair(sig_r)
    zero = jnp.zeros((64, 64), F32)

    def spread(x, w):
        return cat([cat([x, zero], 1), cat([zero, w], 1)], 0)

    closed = s - blk(spread(rr, lr), spread(ri, li))
    e_inv, big = inverses([phi - sig_l, closed])
    be = mm(b, e_inv)
    gfb = mm(e_inv, d)
    gbb = ib + mm(be, d)

    def joined(k):
        return cat([cat([pair(gbb)[k], pair(be)[k]], 1), cat([pair(gfb)[k], pair(e_inv)[k]], 1)], 0)

    small = cat([joined(0), -joined(1)], 1)
    return big[:128], small


def restore(top, inner, y, z):
    ty = mm(top, y)
    zt = mm(z, full(top))
    zty = mm(zt, y)
    low = inner + zty
    r = cat([cat([top[:, :128], -ty[:, :128]], 1), cat([-zt[:, :128], low[:, :128]], 1)], 0)
    i = cat([cat([-top[:, 128:], ty[:, 128:]], 1), cat([zt[:, 128:], -low[:, 128:]], 1)], 0)
    return r, i


def for_rows(r, i):
    r, i = [unrolled(unrolled(x, 0), 1).reshape(32, 8, 256) for x in (r, i)]
    upper = lax.broadcasted_iota(jnp.int32, (32, 8, 256), 1) < 4

    def swapped(x):
        return cat([x[:, 4:], x[:, :4]], 1)

    even = jnp.where(upper, r, swapped(i))
    odd = jnp.where(upper, swapped(r), i)
    return even, odd


def right_adj(lr, li, gr, gi):
    n = lr.shape[0]
    rows = cat([cat([lr, li], 1), cat([li, -lr], 1)], 0)
    out = mm(rows, cat([gr, gi], 1), NT)
    return out[:n], out[n:]


def lesser_parts_body(slab, big, small, y, inject, couple, next_top):
    rest = mm(cat([small, big], 0), y)
    gr, gi = cat([small[:, :128], -rest[:128, :128]], 1), cat([-small[:, 128:], rest[:128, 128:]], 1)
    fr, fi = cat([big[:, :128], -rest[128:, :128]], 1), cat([-big[:, 128:], rest[128:, 128:]], 1)
    hr, hi = 1.5 * gr - fr, 1.5 * gi - fi
    d = rolled(inject, 1)
    lr = cat([gr[:64], hr[64:]], 0) * d
    li = cat([gi[:64], hi[64:]], 0) * d
    mr, mi = right_adj(lr, li, gr, gi)
    c = blk(couple[0], couple[1])
    cn = full(next_top)
    ct, cnt = c.T, cn.T
    w = mm(mm(cn, blk(-mi[:64, :64], mr[:64, :64])), cnt)
    beta = mm(cn, blk(gr[:64, 64:128], gi[:64, 64:128]))
    w = w + mm(mm(beta, times_i(lead_of(slab, c))), beta, NT)
    w = (w - w.T) * 0.5
    q = mm(mm(ct, blk(-mi[64:, 64:], mr[64:, 64:])), c)
    q = q - q.T
    left = mm(
        ct,
        cat(
            [
                blk(gr[64:128, 64:128], gi[64:128, 64:128]),
                blk(hr[64:128, 64:128], hi[64:128, 64:128]),
                blk(gr[64:128, :64], gi[64:128, :64]),
            ],
            1,
        ),
    )
    u, v, zz = left[:, :128], left[:, 128:256], left[:, 256:]
    return [m[:64] for m in (w + times_i(q), beta, u, v, zz)]


def lesser_body(slab, couple, parts, big, small, inner, y, z, inject):
    mine = times_i(lead_of(slab, blk(couple[0], couple[1])))
    sources = {}
    packed = [full(parts(t, 0)) for t in range(8)]
    for t in range(8):
        if t:
            beta = full(parts(t - 1, 1))
            both = packed[t - 1]
            w = (both - both.T) * 0.5
            sig = w + mm(mm(beta, sig), beta, NT) if t > 1 else w
            mine = jnp.where(slab == t, sig, mine)
            c = mm(mm(full(parts(t, 3)), sig), full(parts(t, 2)), NT)
            sources[t] = c - c.T - times_i((packed[t] + packed[t].T) * 0.5)
    back = jnp.zeros_like(sig)
    my_back = back
    for t in range(7, 0, -1):
        zz = full(parts(t, 4))
        back = sources[t] + mm(mm(zz, back), zz, NT)
        my_back = jnp.where(slab == t - 1, back, my_back)
    gr, gi = restore(small, inner, y, z)
    fr, fi = restore(big, inner, y, z)
    hr, hi = 1.5 * gr - fr, 1.5 * gi - fi
    d = rolled(inject, 1)
    right_r, right_i = pair(mine)
    back_r, back_i = pair(0.5 * my_back)

    def cols(xr, xi, m):
        out = mm(cat([xr, xi], 1), m)
        return out

    fm = cat([cat([right_r, right_i], 1), cat([-right_i, right_r], 1)], 0)
    bm = cat([cat([back_r, back_i], 1), cat([-back_i, back_r], 1)], 0)
    on_f = cols(hr[:, 64:128], hi[:, 64:128], fm)
    on_b = cols(gr[:, :64], gi[:, :64], bm)
    add_r = cat([on_b[:, :64], on_f[:, :64]], 1)
    add_i = cat([on_b[:, 64:], on_f[:, 64:]], 1)
    lr, li = -hi * d, hr * d
    lr = cat([lr[:, :128] + add_r, lr[:, 128:]], 1)
    li = cat([li[:, :128] + add_i, li[:, 128:]], 1)
    nr, ni = right_adj(lr, li, gr, gi)
    return nr - nr.T, ni + ni.T


VM = pl.BlockSpec(memory_space=pltpu.VMEM)
SM = pl.BlockSpec(memory_space=pltpu.SMEM)


def call(kernel, outs, specs, micros, scratch=()):
    return pl.pallas_call(
        kernel,
        out_shape=[jax.ShapeDtypeStruct(o, F32) for o in outs],
        in_specs=specs,
        out_specs=[VM] * len(outs),
        scratch_shapes=list(scratch),
        compiler_params=pltpu.CompilerParams(vmem_limit_bytes=40 * 2**20),
        cost_estimate=pl.CostEstimate(flops=int(micros * 1.1e9), bytes_accessed=1 << 20, transcendentals=0),
    )


def eliminate_kernel(energy, onsite, hop, s, inner, y, z):
    def run(inverses):
        s[...], inner[...], y[...], z[...] = eliminate_body(inverses, energy[0], onsite[...], (hop[0, 0], hop[1, 0]))

    guarded(run)


def put(ref, values):
    for k, v in enumerate(values):
        ref[k] = v


def maps_kernel(slab, s, couple, next_top, sends, raw):
    me = slab[0]

    def run(inverses):
        left, right, own = maps_body(inverses, me, s[...], (couple[0, 0], couple[1, 0]), next_top[...])
        put(raw, own)
        for t in range(8):
            put(sends.at[t], choose(me < t, left, right))

    guarded(run)


def put_rows(ref, r, i):
    even, odd = for_rows(r, i)
    ref[:, 0] = even
    ref[:, 1] = odd


def close_kernel(slab, couple, sent, s, inner, y, z, raw, rows, big, small, kept):
    def load(ref):
        return lambda t: [ref[t, k] for k in range(4)]

    def run(inverses):
        sig_l, sig_r = tree_body(inverses, slab[0], load(sent), lambda k, m: put(kept.at[k], m), load(kept))
        own = [raw[k] for k in range(4)]
        big[...], small[...] = close_body(
            inverses, slab[0], (couple[0, 0], couple[1, 0]), sig_l, sig_r, s[...], inner[...], y[...], z[...], own
        )
        put_rows(rows, *restore(big[...], inner[...], y[...], z[...]))

    guarded(run)


def lesser_parts_kernel(slab, big, small, y, inject, couple, next_top, parts):
    p = lesser_parts_body(
        slab[0], big[...], small[...], y[...], inject[:, 0], (couple[0, 0], couple[1, 0]), next_top[...]
    )
    put(parts, p)


def lesser_kernel(slab, couple, parts, big, small, inner, y, z, inject, rows):
    r, i = lesser_body(
        slab[0],
        (couple[0, 0], couple[1, 0]),
        lambda t, k: parts[t, k],
        big[...],
        small[...],
        inner[...],
        y[...],
        z[...],
        inject[:, 0],
    )
    put_rows(rows, r, i)


def convolve_kernel(table, piece, out):
    for j in range(4):
        x = cat([piece[:, j], piece[:, 4 + j]], 0)
        o = mm(table[...], x)
        out[0, 0, :, j] = o[:64]
        out[1, 0, :, j] = o[64:]


def tables_kernel(kern, out):
    for k in range(2):
        t = []
        for c in range(2):
            x = jnp.broadcast_to(kern[k, c : c + 1, :], (64, 128))
            t.append(pltpu.roll(x, 65, 1, stride=1, stride_axis=0)[:, :64])
        out[k] = blk(t[0], t[1])


def per_device(energies, onsite, hopping, coupling, injection, kernels):
    slab = lax.axis_index("slab").astype(jnp.int32).reshape(1)

    def swapped_over(x, axis):
        return lax.all_to_all(x, axis, split_axis=0, concat_axis=0, tiled=True)

    top = jnp.concatenate([coupling[0, 0], -coupling[1, 0]], axis=1)
    next_top = lax.ppermute(top, "slab", [(t, (t + 7) % 8) for t in range(8)])
    m256, half = (256, 256), (128, 256)
    s, inner, y, z = call(eliminate_kernel, [m256, half, m256, half], [SM, VM, VM], 8)(energies, onsite, hopping)
    sends, raw = call(maps_kernel, [(8, 4, 64, 128), (4, 64, 128)], [SM] + [VM] * 3, 6)(slab, s, coupling, next_top)
    sent = swapped_over(sends, "slab")
    rows, big, small = call(
        close_kernel,
        [(32, 2, 8, 256), half, half],
        [SM] + [VM] * 7,
        25,
        [pltpu.VMEM((7, 4, 64, 128), F32)],
    )(slab, coupling, sent, s, inner, y, z, raw)

    def to_rows(x):
        return swapped_over(x.reshape(64, 8, 256), "energy")

    got_r = to_rows(rows)
    (parts,) = call(lesser_parts_kernel, [(5, 64, 128)], [SM] + [VM] * 6, 2)(
        slab, big, small, y, injection, coupling, next_top
    )
    all_parts = lax.all_gather(parts, "slab")
    late_kernels, _ = lax.optimization_barrier((kernels, parts))
    reversed_kernels = jnp.pad(late_kernels[:, :, ::-1], ((0, 0), (0, 0), (0, 1)))
    (tables,) = call(tables_kernel, [(2, 128, 128)], [VM], 1)(reversed_kernels)
    (rows_l,) = call(lesser_kernel, [(32, 2, 8, 256)], [SM] + [VM] * 8, 8)(
        slab, coupling, all_parts, big, small, inner, y, z, injection
    )
    got_l = to_rows(rows_l)
    conv = call(convolve_kernel, [(2, 1, 64, 4, 256)], [VM] * 2, 2)
    return conv(tables[0], got_r)[0], conv(tables[1], got_l)[0]


def solution(mesh):
    in_specs = (
        P("energy"),
        P("slab", None),
        P(None, "slab", None, None),
        P(None, "slab", None, None),
        P("energy", "slab", None),
        P(),
    )
    out_specs = (P(None, "slab", None, "energy", None), P(None, "slab", None, "energy", None))
    return jax.shard_map(per_device, mesh=mesh, in_specs=in_specs, out_specs=out_specs, check_vma=False)
```

```python
import functools

import jax
import jax.numpy as jnp
from jax import lax
from jax.experimental import pallas as pl
from jax.experimental.pallas import tpu as pltpu
from jax.sharding import PartitionSpec as P

ETA = 0.02
F32 = jnp.float32
BF16 = jnp.bfloat16
NN = (((1,), (0,)), ((), ()))
NT = (((1,), (1,)), ((), ()))


def mmh(a, b, dims=NN):
    return lax.dot_general(a, b, dims, precision=lax.Precision.HIGHEST, preferred_element_type=F32)


def halves(x):
    high = x.astype(BF16)
    return high, (x - high.astype(F32)).astype(BF16)


def mm1(a, b, dims=NN):
    return lax.dot_general(a, b, dims, preferred_element_type=F32)


def mm3(a, b, dims=NN):
    return mm1(a[0], b[0], dims) + (mm1(a[0], b[1], dims) + mm1(a[1], b[0], dims))


def mm(a, b, dims=NN):
    return mm3(halves(a), halves(b), dims)


def cat(parts, axis):
    return jnp.concatenate(parts, axis=axis)


def blk(r, i):
    return cat([cat([r, -i], 1), cat([i, r], 1)], 0)


def pair(z):
    n = z.shape[1] // 2
    return z[:n, :n], -z[:n, n:]


def full(top):
    n = top.shape[0]
    return cat([top, cat([-top[:, n:], top[:, :n]], 1)], 0)


def eye(n):
    return (lax.broadcasted_iota(jnp.int32, (n, n), 0) == lax.broadcasted_iota(jnp.int32, (n, n), 1)).astype(F32)


def imag_eye(n):
    return blk(jnp.zeros((n, n), F32), eye(n))


def times_i(z):
    n = z.shape[0] // 2
    return cat([-z[n:], z[:n]], 0)


def lowest(values):
    return functools.reduce(jnp.minimum, values)


def scaled(low, floor):
    base = jnp.maximum(low, floor)
    shift = 1.0 + base
    gain = 4.0 / (shift * shift)
    return shift, gain, jnp.minimum(gain * low * (shift - low), gain * base)


ENOUGH = 1e-4


def corrected(mats, xs):
    rs = [eye(z.shape[0]) - mmh(z, x) for z, x in zip(mats, xs)]
    size = functools.reduce(jnp.maximum, [jnp.sum(r * r) for r in rs])
    return size, tuple(x + mm1(x.astype(BF16), r.astype(BF16)) for x, r in zip(xs, rs))


def bound(z):
    zt = z.T
    w = mm1(z.astype(BF16), zt.astype(BF16))
    return 1.0 / (1.01 * jnp.max(jnp.sum(jnp.abs(w), axis=1, keepdims=True))), w, zt


FLOOR = 0.035


def last_steps():
    low = FLOOR
    for _ in range(4):
        shift = 1.0 + low
        gain = 4.0 / (shift * shift)
        yield shift, gain
        low *= gain


def quick(sizes):
    def inverses(mats, factor=3.0):
        eyes = [eye(z.shape[0]) for z in mats]
        parts = [halves(z) for z in mats]
        shift = 1.0 + FLOOR
        gain = 4.0 / (shift * shift)
        lows, guesses = [], []
        for z, one in zip(mats, eyes):
            inv_u, w, zt = bound(z)
            r = shift * one - w * inv_u
            guesses.append(((gain * inv_u) * mm1(zt.astype(BF16), r.astype(BF16))).astype(BF16))
            lows.append((factor * ETA * ETA) * inv_u)
        low = lowest(lows)
        rise = gain * (shift - FLOOR)
        count = sum((low < FLOOR * rise**-k).astype(jnp.int32) for k in range(1, 20))

        def step(shift, gain, guesses):
            rs = [(shift * one - mm1(p[0], x)).astype(BF16) for p, one, x in zip(parts, eyes, guesses)]
            return tuple((gain * mm1(x, r)).astype(BF16) for x, r in zip(guesses, rs))

        guesses = lax.fori_loop(0, count, lambda _, xs: step(shift, gain, xs), tuple(guesses))
        for late_shift, late_gain in last_steps():
            guesses = step(late_shift, late_gain, guesses)
        better = []
        for (zh, zl), one, x in zip(parts, eyes, guesses):
            rh, rl = halves(one - (mm1(zh, x) + mm1(zl, x)))
            better.append(x.astype(F32) + (mm1(x, rh) + mm1(x, rl)))
        size, better = corrected(mats, better)
        sizes.append(size)
        return better

    return inverses


def careful(mats, factor=1.0):
    n = len(mats)
    eyes = [eye(z.shape[0]) for z in mats]
    parts = [halves(z) for z in mats]
    lows, xs = [], []
    for z in mats:
        inv_u, _, zt = bound(z)
        lows.append((ETA * ETA) * inv_u)
        xs.append(zt * inv_u)

    def step(state):
        lows, xs = state
        plans = [scaled(low, 1e-3) for low in lows]
        new = []
        for k in range(n):
            xp = halves(xs[k])
            r = plans[k][0] * eyes[k] - mm3(parts[k], xp)
            new.append(plans[k][1] * mm3(xp, halves(r)))
        return tuple(p[2] for p in plans), tuple(new)

    _, xs = lax.while_loop(lambda state: lowest(state[0]) < 0.999, step, (tuple(lows), tuple(xs)))

    def again(state):
        count, size, _ = state
        return (count < 8) & jnp.logical_not(size <= ENOUGH)

    def more(state):
        count, _, xs = state
        size, xs = corrected(mats, xs)
        return count + 1, size, xs

    size, xs = corrected(mats, xs)
    return lax.while_loop(again, more, (jnp.int32(0), size, xs))[2]


def guarded(run):
    sizes = []
    run(quick(sizes))

    @pl.when(jnp.logical_not(functools.reduce(jnp.maximum, sizes) <= ENOUGH))
    def _():
        run(careful)


def rolled(x, axis):
    n = x.shape[axis]
    if axis == 0:
        return cat([x[n - 64 :], x[: n - 64]], 0)
    return cat([x[:, n - 64 :], x[:, : n - 64]], 1)


def unrolled(x, axis):
    if axis == 0:
        return cat([x[64:], x[:64]], 0)
    return cat([x[:, 64:], x[:, :64]], 1)


def eliminate_body(inverses, energy, onsite, hop):
    h0 = rolled(rolled(hop[0], 0), 1)
    h1 = rolled(rolled(hop[1], 0), 1)
    on = rolled(onsite, 1)
    one = eye(256)
    ar = one * (energy - on) - (h0 + h0.T) * 0.5
    ai = one * ETA - (h1 - h1.T) * 0.5

    def part(rows, cols):
        return blk(ar[rows, cols], ai[rows, cols])

    b, i = slice(0, 128), slice(128, 256)
    (inner,) = inverses([part(i, i)], 1.0)
    abi = part(b, i)
    y = mm(abi, inner)
    z = mm(inner, part(i, b))
    s = part(b, b) - mm(abi, z)
    return s, inner[:128], y, z[:128]


def corners(s):
    r, i = pair(s)
    lo, hi = slice(0, 64), slice(64, 128)
    return [[blk(r[p, q], i[p, q]) for q in (lo, hi)] for p in (lo, hi)]


def lead_of(slab, c):
    return jnp.where(slab == 0, mm(c, c, NT), 0.0)


def maps_body(inverses, slab, s, couple, next_top):
    (bb, bf), (fb, ff) = corners(s)
    c = blk(couple[0], couple[1])
    cn = full(next_top)
    ff = ff + times_i(lead_of(slab, c))
    ib, if_ = inverses([bb, ff])
    b = -mm(ib, bf)
    d = -mm(fb, ib)
    phi = ff + mm(d, bf)
    br = -mm(if_, fb)
    dr = -mm(bf, if_)
    psi = bb + mm(dr, fb)
    ct = c.T
    cnt = cn.T
    left = [mm(mm(cn, ib), cnt), mm(cn, b), mm(d, cnt), phi]
    right = [mm(mm(ct, if_), c), mm(ct, br), mm(dr, c), psi]
    raw = [ib, b, d, phi]
    return [u[:64] for u in left], [u[:64] for u in right], [u[:64] for u in raw]


def compose(outer, inner, phi_inv):
    a2, b2, d2, _ = outer
    a1, b1, d1, phi1 = inner
    pq = mm(phi_inv, cat([b1, d2], 1))
    quad = mm(cat([b2, d1], 0), pq)
    n = a1.shape[0]
    return [a2 + quad[:n, n:], quad[:n, :n], quad[n:, n:], phi1 - quad[n:, :n]]


def level(inverses, slots):
    phis = inverses([outer[3] - inner[0] for outer, inner in slots])
    return [[u[:64] for u in compose(o, i, p)] for (o, i), p in zip(slots, phis)]


def constant_map(value):
    zero = jnp.zeros_like(value)
    return [value, zero, zero, imag_eye(64)]


def choose(cond, one, other):
    return [jnp.where(cond, x, y) for x, y in zip(one, other)]


def tree_body(inverses, slab, sent, put, get):
    none = constant_map(jnp.zeros((128, 128), F32))

    def wide(tops):
        return [full(u) for u in tops]

    lefts = (slab + 1) // 2

    def fetch(is_left, place):
        source = jnp.where(is_left, slab - 1 - place, slab + 1 + place)
        there = (source >= 0) & (source < 8)
        return choose(there, wide(sent(jnp.clip(source, 0, 7))), none)

    slots = []
    for k in range(4):
        is_left = k < lefts
        place = 2 * jnp.where(is_left, k, k - lefts)
        slots.append((fetch(is_left, place), fetch(is_left, place + 1)))
    for k, m in enumerate(level(inverses, slots)):
        put(k, m)

    twos = (lefts + 1) // 2
    slots = []
    for k in range(3):
        is_left = k < twos
        first = jnp.where(is_left, 2 * k, lefts + 2 * (k - twos))
        stop = jnp.where(is_left, lefts, 4)
        outer = choose(first < stop, wide(get(jnp.minimum(first, 3))), none)
        inner = choose(first + 1 < stop, wide(get(jnp.minimum(first + 1, 3))), none)
        slots.append((outer, inner))
    for k, m in enumerate(level(inverses, slots)):
        put(4 + k, m)

    slots = []
    for first, stop in ((0, twos), (twos, 3)):
        outer = choose(first < stop, wide(get(4 + jnp.minimum(first, 2))), none)
        inner = choose(first + 1 < stop, wide(get(4 + jnp.minimum(first + 1, 2))), none)
        slots.append((outer, inner))
    phis = inverses([outer[3] - inner[0] for outer, inner in slots])
    return [o[0] + mm(mm(o[1], p), o[2]) for (o, _), p in zip(slots, phis)]


def close_body(inverses, slab, couple, sig_l, sig_r, s, inner, y, z, raw):
    ib, b, d, phi = [full(u) for u in raw]
    lr, li = pair(sig_l - times_i(lead_of(slab, blk(couple[0], couple[1]))))
    rr, ri = pair(sig_r)
    zero = jnp.zeros((64, 64), F32)

    def spread(x, w):
        return cat([cat([x, zero], 1), cat([zero, w], 1)], 0)

    closed = s - blk(spread(rr, lr), spread(ri, li))
    e_inv, big = inverses([phi - sig_l, closed])
    be = mm(b, e_inv)
    gfb = mm(e_inv, d)
    gbb = ib + mm(be, d)

    def joined(k):
        return cat([cat([pair(gbb)[k], pair(be)[k]], 1), cat([pair(gfb)[k], pair(e_inv)[k]], 1)], 0)

    small = cat([joined(0), -joined(1)], 1)
    return big[:128], small


def restore(top, inner, y, z):
    ty = mm(top, y)
    zt = mm(z, full(top))
    zty = mm(zt, y)
    low = inner + zty
    r = cat([cat([top[:, :128], -ty[:, :128]], 1), cat([-zt[:, :128], low[:, :128]], 1)], 0)
    i = cat([cat([-top[:, 128:], ty[:, 128:]], 1), cat([zt[:, 128:], -low[:, 128:]], 1)], 0)
    return r, i


def for_rows(r, i):
    r, i = [unrolled(unrolled(x, 0), 1).reshape(32, 8, 256) for x in (r, i)]
    upper = lax.broadcasted_iota(jnp.int32, (32, 8, 256), 1) < 4

    def swapped(x):
        return cat([x[:, 4:], x[:, :4]], 1)

    even = jnp.where(upper, r, swapped(i))
    odd = jnp.where(upper, swapped(r), i)
    return even, odd


def right_adj(lr, li, gr, gi):
    n = lr.shape[0]
    rows = cat([cat([lr, li], 1), cat([li, -lr], 1)], 0)
    out = mm(rows, cat([gr, gi], 1), NT)
    return out[:n], out[n:]


def lesser_parts_body(slab, big, small, y, inject, couple, next_top):
    rest = mm(cat([small, big], 0), y)
    gr, gi = cat([small[:, :128], -rest[:128, :128]], 1), cat([-small[:, 128:], rest[:128, 128:]], 1)
    fr, fi = cat([big[:, :128], -rest[128:, :128]], 1), cat([-big[:, 128:], rest[128:, 128:]], 1)
    hr, hi = 1.5 * gr - fr, 1.5 * gi - fi
    d = rolled(inject, 1)
    lr = cat([gr[:64], hr[64:]], 0) * d
    li = cat([gi[:64], hi[64:]], 0) * d
    mr, mi = right_adj(lr, li, gr, gi)
    c = blk(couple[0], couple[1])
    cn = full(next_top)
    ct, cnt = c.T, cn.T
    w = mm(mm(cn, blk(-mi[:64, :64], mr[:64, :64])), cnt)
    beta = mm(cn, blk(gr[:64, 64:128], gi[:64, 64:128]))
    w = w + mm(mm(beta, times_i(lead_of(slab, c))), beta, NT)
    w = (w - w.T) * 0.5
    q = mm(mm(ct, blk(-mi[64:, 64:], mr[64:, 64:])), c)
    q = q - q.T
    left = mm(
        ct,
        cat(
            [
                blk(gr[64:128, 64:128], gi[64:128, 64:128]),
                blk(hr[64:128, 64:128], hi[64:128, 64:128]),
                blk(gr[64:128, :64], gi[64:128, :64]),
            ],
            1,
        ),
    )
    u, v, zz = left[:, :128], left[:, 128:256], left[:, 256:]
    return [m[:64] for m in (w + times_i(q), beta, u, v, zz)]


def lesser_body(slab, couple, parts, big, small, inner, y, z, inject):
    mine = times_i(lead_of(slab, blk(couple[0], couple[1])))
    sources = {}
    packed = [full(parts(t, 0)) for t in range(8)]
    for t in range(8):
        if t:
            beta = full(parts(t - 1, 1))
            both = packed[t - 1]
            w = (both - both.T) * 0.5
            sig = w + mm(mm(beta, sig), beta, NT) if t > 1 else w
            mine = jnp.where(slab == t, sig, mine)
            c = mm(mm(full(parts(t, 3)), sig), full(parts(t, 2)), NT)
            sources[t] = c - c.T - times_i((packed[t] + packed[t].T) * 0.5)
    back = jnp.zeros_like(sig)
    my_back = back
    for t in range(7, 0, -1):
        zz = full(parts(t, 4))
        back = sources[t] + mm(mm(zz, back), zz, NT)
        my_back = jnp.where(slab == t - 1, back, my_back)
    gr, gi = restore(small, inner, y, z)
    fr, fi = restore(big, inner, y, z)
    hr, hi = 1.5 * gr - fr, 1.5 * gi - fi
    d = rolled(inject, 1)
    right_r, right_i = pair(mine)
    back_r, back_i = pair(0.5 * my_back)

    def cols(xr, xi, m):
        out = mm(cat([xr, xi], 1), m)
        return out

    fm = cat([cat([right_r, right_i], 1), cat([-right_i, right_r], 1)], 0)
    bm = cat([cat([back_r, back_i], 1), cat([-back_i, back_r], 1)], 0)
    on_f = cols(hr[:, 64:128], hi[:, 64:128], fm)
    on_b = cols(gr[:, :64], gi[:, :64], bm)
    add_r = cat([on_b[:, :64], on_f[:, :64]], 1)
    add_i = cat([on_b[:, 64:], on_f[:, 64:]], 1)
    lr, li = -hi * d, hr * d
    lr = cat([lr[:, :128] + add_r, lr[:, 128:]], 1)
    li = cat([li[:, :128] + add_i, li[:, 128:]], 1)
    nr, ni = right_adj(lr, li, gr, gi)
    return nr - nr.T, ni + ni.T


VM = pl.BlockSpec(memory_space=pltpu.VMEM)
SM = pl.BlockSpec(memory_space=pltpu.SMEM)


def call(kernel, outs, specs, micros, scratch=()):
    return pl.pallas_call(
        kernel,
        out_shape=[jax.ShapeDtypeStruct(o, F32) for o in outs],
        in_specs=specs,
        out_specs=[VM] * len(outs),
        scratch_shapes=list(scratch),
        compiler_params=pltpu.CompilerParams(vmem_limit_bytes=40 * 2**20),
        cost_estimate=pl.CostEstimate(flops=int(micros * 1.1e9), bytes_accessed=1 << 20, transcendentals=0),
    )


def put(ref, values):
    for k, v in enumerate(values):
        ref[k] = v


def maps_kernel(slab, energy, onsite, hop, couple, next_top, s, inner, y, z, sends, raw):
    chip, core = slab[0] // 2, lax.rem(slab[0], 2)

    def run(inverses):
        s[...], inner[...], y[...], z[...] = eliminate_body(inverses, energy[0], onsite[...], (hop[0, 0], hop[1, 0]))
        left, right, own = maps_body(inverses, slab[0], s[...], (couple[0, 0], couple[1, 0]), next_top[...])
        put(raw, own)
        for t in range(4):
            put(sends.at[t], choose((chip < t) | ((chip == t) & (core == 0)), left, right))

    guarded(run)


def put_rows(ref, r, i):
    even, odd = for_rows(r, i)
    ref[:, 0] = even
    ref[:, 1] = odd


def close_kernel(
    slab, couple, next_top, inject, near, far, s, inner, y, z, raw, rows, big, small, parts, kept
):
    me = slab[0]
    own_couple = (couple[0, 0], couple[1, 0])

    def sent(t):
        same = lax.rem(t, 2) == lax.rem(me, 2)
        return [jnp.where(same, near[t // 2, k], far[t // 2, k]) for k in range(4)]

    def run(inverses):
        def get(t):
            return [kept[t, k] for k in range(4)]

        sig_l, sig_r = tree_body(inverses, me, sent, lambda k, m: put(kept.at[k], m), get)
        own = [raw[k] for k in range(4)]
        whole, corner = close_body(
            inverses, me, own_couple, sig_l, sig_r, s[...], inner[...], y[...], z[...], own
        )
        big[...], small[...] = whole, corner
        put(parts, lesser_parts_body(me, whole, corner, y[...], inject[:, 0], own_couple, next_top[...]))
        put_rows(rows, *restore(whole, inner[...], y[...], z[...]))

    guarded(run)


def lesser_kernel(slab, couple, parts, big, small, inner, y, z, inject, rows):
    r, i = lesser_body(
        slab[0],
        (couple[0, 0], couple[1, 0]),
        lambda t, k: parts[t, k],
        big[...],
        small[...],
        inner[...],
        y[...],
        z[...],
        inject[:, 0],
    )
    put_rows(rows, r, i)


def convolve_kernel(table, piece, out):
    for j in range(4):
        x = cat([piece[:, j], piece[:, 4 + j]], 0)
        o = mm(table[...], x)
        out[0, 0, :, j] = o[:64]
        out[1, 0, :, j] = o[64:]


def tables_kernel(kern, out):
    for k in range(2):
        t = []
        for c in range(2):
            x = jnp.broadcast_to(kern[k, c : c + 1, :], (64, 128))
            t.append(pltpu.roll(x, 65, 1, stride=1, stride_axis=0)[:, :64])
        out[k] = blk(t[0], t[1])


def per_device(energies, onsite, hopping, coupling, injection, kernels):
    slab = lax.axis_index("slab").astype(jnp.int32).reshape(1)

    def swapped_over(x, axis):
        return lax.all_to_all(x, axis, split_axis=0, concat_axis=0, tiled=True)

    top = jnp.concatenate([coupling[0, 0], -coupling[1, 0]], axis=1)
    next_top = lax.ppermute(top, "slab", [(t, (t + 7) % 8) for t in range(8)])
    m256, half = (256, 256), (128, 256)
    port = (4, 64, 128)
    s, inner, y, z, sends, raw = call(
        maps_kernel, [m256, half, m256, half, (4, *port), port], [SM, SM] + [VM] * 4, 11
    )(slab, energies, onsite, hopping, coupling, next_top)
    near = lax.all_to_all(
        sends, "slab", split_axis=0, concat_axis=0, tiled=True, axis_index_groups=[[0, 2, 4, 6], [1, 3, 5, 7]]
    )
    far = lax.ppermute(near, "slab", [(t, t ^ 1) for t in range(8)])
    rows, big, small, parts = call(
        close_kernel,
        [(32, 2, 8, 256), half, half, (5, 64, 128)],
        [SM] + [VM] * 10,
        25,
        [pltpu.VMEM((7, 4, 64, 128), F32)],
    )(slab, coupling, next_top, injection, near, far, s, inner, y, z, raw)

    def to_rows(x):
        return swapped_over(x.reshape(64, 8, 256), "energy")

    got_r = to_rows(rows)
    all_parts = lax.all_gather(parts, "slab")
    late_kernels, _ = lax.optimization_barrier((kernels, parts))
    reversed_kernels = jnp.pad(late_kernels[:, :, ::-1], ((0, 0), (0, 0), (0, 1)))
    (tables,) = call(tables_kernel, [(2, 128, 128)], [VM], 1)(reversed_kernels)
    (rows_l,) = call(lesser_kernel, [(32, 2, 8, 256)], [SM] + [VM] * 8, 8)(
        slab, coupling, all_parts, big, small, inner, y, z, injection
    )
    got_l = to_rows(rows_l)
    conv = call(convolve_kernel, [(2, 1, 64, 4, 256)], [VM] * 2, 2)
    return conv(tables[0], got_r)[0], conv(tables[1], got_l)[0]


def solution(mesh):
    in_specs = (
        P("energy"),
        P("slab", None),
        P(None, "slab", None, None),
        P(None, "slab", None, None),
        P("energy", "slab", None),
        P(),
    )
    out_specs = (P(None, "slab", None, "energy", None), P(None, "slab", None, "energy", None))
    return jax.shard_map(per_device, mesh=mesh, in_specs=in_specs, out_specs=out_specs, check_vma=False)
```

```python
import functools

import jax
import jax.numpy as jnp
from jax import lax
from jax.experimental import pallas as pl
from jax.experimental.pallas import tpu as pltpu
from jax.sharding import PartitionSpec as P

ETA = 0.02
F32 = jnp.float32
BF16 = jnp.bfloat16
NN = (((1,), (0,)), ((), ()))
NT = (((1,), (1,)), ((), ()))


def mmh(a, b, dims=NN):
    return lax.dot_general(a, b, dims, precision=lax.Precision.HIGHEST, preferred_element_type=F32)


def halves(x):
    high = x.astype(BF16)
    return high, (x - high.astype(F32)).astype(BF16)


def mm1(a, b, dims=NN):
    return lax.dot_general(a, b, dims, preferred_element_type=F32)


def mm3(a, b, dims=NN):
    return mm1(a[0], b[0], dims) + (mm1(a[0], b[1], dims) + mm1(a[1], b[0], dims))


def mm(a, b, dims=NN):
    return mm3(halves(a), halves(b), dims)


def cat(parts, axis):
    return jnp.concatenate(parts, axis=axis)


def blk(r, i):
    return cat([cat([r, -i], 1), cat([i, r], 1)], 0)


def pair(z):
    n = z.shape[1] // 2
    return z[:n, :n], -z[:n, n:]


def full(top):
    n = top.shape[0]
    return cat([top, cat([-top[:, n:], top[:, :n]], 1)], 0)


def eye(n):
    return (lax.broadcasted_iota(jnp.int32, (n, n), 0) == lax.broadcasted_iota(jnp.int32, (n, n), 1)).astype(F32)


def imag_eye(n):
    return blk(jnp.zeros((n, n), F32), eye(n))


def times_i(z):
    n = z.shape[0] // 2
    return cat([-z[n:], z[:n]], 0)


def lowest(values):
    return functools.reduce(jnp.minimum, values)


def scaled(low, floor):
    base = jnp.maximum(low, floor)
    shift = 1.0 + base
    gain = 4.0 / (shift * shift)
    return shift, gain, jnp.minimum(gain * low * (shift - low), gain * base)


ENOUGH = 1e-4


def corrected(mats, xs):
    rs = [eye(z.shape[0]) - mmh(z, x) for z, x in zip(mats, xs)]
    size = functools.reduce(jnp.maximum, [jnp.sum(r * r) for r in rs])
    return size, tuple(x + mm1(x.astype(BF16), r.astype(BF16)) for x, r in zip(xs, rs))


def bound(z):
    zt = z.T
    w = mm1(z.astype(BF16), zt.astype(BF16))
    return 1.0 / (1.01 * jnp.max(jnp.sum(jnp.abs(w), axis=1, keepdims=True))), w, zt


FLOOR = 0.035


def last_steps():
    low = FLOOR
    for _ in range(4):
        shift = 1.0 + low
        gain = 4.0 / (shift * shift)
        yield shift, gain
        low *= gain


def quick(sizes):
    def inverses(mats, factor=2.0):
        eyes = [eye(z.shape[0]) for z in mats]
        parts = [halves(z) for z in mats]
        shift = 1.0 + FLOOR
        gain = 4.0 / (shift * shift)
        lows, guesses = [], []
        for z, one in zip(mats, eyes):
            inv_u, w, zt = bound(z)
            r = shift * one - w * inv_u
            guesses.append(((gain * inv_u) * mm1(zt.astype(BF16), r.astype(BF16))).astype(BF16))
            lows.append((factor * ETA * ETA) * inv_u)
        low = lowest(lows)
        rise = gain * (shift - FLOOR)
        count = sum((low < FLOOR * rise**-k).astype(jnp.int32) for k in range(1, 20))

        def step(shift, gain, guesses):
            rs = [(shift * one - mm1(p[0], x)).astype(BF16) for p, one, x in zip(parts, eyes, guesses)]
            return tuple((gain * mm1(x, r)).astype(BF16) for x, r in zip(guesses, rs))

        guesses = lax.fori_loop(0, count, lambda _, xs: step(shift, gain, xs), tuple(guesses))
        for late_shift, late_gain in last_steps():
            guesses = step(late_shift, late_gain, guesses)
        better = []
        for (zh, zl), one, x in zip(parts, eyes, guesses):
            rh, rl = halves(one - (mm1(zh, x) + mm1(zl, x)))
            better.append(x.astype(F32) + (mm1(x, rh) + mm1(x, rl)))
        size, better = corrected(mats, better)
        sizes.append(size)
        return better

    return inverses


def careful(mats, factor=1.0):
    n = len(mats)
    eyes = [eye(z.shape[0]) for z in mats]
    parts = [halves(z) for z in mats]
    lows, xs = [], []
    for z in mats:
        inv_u, _, zt = bound(z)
        lows.append((ETA * ETA) * inv_u)
        xs.append(zt * inv_u)

    def step(state):
        lows, xs = state
        plans = [scaled(low, 1e-3) for low in lows]
        new = []
        for k in range(n):
            xp = halves(xs[k])
            r = plans[k][0] * eyes[k] - mm3(parts[k], xp)
            new.append(plans[k][1] * mm3(xp, halves(r)))
        return tuple(p[2] for p in plans), tuple(new)

    _, xs = lax.while_loop(lambda state: lowest(state[0]) < 0.999, step, (tuple(lows), tuple(xs)))

    def again(state):
        count, size, _ = state
        return (count < 8) & jnp.logical_not(size <= ENOUGH)

    def more(state):
        count, _, xs = state
        size, xs = corrected(mats, xs)
        return count + 1, size, xs

    size, xs = corrected(mats, xs)
    return lax.while_loop(again, more, (jnp.int32(0), size, xs))[2]


def guarded(run):
    sizes = []
    run(quick(sizes))

    @pl.when(jnp.logical_not(functools.reduce(jnp.maximum, sizes) <= ENOUGH))
    def _():
        run(careful)


def rolled(x, axis):
    n = x.shape[axis]
    if axis == 0:
        return cat([x[n - 64 :], x[: n - 64]], 0)
    return cat([x[:, n - 64 :], x[:, : n - 64]], 1)


def unrolled(x, axis):
    if axis == 0:
        return cat([x[64:], x[:64]], 0)
    return cat([x[:, 64:], x[:, :64]], 1)


def eliminate_body(inverses, energy, onsite, hop):
    h0 = rolled(rolled(hop[0], 0), 1)
    h1 = rolled(rolled(hop[1], 0), 1)
    on = rolled(onsite, 1)
    one = eye(256)
    ar = one * (energy - on) - (h0 + h0.T) * 0.5
    ai = one * ETA - (h1 - h1.T) * 0.5

    def part(rows, cols):
        return blk(ar[rows, cols], ai[rows, cols])

    b, i = slice(0, 128), slice(128, 256)
    (inner,) = inverses([part(i, i)], 1.0)
    abi = part(b, i)
    y = mm(abi, inner)
    z = mm(inner, part(i, b))
    s = part(b, b) - mm(abi, z)
    return s, inner[:128], y, z[:128]


def corners(s):
    r, i = pair(s)
    lo, hi = slice(0, 64), slice(64, 128)
    return [[blk(r[p, q], i[p, q]) for q in (lo, hi)] for p in (lo, hi)]


def lead_of(slab, c):
    return jnp.where(slab == 0, mm(c, c, NT), 0.0)


def maps_body(inverses, slab, s, couple, next_top):
    (bb, bf), (fb, ff) = corners(s)
    c = blk(couple[0], couple[1])
    cn = full(next_top)
    ff = ff + times_i(lead_of(slab, c))
    ib, if_ = inverses([bb, ff])
    b = -mm(ib, bf)
    d = -mm(fb, ib)
    phi = ff + mm(d, bf)
    br = -mm(if_, fb)
    dr = -mm(bf, if_)
    psi = bb + mm(dr, fb)
    ct = c.T
    cnt = cn.T
    left = [mm(mm(cn, ib), cnt), mm(cn, b), mm(d, cnt), phi]
    right = [mm(mm(ct, if_), c), mm(ct, br), mm(dr, c), psi]
    raw = [ib, b, d, phi]
    return [u[:64] for u in left], [u[:64] for u in right], [u[:64] for u in raw]


def compose(outer, inner, phi_inv):
    a2, b2, d2, _ = outer
    a1, b1, d1, phi1 = inner
    pq = mm(phi_inv, cat([b1, d2], 1))
    quad = mm(cat([b2, d1], 0), pq)
    n = a1.shape[0]
    return [a2 + quad[:n, n:], quad[:n, :n], quad[n:, n:], phi1 - quad[n:, :n]]


def level(inverses, slots):
    phis = inverses([outer[3] - inner[0] for outer, inner in slots])
    return [[u[:64] for u in compose(o, i, p)] for (o, i), p in zip(slots, phis)]


def constant_map(value):
    zero = jnp.zeros_like(value)
    return [value, zero, zero, imag_eye(64)]


def choose(cond, one, other):
    return [jnp.where(cond, x, y) for x, y in zip(one, other)]


def tree_body(inverses, slab, sent, put, get):
    none = constant_map(jnp.zeros((128, 128), F32))

    def wide(tops):
        return [full(u) for u in tops]

    lefts = (slab + 1) // 2

    def fetch(is_left, place):
        source = jnp.where(is_left, slab - 1 - place, slab + 1 + place)
        there = (source >= 0) & (source < 8)
        return choose(there, wide(sent(jnp.clip(source, 0, 7))), none)

    slots = []
    for k in range(4):
        is_left = k < lefts
        place = 2 * jnp.where(is_left, k, k - lefts)
        slots.append((fetch(is_left, place), fetch(is_left, place + 1)))
    for k, m in enumerate(level(inverses, slots)):
        put(k, m)

    twos = (lefts + 1) // 2
    slots = []
    for k in range(3):
        is_left = k < twos
        first = jnp.where(is_left, 2 * k, lefts + 2 * (k - twos))
        stop = jnp.where(is_left, lefts, 4)
        outer = choose(first < stop, wide(get(jnp.minimum(first, 3))), none)
        inner = choose(first + 1 < stop, wide(get(jnp.minimum(first + 1, 3))), none)
        slots.append((outer, inner))
    for k, m in enumerate(level(inverses, slots)):
        put(4 + k, m)

    slots = []
    for first, stop in ((0, twos), (twos, 3)):
        outer = choose(first < stop, wide(get(4 + jnp.minimum(first, 2))), none)
        inner = choose(first + 1 < stop, wide(get(4 + jnp.minimum(first + 1, 2))), none)
        slots.append((outer, inner))
    phis = inverses([outer[3] - inner[0] for outer, inner in slots])
    return [o[0] + mm(mm(o[1], p), o[2]) for (o, _), p in zip(slots, phis)]


def close_body(inverses, slab, couple, sig_l, sig_r, s, inner, y, z, raw):
    ib, b, d, phi = [full(u) for u in raw]
    lr, li = pair(sig_l - times_i(lead_of(slab, blk(couple[0], couple[1]))))
    rr, ri = pair(sig_r)
    zero = jnp.zeros((64, 64), F32)

    def spread(x, w):
        return cat([cat([x, zero], 1), cat([zero, w], 1)], 0)

    closed = s - blk(spread(rr, lr), spread(ri, li))
    e_inv, big = inverses([phi - sig_l, closed])
    be = mm(b, e_inv)
    gfb = mm(e_inv, d)
    gbb = ib + mm(be, d)

    def joined(k):
        return cat([cat([pair(gbb)[k], pair(be)[k]], 1), cat([pair(gfb)[k], pair(e_inv)[k]], 1)], 0)

    small = cat([joined(0), -joined(1)], 1)
    return big[:128], small


def restore(top, inner, y, z):
    ty = mm(top, y)
    zt = mm(z, full(top))
    zty = mm(zt, y)
    low = inner + zty
    r = cat([cat([top[:, :128], -ty[:, :128]], 1), cat([-zt[:, :128], low[:, :128]], 1)], 0)
    i = cat([cat([-top[:, 128:], ty[:, 128:]], 1), cat([zt[:, 128:], -low[:, 128:]], 1)], 0)
    return r, i


def for_rows(r, i):
    r, i = [unrolled(unrolled(x, 0), 1).reshape(32, 8, 256) for x in (r, i)]
    upper = lax.broadcasted_iota(jnp.int32, (32, 8, 256), 1) < 4

    def swapped(x):
        return cat([x[:, 4:], x[:, :4]], 1)

    even = jnp.where(upper, r, swapped(i))
    odd = jnp.where(upper, swapped(r), i)
    return even, odd


def right_adj(lr, li, gr, gi):
    n = lr.shape[0]
    rows = cat([cat([lr, li], 1), cat([li, -lr], 1)], 0)
    out = mm(rows, cat([gr, gi], 1), NT)
    return out[:n], out[n:]


def lesser_parts_body(slab, big, small, y, inject, couple, next_top):
    rest = mm(cat([small, big], 0), y)
    gr, gi = cat([small[:, :128], -rest[:128, :128]], 1), cat([-small[:, 128:], rest[:128, 128:]], 1)
    fr, fi = cat([big[:, :128], -rest[128:, :128]], 1), cat([-big[:, 128:], rest[128:, 128:]], 1)
    hr, hi = 1.5 * gr - fr, 1.5 * gi - fi
    d = rolled(inject, 1)
    lr = cat([gr[:64], hr[64:]], 0) * d
    li = cat([gi[:64], hi[64:]], 0) * d
    mr, mi = right_adj(lr, li, gr, gi)
    c = blk(couple[0], couple[1])
    cn = full(next_top)
    ct, cnt = c.T, cn.T
    w = mm(mm(cn, blk(-mi[:64, :64], mr[:64, :64])), cnt)
    beta = mm(cn, blk(gr[:64, 64:128], gi[:64, 64:128]))
    w = w + mm(mm(beta, times_i(lead_of(slab, c))), beta, NT)
    w = (w - w.T) * 0.5
    q = mm(mm(ct, blk(-mi[64:, 64:], mr[64:, 64:])), c)
    q = q - q.T
    left = mm(
        ct,
        cat(
            [
                blk(gr[64:128, 64:128], gi[64:128, 64:128]),
                blk(hr[64:128, 64:128], hi[64:128, 64:128]),
                blk(gr[64:128, :64], gi[64:128, :64]),
            ],
            1,
        ),
    )
    u, v, zz = left[:, :128], left[:, 128:256], left[:, 256:]
    return [m[:64] for m in (w + times_i(q), beta, u, v, zz)]


def lesser_body(slab, couple, parts, big, small, inner, y, z, inject):
    mine = times_i(lead_of(slab, blk(couple[0], couple[1])))
    sources = {}
    packed = [full(parts(t, 0)) for t in range(8)]
    for t in range(8):
        if t:
            beta = full(parts(t - 1, 1))
            both = packed[t - 1]
            w = (both - both.T) * 0.5
            sig = w + mm(mm(beta, sig), beta, NT) if t > 1 else w
            mine = jnp.where(slab == t, sig, mine)
            c = mm(mm(full(parts(t, 3)), sig), full(parts(t, 2)), NT)
            sources[t] = c - c.T - times_i((packed[t] + packed[t].T) * 0.5)
    back = jnp.zeros_like(sig)
    my_back = back
    for t in range(7, 0, -1):
        zz = full(parts(t, 4))
        back = sources[t] + mm(mm(zz, back), zz, NT)
        my_back = jnp.where(slab == t - 1, back, my_back)
    gr, gi = restore(small, inner, y, z)
    fr, fi = restore(big, inner, y, z)
    hr, hi = 1.5 * gr - fr, 1.5 * gi - fi
    d = rolled(inject, 1)
    right_r, right_i = pair(mine)
    back_r, back_i = pair(0.5 * my_back)

    def cols(xr, xi, m):
        out = mm(cat([xr, xi], 1), m)
        return out

    fm = cat([cat([right_r, right_i], 1), cat([-right_i, right_r], 1)], 0)
    bm = cat([cat([back_r, back_i], 1), cat([-back_i, back_r], 1)], 0)
    on_f = cols(hr[:, 64:128], hi[:, 64:128], fm)
    on_b = cols(gr[:, :64], gi[:, :64], bm)
    add_r = cat([on_b[:, :64], on_f[:, :64]], 1)
    add_i = cat([on_b[:, 64:], on_f[:, 64:]], 1)
    lr, li = -hi * d, hr * d
    lr = cat([lr[:, :128] + add_r, lr[:, 128:]], 1)
    li = cat([li[:, :128] + add_i, li[:, 128:]], 1)
    nr, ni = right_adj(lr, li, gr, gi)
    return nr - nr.T, ni + ni.T


VM = pl.BlockSpec(memory_space=pltpu.VMEM)
SM = pl.BlockSpec(memory_space=pltpu.SMEM)


def call(kernel, outs, specs, micros, scratch=()):
    return pl.pallas_call(
        kernel,
        out_shape=[jax.ShapeDtypeStruct(o, F32) for o in outs],
        in_specs=specs,
        out_specs=[VM] * len(outs),
        scratch_shapes=list(scratch),
        compiler_params=pltpu.CompilerParams(vmem_limit_bytes=40 * 2**20),
        cost_estimate=pl.CostEstimate(flops=int(micros * 1.1e9), bytes_accessed=1 << 20, transcendentals=0),
    )


def put(ref, values):
    for k, v in enumerate(values):
        ref[k] = v


def eliminate_kernel(energy, onsite, hop, s, inner, y, z):
    def run(inverses):
        s[...], inner[...], y[...], z[...] = eliminate_body(inverses, energy[0], onsite[...], (hop[0, 0], hop[1, 0]))

    guarded(run)


def maps_kernel(slab, s, couple, next_top, sends, raw):
    chip, core = slab[0] // 2, lax.rem(slab[0], 2)

    def run(inverses):
        left, right, own = maps_body(inverses, slab[0], s[...], (couple[0, 0], couple[1, 0]), next_top[...])
        put(raw, own)
        for t in range(4):
            put(sends.at[t], choose((chip < t) | ((chip == t) & (core == 0)), left, right))

    guarded(run)


def put_rows(ref, r, i):
    even, odd = for_rows(r, i)
    ref[:, 0] = even
    ref[:, 1] = odd


def close_kernel(
    slab, couple, next_top, inject, near, far, s, inner, y, z, raw, rows, big, small, parts, kept
):
    me = slab[0]
    own_couple = (couple[0, 0], couple[1, 0])

    def sent(t):
        same = lax.rem(t, 2) == lax.rem(me, 2)
        return [jnp.where(same, near[t // 2, k], far[t // 2, k]) for k in range(4)]

    def run(inverses):
        def get(t):
            return [kept[t, k] for k in range(4)]

        sig_l, sig_r = tree_body(inverses, me, sent, lambda k, m: put(kept.at[k], m), get)
        own = [raw[k] for k in range(4)]
        whole, corner = close_body(
            inverses, me, own_couple, sig_l, sig_r, s[...], inner[...], y[...], z[...], own
        )
        big[...], small[...] = whole, corner
        put(parts, lesser_parts_body(me, whole, corner, y[...], inject[:, 0], own_couple, next_top[...]))
        put_rows(rows, *restore(whole, inner[...], y[...], z[...]))

    guarded(run)


def lesser_kernel(slab, couple, parts, big, small, inner, y, z, inject, rows):
    r, i = lesser_body(
        slab[0],
        (couple[0, 0], couple[1, 0]),
        lambda t, k: parts[t, k],
        big[...],
        small[...],
        inner[...],
        y[...],
        z[...],
        inject[:, 0],
    )
    put_rows(rows, r, i)


def convolve_kernel(table, piece, out):
    for j in range(4):
        x = cat([piece[:, j], piece[:, 4 + j]], 0)
        o = mm(table[...], x)
        out[0, 0, :, j] = o[:64]
        out[1, 0, :, j] = o[64:]


def tables_kernel(kern, out):
    for k in range(2):
        t = []
        for c in range(2):
            x = jnp.broadcast_to(kern[k, c : c + 1, :], (64, 128))
            t.append(pltpu.roll(x, 65, 1, stride=1, stride_axis=0)[:, :64])
        out[k] = blk(t[0], t[1])


def per_device(energies, onsite, hopping, coupling, injection, kernels):
    slab = lax.axis_index("slab").astype(jnp.int32).reshape(1)

    def swapped_over(x, axis):
        return lax.all_to_all(x, axis, split_axis=0, concat_axis=0, tiled=True)

    top = jnp.concatenate([coupling[0, 0], -coupling[1, 0]], axis=1)
    next_top = lax.ppermute(top, "slab", [(t, (t + 7) % 8) for t in range(8)])
    m256, half = (256, 256), (128, 256)
    port = (4, 64, 128)
    s, inner, y, z = call(eliminate_kernel, [m256, half, m256, half], [SM, VM, VM], 6)(energies, onsite, hopping)
    sends, raw = call(maps_kernel, [(4, *port), port], [SM] + [VM] * 3, 5)(slab, s, coupling, next_top)
    near = lax.all_to_all(
        sends, "slab", split_axis=0, concat_axis=0, tiled=True, axis_index_groups=[[0, 2, 4, 6], [1, 3, 5, 7]]
    )
    far = lax.ppermute(near, "slab", [(t, t ^ 1) for t in range(8)])
    rows, big, small, parts = call(
        close_kernel,
        [(32, 2, 8, 256), half, half, (5, 64, 128)],
        [SM] + [VM] * 10,
        25,
        [pltpu.VMEM((7, 4, 64, 128), F32)],
    )(slab, coupling, next_top, injection, near, far, s, inner, y, z, raw)

    def to_rows(x):
        return swapped_over(x.reshape(64, 8, 256), "energy")

    got_r = to_rows(rows)
    all_parts = lax.all_gather(parts, "slab")
    late_kernels, _ = lax.optimization_barrier((kernels, parts))
    reversed_kernels = jnp.pad(late_kernels[:, :, ::-1], ((0, 0), (0, 0), (0, 1)))
    (tables,) = call(tables_kernel, [(2, 128, 128)], [VM], 1)(reversed_kernels)
    (rows_l,) = call(lesser_kernel, [(32, 2, 8, 256)], [SM] + [VM] * 8, 8)(
        slab, coupling, all_parts, big, small, inner, y, z, injection
    )
    got_l = to_rows(rows_l)
    conv = call(convolve_kernel, [(2, 1, 64, 4, 256)], [VM] * 2, 2)
    return conv(tables[0], got_r)[0], conv(tables[1], got_l)[0]


def solution(mesh):
    in_specs = (
        P("energy"),
        P("slab", None),
        P(None, "slab", None, None),
        P(None, "slab", None, None),
        P("energy", "slab", None),
        P(),
    )
    out_specs = (P(None, "slab", None, "energy", None), P(None, "slab", None, "energy", None))
    return jax.shard_map(per_device, mesh=mesh, in_specs=in_specs, out_specs=out_specs, check_vma=False)
```

```python
import functools

import jax
import jax.numpy as jnp
from jax import lax
from jax.experimental import pallas as pl
from jax.experimental.pallas import tpu as pltpu
from jax.sharding import PartitionSpec as P

ETA = 0.02
F32 = jnp.float32
BF16 = jnp.bfloat16
NN = (((1,), (0,)), ((), ()))
NT = (((1,), (1,)), ((), ()))


def mmh(a, b, dims=NN):
    return lax.dot_general(a, b, dims, precision=lax.Precision.HIGHEST, preferred_element_type=F32)


def halves(x):
    high = x.astype(BF16)
    return high, (x - high.astype(F32)).astype(BF16)


def mm1(a, b, dims=NN):
    return lax.dot_general(a, b, dims, preferred_element_type=F32)


def mm3(a, b, dims=NN):
    return mm1(a[0], b[0], dims) + (mm1(a[0], b[1], dims) + mm1(a[1], b[0], dims))


def mm(a, b, dims=NN):
    return mm3(halves(a), halves(b), dims)


def cat(parts, axis):
    return jnp.concatenate(parts, axis=axis)


def blk(r, i):
    return cat([cat([r, -i], 1), cat([i, r], 1)], 0)


def pair(z):
    n = z.shape[1] // 2
    return z[:n, :n], -z[:n, n:]


def full(top):
    n = top.shape[0]
    return cat([top, cat([-top[:, n:], top[:, :n]], 1)], 0)


def eye(n):
    return (lax.broadcasted_iota(jnp.int32, (n, n), 0) == lax.broadcasted_iota(jnp.int32, (n, n), 1)).astype(F32)


def imag_eye(n):
    return blk(jnp.zeros((n, n), F32), eye(n))


def times_i(z):
    n = z.shape[0] // 2
    return cat([-z[n:], z[:n]], 0)


def lowest(values):
    return functools.reduce(jnp.minimum, values)


def scaled(low, floor):
    base = jnp.maximum(low, floor)
    shift = 1.0 + base
    gain = 4.0 / (shift * shift)
    return shift, gain, jnp.minimum(gain * low * (shift - low), gain * base)


ENOUGH = 1e-4


def corrected(mats, xs):
    rs = [eye(z.shape[0]) - mmh(z, x) for z, x in zip(mats, xs)]
    size = functools.reduce(jnp.maximum, [jnp.sum(r * r) for r in rs])
    return size, tuple(x + mm1(x.astype(BF16), r.astype(BF16)) for x, r in zip(xs, rs))


def bound(z):
    zt = z.T
    w = mm1(z.astype(BF16), zt.astype(BF16))
    return 1.0 / (1.01 * jnp.max(jnp.sum(jnp.abs(w), axis=1, keepdims=True))), w, zt


FLOOR = 0.035


def last_steps():
    low = FLOOR
    for _ in range(4):
        shift = 1.0 + low
        gain = 4.0 / (shift * shift)
        yield shift, gain
        low *= gain


def quick(sizes):
    def inverses(mats, factor=2.0):
        eyes = [eye(z.shape[0]) for z in mats]
        parts = [halves(z) for z in mats]
        shift = 1.0 + FLOOR
        gain = 4.0 / (shift * shift)
        lows, guesses = [], []
        for z, one in zip(mats, eyes):
            inv_u, w, zt = bound(z)
            r = shift * one - w * inv_u
            guesses.append(((gain * inv_u) * mm1(zt.astype(BF16), r.astype(BF16))).astype(BF16))
            lows.append((factor * ETA * ETA) * inv_u)
        low = lowest(lows)
        rise = gain * (shift - FLOOR)
        count = sum((low < FLOOR * rise**-k).astype(jnp.int32) for k in range(1, 20))

        def step(shift, gain, guesses):
            rs = [(shift * one - mm1(p[0], x)).astype(BF16) for p, one, x in zip(parts, eyes, guesses)]
            return tuple((gain * mm1(x, r)).astype(BF16) for x, r in zip(guesses, rs))

        guesses = lax.fori_loop(0, count, lambda _, xs: step(shift, gain, xs), tuple(guesses))
        for late_shift, late_gain in last_steps():
            guesses = step(late_shift, late_gain, guesses)
        better = []
        for (zh, zl), one, x in zip(parts, eyes, guesses):
            rh, rl = halves(one - (mm1(zh, x) + mm1(zl, x)))
            better.append(x.astype(F32) + (mm1(x, rh) + mm1(x, rl)))
        size, better = corrected(mats, better)
        sizes.append(size)
        return better

    return inverses


def careful(mats, factor=1.0):
    n = len(mats)
    eyes = [eye(z.shape[0]) for z in mats]
    parts = [halves(z) for z in mats]
    lows, xs = [], []
    for z in mats:
        inv_u, _, zt = bound(z)
        lows.append((ETA * ETA) * inv_u)
        xs.append(zt * inv_u)

    def step(state):
        lows, xs = state
        plans = [scaled(low, 1e-3) for low in lows]
        new = []
        for k in range(n):
            xp = halves(xs[k])
            r = plans[k][0] * eyes[k] - mm3(parts[k], xp)
            new.append(plans[k][1] * mm3(xp, halves(r)))
        return tuple(p[2] for p in plans), tuple(new)

    _, xs = lax.while_loop(lambda state: lowest(state[0]) < 0.999, step, (tuple(lows), tuple(xs)))

    def again(state):
        count, size, _ = state
        return (count < 8) & jnp.logical_not(size <= ENOUGH)

    def more(state):
        count, _, xs = state
        size, xs = corrected(mats, xs)
        return count + 1, size, xs

    size, xs = corrected(mats, xs)
    return lax.while_loop(again, more, (jnp.int32(0), size, xs))[2]


def guarded(run):
    sizes = []
    run(quick(sizes))

    @pl.when(jnp.logical_not(functools.reduce(jnp.maximum, sizes) <= ENOUGH))
    def _():
        run(careful)


def rolled(x, axis):
    n = x.shape[axis]
    if axis == 0:
        return cat([x[n - 64 :], x[: n - 64]], 0)
    return cat([x[:, n - 64 :], x[:, : n - 64]], 1)


def unrolled(x, axis):
    if axis == 0:
        return cat([x[64:], x[:64]], 0)
    return cat([x[:, 64:], x[:, :64]], 1)


def eliminate_body(inverses, detune, hop):
    h0 = rolled(rolled(hop[0], 0), 1)
    h1 = rolled(rolled(hop[1], 0), 1)
    one = eye(256)
    ar = one * rolled(detune, 1) - (h0 + h0.T) * 0.5
    ai = one * ETA - (h1 - h1.T) * 0.5

    def part(rows, cols):
        return blk(ar[rows, cols], ai[rows, cols])

    b, i = slice(0, 128), slice(128, 256)
    (inner,) = inverses([part(i, i)], 1.0)
    abi = part(b, i)
    y = mm(abi, inner)
    z = mm(inner, part(i, b))
    s = part(b, b) - mm(abi, z)
    return s, inner[:128], y, z[:128]


def corners(s):
    r, i = pair(s)
    lo, hi = slice(0, 64), slice(64, 128)
    return [[blk(r[p, q], i[p, q]) for q in (lo, hi)] for p in (lo, hi)]


def lead_of(slab, c):
    return jnp.where(slab == 0, mm(c, c, NT), 0.0)


def maps_body(inverses, slab, s, couple, next_couple):
    (bb, bf), (fb, ff) = corners(s)
    c = blk(couple[0], couple[1])
    cn = blk(next_couple[0], next_couple[1])
    ff = ff + times_i(lead_of(slab, c))
    ib, if_ = inverses([bb, ff])
    b = -mm(ib, bf)
    d = -mm(fb, ib)
    phi = ff + mm(d, bf)
    br = -mm(if_, fb)
    dr = -mm(bf, if_)
    psi = bb + mm(dr, fb)
    ct = c.T
    cnt = cn.T
    left = [mm(mm(cn, ib), cnt), mm(cn, b), mm(d, cnt), phi]
    right = [mm(mm(ct, if_), c), mm(ct, br), mm(dr, c), psi]
    raw = [ib, b, d, phi]
    return [u[:64] for u in left], [u[:64] for u in right], [u[:64] for u in raw]


def compose(outer, inner, phi_inv):
    a2, b2, d2, _ = outer
    a1, b1, d1, phi1 = inner
    pq = mm(phi_inv, cat([b1, d2], 1))
    quad = mm(cat([b2, d1], 0), pq)
    n = a1.shape[0]
    return [a2 + quad[:n, n:], quad[:n, :n], quad[n:, n:], phi1 - quad[n:, :n]]


def level(inverses, slots):
    phis = inverses([outer[3] - inner[0] for outer, inner in slots])
    return [[u[:64] for u in compose(o, i, p)] for (o, i), p in zip(slots, phis)]


def constant_map(value):
    zero = jnp.zeros_like(value)
    return [value, zero, zero, imag_eye(64)]


def choose(cond, one, other):
    return [jnp.where(cond, x, y) for x, y in zip(one, other)]


def tree_body(inverses, slab, sent, put, get):
    none = constant_map(jnp.zeros((128, 128), F32))

    def wide(tops):
        return [full(u) for u in tops]

    lefts = (slab + 1) // 2

    def fetch(is_left, place):
        source = jnp.where(is_left, slab - 1 - place, slab + 1 + place)
        there = (source >= 0) & (source < 8)
        return choose(there, wide(sent(jnp.clip(source, 0, 7))), none)

    slots = []
    for k in range(4):
        is_left = k < lefts
        place = 2 * jnp.where(is_left, k, k - lefts)
        slots.append((fetch(is_left, place), fetch(is_left, place + 1)))
    for k, m in enumerate(level(inverses, slots)):
        put(k, m)

    skip = jnp.where(lefts == 1, 1, 0)
    last = choose(lax.rem(lefts, 2) == 0, wide(get(3)), none)
    slots = [(wide(get(skip)), wide(get(skip + 1))), (wide(get(skip + 2)), last)]
    for k, m in enumerate(level(inverses, slots)):
        put(4 + k, m)

    second = wide(get(5))
    left = choose(lefts == 0, none, wide(get(jnp.where(lefts == 1, 0, 4))))
    right = choose(lefts == 4, none, wide(get(jnp.where(lefts == 3, 3, jnp.where(lefts == 2, 5, 4)))))
    slots = [(left, choose(lefts >= 3, second, none)), (right, choose(lefts <= 1, second, none))]
    phis = inverses([outer[3] - inner[0] for outer, inner in slots])
    return [o[0] + mm(mm(o[1], p), o[2]) for (o, _), p in zip(slots, phis)]


def close_body(inverses, slab, couple, sig_l, sig_r, s, inner, y, z, raw):
    ib, b, d, phi = [full(u) for u in raw]
    lr, li = pair(sig_l - times_i(lead_of(slab, blk(couple[0], couple[1]))))
    rr, ri = pair(sig_r)
    zero = jnp.zeros((64, 64), F32)

    def spread(x, w):
        return cat([cat([x, zero], 1), cat([zero, w], 1)], 0)

    closed = s - blk(spread(rr, lr), spread(ri, li))
    e_inv, big = inverses([phi - sig_l, closed])
    be = mm(b, e_inv)
    gfb = mm(e_inv, d)
    gbb = ib + mm(be, d)

    def joined(k):
        return cat([cat([pair(gbb)[k], pair(be)[k]], 1), cat([pair(gfb)[k], pair(e_inv)[k]], 1)], 0)

    small = cat([joined(0), -joined(1)], 1)
    return big[:128], small


def restore(top, inner, y, z):
    ty = mm(top, y)
    zt = mm(z, full(top))
    zty = mm(zt, y)
    low = inner + zty
    r = cat([cat([top[:, :128], -ty[:, :128]], 1), cat([-zt[:, :128], low[:, :128]], 1)], 0)
    i = cat([cat([-top[:, 128:], ty[:, 128:]], 1), cat([zt[:, 128:], -low[:, 128:]], 1)], 0)
    return r, i


def for_rows(r, i):
    r, i = [unrolled(unrolled(x, 0), 1).reshape(32, 8, 256) for x in (r, i)]
    upper = lax.broadcasted_iota(jnp.int32, (32, 8, 256), 1) < 4

    def swapped(x):
        return cat([x[:, 4:], x[:, :4]], 1)

    even = jnp.where(upper, r, swapped(i))
    odd = jnp.where(upper, swapped(r), i)
    return even, odd


def right_adj(lr, li, gr, gi):
    n = lr.shape[0]
    rows = cat([cat([lr, li], 1), cat([li, -lr], 1)], 0)
    out = mm(rows, cat([gr, gi], 1), NT)
    return out[:n], out[n:]


def lesser_parts_body(slab, big, small, y, inject, couple, next_couple):
    rest = mm(cat([small, big], 0), y)
    gr, gi = cat([small[:, :128], -rest[:128, :128]], 1), cat([-small[:, 128:], rest[:128, 128:]], 1)
    fr, fi = cat([big[:, :128], -rest[128:, :128]], 1), cat([-big[:, 128:], rest[128:, 128:]], 1)
    hr, hi = 1.5 * gr - fr, 1.5 * gi - fi
    d = rolled(inject, 1)
    lr = cat([gr[:64], hr[64:]], 0) * d
    li = cat([gi[:64], hi[64:]], 0) * d
    mr, mi = right_adj(lr, li, gr, gi)
    c = blk(couple[0], couple[1])
    cn = blk(next_couple[0], next_couple[1])
    ct, cnt = c.T, cn.T
    w = mm(mm(cn, blk(-mi[:64, :64], mr[:64, :64])), cnt)
    beta = mm(cn, blk(gr[:64, 64:128], gi[:64, 64:128]))
    w = w + mm(mm(beta, times_i(lead_of(slab, c))), beta, NT)
    w = (w - w.T) * 0.5
    q = mm(mm(ct, blk(-mi[64:, 64:], mr[64:, 64:])), c)
    q = q - q.T
    left = mm(
        ct,
        cat(
            [
                blk(gr[64:128, 64:128], gi[64:128, 64:128]),
                blk(hr[64:128, 64:128], hi[64:128, 64:128]),
                blk(gr[64:128, :64], gi[64:128, :64]),
            ],
            1,
        ),
    )
    u, v, zz = left[:, :128], left[:, 128:256], left[:, 256:]
    return [m[:64] for m in (w + times_i(q), beta, u, v, zz)]


def lesser_body(slab, couple, parts, big, small, inner, y, z, inject):
    mine = times_i(lead_of(slab, blk(couple[0], couple[1])))
    sources = {}
    packed = [full(parts(t, 0)) for t in range(8)]
    for t in range(8):
        if t:
            beta = full(parts(t - 1, 1))
            both = packed[t - 1]
            w = (both - both.T) * 0.5
            sig = w + mm(mm(beta, sig), beta, NT) if t > 1 else w
            mine = jnp.where(slab == t, sig, mine)
            c = mm(mm(full(parts(t, 3)), sig), full(parts(t, 2)), NT)
            sources[t] = c - c.T - times_i((packed[t] + packed[t].T) * 0.5)
    back = jnp.zeros_like(sig)
    my_back = back
    for t in range(7, 0, -1):
        zz = full(parts(t, 4))
        back = sources[t] + mm(mm(zz, back), zz, NT)
        my_back = jnp.where(slab == t - 1, back, my_back)
    gr, gi = restore(small, inner, y, z)
    fr, fi = restore(big, inner, y, z)
    hr, hi = 1.5 * gr - fr, 1.5 * gi - fi
    d = rolled(inject, 1)
    right_r, right_i = pair(mine)
    back_r, back_i = pair(0.5 * my_back)

    def cols(xr, xi, m):
        out = mm(cat([xr, xi], 1), m)
        return out

    fm = cat([cat([right_r, right_i], 1), cat([-right_i, right_r], 1)], 0)
    bm = cat([cat([back_r, back_i], 1), cat([-back_i, back_r], 1)], 0)
    on_f = cols(hr[:, 64:128], hi[:, 64:128], fm)
    on_b = cols(gr[:, :64], gi[:, :64], bm)
    add_r = cat([on_b[:, :64], on_f[:, :64]], 1)
    add_i = cat([on_b[:, 64:], on_f[:, 64:]], 1)
    lr, li = -hi * d, hr * d
    lr = cat([lr[:, :128] + add_r, lr[:, 128:]], 1)
    li = cat([li[:, :128] + add_i, li[:, 128:]], 1)
    nr, ni = right_adj(lr, li, gr, gi)
    return nr - nr.T, ni + ni.T


VM = pl.BlockSpec(memory_space=pltpu.VMEM)
SM = pl.BlockSpec(memory_space=pltpu.SMEM)


def call(kernel, outs, specs, micros, scratch=()):
    return pl.pallas_call(
        kernel,
        out_shape=[jax.ShapeDtypeStruct(o, F32) for o in outs],
        in_specs=specs,
        out_specs=[VM] * len(outs),
        scratch_shapes=list(scratch),
        compiler_params=pltpu.CompilerParams(vmem_limit_bytes=40 * 2**20),
        cost_estimate=pl.CostEstimate(flops=int(micros * 1.1e9), bytes_accessed=1 << 20, transcendentals=0),
    )


def put(ref, values):
    for k, v in enumerate(values):
        ref[k] = v


def eliminate_kernel(detune, hop, s, inner, y, z):
    def run(inverses):
        s[...], inner[...], y[...], z[...] = eliminate_body(inverses, detune[...], (hop[0, 0], hop[1, 0]))

    guarded(run)


def maps_kernel(slab, s, couple, next_couple, sends, raw):
    chip, core = slab[0] // 2, lax.rem(slab[0], 2)

    def run(inverses):
        left, right, own = maps_body(inverses, slab[0], s[...], (couple[0, 0], couple[1, 0]), (next_couple[0, 0], next_couple[1, 0]))
        put(raw, own)
        for t in range(4):
            put(sends.at[t], choose((chip < t) | ((chip == t) & (core == 0)), left, right))

    guarded(run)


def put_rows(ref, r, i):
    even, odd = for_rows(r, i)
    ref[:, 0] = even
    ref[:, 1] = odd


def close_kernel(
    slab, couple, next_couple, inject, near, far, s, inner, y, z, raw, rows, big, small, parts, kept
):
    me = slab[0]
    own_couple = (couple[0, 0], couple[1, 0])

    def sent(t):
        same = lax.rem(t, 2) == lax.rem(me, 2)
        return [jnp.where(same, near[t // 2, k], far[t // 2, k]) for k in range(4)]

    def run(inverses):
        def get(t):
            return [kept[t, k] for k in range(4)]

        sig_l, sig_r = tree_body(inverses, me, sent, lambda k, m: put(kept.at[k], m), get)
        own = [raw[k] for k in range(4)]
        whole, corner = close_body(
            inverses, me, own_couple, sig_l, sig_r, s[...], inner[...], y[...], z[...], own
        )
        big[...], small[...] = whole, corner
        put(parts, lesser_parts_body(me, whole, corner, y[...], inject[:, 0], own_couple, (next_couple[0, 0], next_couple[1, 0])))
        put_rows(rows, *restore(whole, inner[...], y[...], z[...]))

    guarded(run)


def lesser_kernel(slab, couple, parts, big, small, inner, y, z, inject, rows):
    r, i = lesser_body(
        slab[0],
        (couple[0, 0], couple[1, 0]),
        lambda t, k: parts[t, k],
        big[...],
        small[...],
        inner[...],
        y[...],
        z[...],
        inject[:, 0],
    )
    put_rows(rows, r, i)


def convolve_kernel(table, piece, out):
    for j in range(4):
        x = cat([piece[:, j], piece[:, 4 + j]], 0)
        o = mm(table[...], x)
        out[0, 0, :, j] = o[:64]
        out[1, 0, :, j] = o[64:]


def tables_kernel(kern, out):
    for k in range(2):
        t = []
        for c in range(2):
            x = jnp.broadcast_to(kern[k, c : c + 1, :], (64, 128))
            t.append(pltpu.roll(x, 65, 1, stride=1, stride_axis=0)[:, :64])
        out[k] = blk(t[0], t[1])


def per_device(energies, onsite, hopping, coupling, injection, kernels):
    slab = lax.axis_index("slab").astype(jnp.int32).reshape(1)

    def swapped_over(x, axis):
        return lax.all_to_all(x, axis, split_axis=0, concat_axis=0, tiled=True)

    next_couple = lax.ppermute(coupling, "slab", [(t, (t + 7) % 8) for t in range(8)])
    m256, half = (256, 256), (128, 256)
    port = (4, 64, 128)
    s, inner, y, z = call(eliminate_kernel, [m256, half, m256, half], [VM, VM], 6)(energies[:, None] - onsite, hopping)
    sends, raw = call(maps_kernel, [(4, *port), port], [SM] + [VM] * 3, 5)(slab, s, coupling, next_couple)
    near = lax.all_to_all(
        sends, "slab", split_axis=0, concat_axis=0, tiled=True, axis_index_groups=[[0, 2, 4, 6], [1, 3, 5, 7]]
    )
    far = lax.ppermute(near, "slab", [(t, t ^ 1) for t in range(8)])
    rows, big, small, parts = call(
        close_kernel,
        [(32, 2, 8, 256), half, half, (5, 64, 128)],
        [SM] + [VM] * 10,
        25,
        [pltpu.VMEM((6, 4, 64, 128), F32)],
    )(slab, coupling, next_couple, injection, near, far, s, inner, y, z, raw)

    def to_rows(x):
        return swapped_over(x.reshape(64, 8, 256), "energy")

    got_r = to_rows(rows)
    all_parts = lax.all_gather(parts, "slab")
    late_kernels, _ = lax.optimization_barrier((kernels, parts))
    reversed_kernels = jnp.pad(late_kernels[:, :, ::-1], ((0, 0), (0, 0), (0, 1)))
    (tables,) = call(tables_kernel, [(2, 128, 128)], [VM], 1)(reversed_kernels)
    (rows_l,) = call(lesser_kernel, [(32, 2, 8, 256)], [SM] + [VM] * 8, 8)(
        slab, coupling, all_parts, big, small, inner, y, z, injection
    )
    got_l = to_rows(rows_l)
    conv = call(convolve_kernel, [(2, 1, 64, 4, 256)], [VM] * 2, 2)
    return conv(tables[0], got_r)[0], conv(tables[1], got_l)[0]


def solution(mesh):
    in_specs = (
        P("energy"),
        P("slab", None),
        P(None, "slab", None, None),
        P(None, "slab", None, None),
        P("energy", "slab", None),
        P(),
    )
    out_specs = (P(None, "slab", None, "energy", None), P(None, "slab", None, "energy", None))
    return jax.shard_map(per_device, mesh=mesh, in_specs=in_specs, out_specs=out_specs, check_vma=False)
```

```python
import functools

import jax
import jax.numpy as jnp
from jax import lax
from jax.experimental import pallas as pl
from jax.experimental.pallas import tpu as pltpu
from jax.sharding import PartitionSpec as P

ETA = 0.02
F32 = jnp.float32
BF16 = jnp.bfloat16
NN = (((1,), (0,)), ((), ()))
NT = (((1,), (1,)), ((), ()))


def mmh(a, b, dims=NN):
    return lax.dot_general(a, b, dims, precision=lax.Precision.HIGHEST, preferred_element_type=F32)


def halves(x):
    high = x.astype(BF16)
    return high, (x - high.astype(F32)).astype(BF16)


def mm1(a, b, dims=NN):
    return lax.dot_general(a, b, dims, preferred_element_type=F32)


def mm3(a, b, dims=NN):
    return mm1(a[0], b[0], dims) + (mm1(a[0], b[1], dims) + mm1(a[1], b[0], dims))


def mm(a, b, dims=NN):
    return mm3(halves(a), halves(b), dims)


def cat(parts, axis):
    return jnp.concatenate(parts, axis=axis)


def blk(r, i):
    return cat([cat([r, -i], 1), cat([i, r], 1)], 0)


def pair(z):
    n = z.shape[1] // 2
    return z[:n, :n], -z[:n, n:]


def full(top):
    n = top.shape[0]
    return cat([top, cat([-top[:, n:], top[:, :n]], 1)], 0)


def eye(n):
    return (lax.broadcasted_iota(jnp.int32, (n, n), 0) == lax.broadcasted_iota(jnp.int32, (n, n), 1)).astype(F32)


def imag_eye(n):
    return blk(jnp.zeros((n, n), F32), eye(n))


def times_i(z):
    n = z.shape[0] // 2
    return cat([-z[n:], z[:n]], 0)


def lowest(values):
    return functools.reduce(jnp.minimum, values)


def scaled(low, floor):
    base = jnp.maximum(low, floor)
    shift = 1.0 + base
    gain = 4.0 / (shift * shift)
    return shift, gain, jnp.minimum(gain * low * (shift - low), gain * base)


ENOUGH = 2e-4


def corrected(mats, xs):
    rs = [eye(z.shape[0]) - mmh(z, x) for z, x in zip(mats, xs)]
    size = functools.reduce(jnp.maximum, [jnp.sum(r * r) for r in rs])
    return size, tuple(x + mm1(x.astype(BF16), r.astype(BF16)) for x, r in zip(xs, rs))


def bound(z):
    zb = z.astype(BF16)
    w = mm1(zb, zb, NT)
    return 1.0 / (1.01 * jnp.max(jnp.sum(jnp.abs(w), axis=1, keepdims=True))), w, z.T


FLOOR = 0.035


def last_steps():
    low = FLOOR
    for _ in range(4):
        shift = 1.0 + low
        gain = 4.0 / (shift * shift)
        yield shift, gain
        low *= gain


def quick(sizes):
    def inverses(mats, factor=2.0):
        eyes = [eye(z.shape[0]) for z in mats]
        parts = [halves(z) for z in mats]
        shift = 1.0 + FLOOR
        gain = 4.0 / (shift * shift)
        lows, guesses = [], []
        for z, one in zip(mats, eyes):
            inv_u, w, zt = bound(z)
            r = shift * one - w * inv_u
            guesses.append(((gain * inv_u) * mm1(zt.astype(BF16), r.astype(BF16))).astype(BF16))
            lows.append((factor * ETA * ETA) * inv_u)
        low = lowest(lows)
        rise = gain * (shift - FLOOR)
        count = sum((low < FLOOR * rise**-k).astype(jnp.int32) for k in range(1, 20))

        def step(_, guesses):
            rs = [(shift * one - mm1(p[0], x)).astype(BF16) for p, one, x in zip(parts, eyes, guesses)]
            return tuple((gain * mm1(x, r)).astype(BF16) for x, r in zip(guesses, rs))

        guesses = lax.fori_loop(0, count, step, tuple(guesses))
        products = [mm1(zh, x) + mm1(zl, x) for (zh, zl), x in zip(parts, guesses)]
        for late, (late_shift, late_gain) in enumerate(last_steps()):
            rs = [(late_shift * one - y).astype(BF16) for one, y in zip(eyes, products)]
            if late < 3:
                both = [
                    late_gain * mm1(cat([x, y.astype(BF16)], 0), r) for x, y, r in zip(guesses, products, rs)
                ]
                guesses = [v[: v.shape[1]].astype(BF16) for v in both]
                products = [v[v.shape[1] :] for v in both]
            else:
                guesses = [(late_gain * mm1(x, r)).astype(BF16) for x, r in zip(guesses, rs)]
        better = []
        for (zh, zl), one, x in zip(parts, eyes, guesses):
            rh, rl = halves(one - (mm1(zh, x) + mm1(zl, x)))
            better.append(x.astype(F32) + (mm1(x, rh) + mm1(x, rl)))
        size, better = corrected(mats, better)
        sizes.append(size)
        return better

    return inverses


def careful(mats, factor=1.0):
    n = len(mats)
    eyes = [eye(z.shape[0]) for z in mats]
    parts = [halves(z) for z in mats]
    lows, xs = [], []
    for z in mats:
        inv_u, _, zt = bound(z)
        lows.append((ETA * ETA) * inv_u)
        xs.append(zt * inv_u)

    def step(state):
        lows, xs = state
        plans = [scaled(low, 1e-3) for low in lows]
        new = []
        for k in range(n):
            xp = halves(xs[k])
            r = plans[k][0] * eyes[k] - mm3(parts[k], xp)
            new.append(plans[k][1] * mm3(xp, halves(r)))
        return tuple(p[2] for p in plans), tuple(new)

    _, xs = lax.while_loop(lambda state: lowest(state[0]) < 0.999, step, (tuple(lows), tuple(xs)))

    def again(state):
        count, size, _ = state
        return (count < 8) & jnp.logical_not(size <= ENOUGH)

    def more(state):
        count, _, xs = state
        size, xs = corrected(mats, xs)
        return count + 1, size, xs

    size, xs = corrected(mats, xs)
    return lax.while_loop(again, more, (jnp.int32(0), size, xs))[2]


def guarded(run):
    sizes = []
    run(quick(sizes))

    @pl.when(jnp.logical_not(functools.reduce(jnp.maximum, sizes) <= ENOUGH))
    def _():
        run(careful)


def rolled(x, axis):
    n = x.shape[axis]
    if axis == 0:
        return cat([x[n - 64 :], x[: n - 64]], 0)
    return cat([x[:, n - 64 :], x[:, : n - 64]], 1)


def unrolled(x, axis):
    if axis == 0:
        return cat([x[64:], x[:64]], 0)
    return cat([x[:, 64:], x[:, :64]], 1)


def eliminate_body(inverses, detune, hop):
    h0 = rolled(rolled(hop[0], 0), 1)
    h1 = rolled(rolled(hop[1], 0), 1)
    one = eye(256)
    ar = one * rolled(detune, 1) - (h0 + h0.T) * 0.5
    ai = one * ETA - (h1 - h1.T) * 0.5

    def part(rows, cols):
        return blk(ar[rows, cols], ai[rows, cols])

    b, i = slice(0, 128), slice(128, 256)
    (inner,) = inverses([part(i, i)], 1.0)
    abi = part(b, i)
    y = mm(abi, inner)
    z = mm(inner, part(i, b))
    s = part(b, b) - mm(abi, z)
    return s, inner[:128], y, z[:128]


def corners(s):
    r, i = pair(s)
    lo, hi = slice(0, 64), slice(64, 128)
    return [[blk(r[p, q], i[p, q]) for q in (lo, hi)] for p in (lo, hi)]


def lead_of(slab, c):
    return jnp.where(slab == 0, mm(c, c, NT), 0.0)


def maps_body(inverses, slab, s, couple, next_couple):
    (bb, bf), (fb, ff) = corners(s)
    c = blk(couple[0], couple[1])
    cn = blk(next_couple[0], next_couple[1])
    ff = ff + times_i(lead_of(slab, c))
    ib, if_ = inverses([bb, ff])
    b = -mm(ib, bf)
    d = -mm(fb, ib)
    phi = ff + mm(d, bf)
    br = -mm(if_, fb)
    dr = -mm(bf, if_)
    psi = bb + mm(dr, fb)
    ct = c.T
    cnt = cn.T
    left = [mm(mm(cn, ib), cnt), mm(cn, b), mm(d, cnt), phi]
    right = [mm(mm(ct, if_), c), mm(ct, br), mm(dr, c), psi]
    raw = [ib, b, d, phi]
    return [u[:64] for u in left], [u[:64] for u in right], [u[:64] for u in raw]


def compose(outer, inner, phi_inv):
    a2, b2, d2, _ = outer
    a1, b1, d1, phi1 = inner
    pq = mm(phi_inv, cat([b1, d2], 1))
    quad = mm(cat([b2, d1], 0), pq)
    n = a1.shape[0]
    return [a2 + quad[:n, n:], quad[:n, :n], quad[n:, n:], phi1 - quad[n:, :n]]


def level(inverses, slots):
    phis = inverses([outer[3] - inner[0] for outer, inner in slots])
    return [[u[:64] for u in compose(o, i, p)] for (o, i), p in zip(slots, phis)]


def constant_map(value):
    zero = jnp.zeros_like(value)
    return [value, zero, zero, imag_eye(64)]


def choose(cond, one, other):
    return [jnp.where(cond, x, y) for x, y in zip(one, other)]


def tree_body(inverses, slab, sent, put, get):
    none = constant_map(jnp.zeros((128, 128), F32))

    def wide(tops):
        return [full(u) for u in tops]

    lefts = (slab + 1) // 2

    def fetch(is_left, place):
        source = jnp.where(is_left, slab - 1 - place, slab + 1 + place)
        there = (source >= 0) & (source < 8)
        return choose(there, wide(sent(jnp.clip(source, 0, 7))), none)

    slots = []
    for k in range(4):
        is_left = k < lefts
        place = 2 * jnp.where(is_left, k, k - lefts)
        slots.append((fetch(is_left, place), fetch(is_left, place + 1)))
    for k, m in enumerate(level(inverses, slots)):
        put(k, m)

    skip = jnp.where(lefts == 1, 1, 0)
    last = choose(lax.rem(lefts, 2) == 0, wide(get(3)), none)
    slots = [(wide(get(skip)), wide(get(skip + 1))), (wide(get(skip + 2)), last)]
    for k, m in enumerate(level(inverses, slots)):
        put(4 + k, m)

    second = wide(get(5))
    left = choose(lefts == 0, none, wide(get(jnp.where(lefts == 1, 0, 4))))
    right = choose(lefts == 4, none, wide(get(jnp.where(lefts == 3, 3, jnp.where(lefts == 2, 5, 4)))))
    slots = [(left, choose(lefts >= 3, second, none)), (right, choose(lefts <= 1, second, none))]
    phis = inverses([outer[3] - inner[0] for outer, inner in slots])
    return [o[0] + mm(mm(o[1], p), o[2]) for (o, _), p in zip(slots, phis)]


def close_body(inverses, slab, couple, sig_l, sig_r, s, inner, y, z, raw):
    ib, b, d, phi = [full(u) for u in raw]
    lr, li = pair(sig_l - times_i(lead_of(slab, blk(couple[0], couple[1]))))
    rr, ri = pair(sig_r)
    zero = jnp.zeros((64, 64), F32)

    def spread(x, w):
        return cat([cat([x, zero], 1), cat([zero, w], 1)], 0)

    closed = s - blk(spread(rr, lr), spread(ri, li))
    e_inv, big = inverses([phi - sig_l, closed])
    be = mm(b, e_inv)
    gfb = mm(e_inv, d)
    gbb = ib + mm(be, d)

    def joined(k):
        return cat([cat([pair(gbb)[k], pair(be)[k]], 1), cat([pair(gfb)[k], pair(e_inv)[k]], 1)], 0)

    small = cat([joined(0), -joined(1)], 1)
    return big[:128], small


def restore(top, inner, y, z):
    ty = mm(top, y)
    zt = mm(z, full(top))
    zty = mm(zt, y)
    low = inner + zty
    r = cat([cat([top[:, :128], -ty[:, :128]], 1), cat([-zt[:, :128], low[:, :128]], 1)], 0)
    i = cat([cat([-top[:, 128:], ty[:, 128:]], 1), cat([zt[:, 128:], -low[:, 128:]], 1)], 0)
    return r, i


def for_rows(r, i):
    r, i = [unrolled(unrolled(x, 0), 1).reshape(32, 8, 256) for x in (r, i)]
    upper = lax.broadcasted_iota(jnp.int32, (32, 8, 256), 1) < 4

    def swapped(x):
        return cat([x[:, 4:], x[:, :4]], 1)

    even = jnp.where(upper, r, swapped(i))
    odd = jnp.where(upper, swapped(r), i)
    return even, odd


def right_adj(lr, li, gr, gi):
    n = lr.shape[0]
    rows = cat([cat([lr, li], 1), cat([li, -lr], 1)], 0)
    out = mm(rows, cat([gr, gi], 1), NT)
    return out[:n], out[n:]


def lesser_parts_body(slab, big, small, y, inject, couple, next_couple):
    rest = mm(cat([small, big], 0), y)
    gr, gi = cat([small[:, :128], -rest[:128, :128]], 1), cat([-small[:, 128:], rest[:128, 128:]], 1)
    fr, fi = cat([big[:, :128], -rest[128:, :128]], 1), cat([-big[:, 128:], rest[128:, 128:]], 1)
    hr, hi = 1.5 * gr - fr, 1.5 * gi - fi
    d = rolled(inject, 1)
    lr = cat([gr[:64], hr[64:]], 0) * d
    li = cat([gi[:64], hi[64:]], 0) * d
    mr, mi = right_adj(lr, li, gr, gi)
    c = blk(couple[0], couple[1])
    cn = blk(next_couple[0], next_couple[1])
    ct, cnt = c.T, cn.T
    w = mm(mm(cn, blk(-mi[:64, :64], mr[:64, :64])), cnt)
    beta = mm(cn, blk(gr[:64, 64:128], gi[:64, 64:128]))
    w = w + mm(mm(beta, times_i(lead_of(slab, c))), beta, NT)
    w = (w - w.T) * 0.5
    q = mm(mm(ct, blk(-mi[64:, 64:], mr[64:, 64:])), c)
    q = q - q.T
    left = mm(
        ct,
        cat(
            [
                blk(gr[64:128, 64:128], gi[64:128, 64:128]),
                blk(hr[64:128, 64:128], hi[64:128, 64:128]),
                blk(gr[64:128, :64], gi[64:128, :64]),
            ],
            1,
        ),
    )
    u, v, zz = left[:, :128], left[:, 128:256], left[:, 256:]
    return [m[:64] for m in (w + times_i(q), beta, u, v, zz)]


def lesser_body(slab, couple, parts, big, small, inner, y, z, inject):
    mine = times_i(lead_of(slab, blk(couple[0], couple[1])))
    sources = {}
    packed = [full(parts(t, 0)) for t in range(8)]
    for t in range(8):
        if t:
            beta = full(parts(t - 1, 1))
            both = packed[t - 1]
            w = (both - both.T) * 0.5
            sig = w + mm(mm(beta, sig), beta, NT) if t > 1 else w
            mine = jnp.where(slab == t, sig, mine)
            c = mm(mm(full(parts(t, 3)), sig), full(parts(t, 2)), NT)
            sources[t] = c - c.T - times_i((packed[t] + packed[t].T) * 0.5)
    back = jnp.zeros_like(sig)
    my_back = back
    for t in range(7, 0, -1):
        zz = full(parts(t, 4))
        back = sources[t] + mm(mm(zz, back), zz, NT)
        my_back = jnp.where(slab == t - 1, back, my_back)
    gr, gi = restore(small, inner, y, z)
    fr, fi = restore(big, inner, y, z)
    hr, hi = 1.5 * gr - fr, 1.5 * gi - fi
    d = rolled(inject, 1)
    right_r, right_i = pair(mine)
    back_r, back_i = pair(0.5 * my_back)

    def cols(xr, xi, m):
        out = mm(cat([xr, xi], 1), m)
        return out

    fm = cat([cat([right_r, right_i], 1), cat([-right_i, right_r], 1)], 0)
    bm = cat([cat([back_r, back_i], 1), cat([-back_i, back_r], 1)], 0)
    on_f = cols(hr[:, 64:128], hi[:, 64:128], fm)
    on_b = cols(gr[:, :64], gi[:, :64], bm)
    add_r = cat([on_b[:, :64], on_f[:, :64]], 1)
    add_i = cat([on_b[:, 64:], on_f[:, 64:]], 1)
    lr, li = -hi * d, hr * d
    lr = cat([lr[:, :128] + add_r, lr[:, 128:]], 1)
    li = cat([li[:, :128] + add_i, li[:, 128:]], 1)
    nr, ni = right_adj(lr, li, gr, gi)
    return nr - nr.T, ni + ni.T


VM = pl.BlockSpec(memory_space=pltpu.VMEM)
SM = pl.BlockSpec(memory_space=pltpu.SMEM)


def call(kernel, outs, specs, micros, scratch=()):
    return pl.pallas_call(
        kernel,
        out_shape=[jax.ShapeDtypeStruct(o, F32) for o in outs],
        in_specs=specs,
        out_specs=[VM] * len(outs),
        scratch_shapes=list(scratch),
        compiler_params=pltpu.CompilerParams(vmem_limit_bytes=40 * 2**20),
        cost_estimate=pl.CostEstimate(flops=int(micros * 1.1e9), bytes_accessed=1 << 20, transcendentals=0),
    )


def put(ref, values):
    for k, v in enumerate(values):
        ref[k] = v


def eliminate_kernel(detune, hop, s, inner, y, z):
    def run(inverses):
        s[...], inner[...], y[...], z[...] = eliminate_body(inverses, detune[...], (hop[0, 0], hop[1, 0]))

    guarded(run)


def maps_kernel(slab, s, couple, next_couple, sends, raw):
    chip, core = slab[0] // 2, lax.rem(slab[0], 2)

    def run(inverses):
        left, right, own = maps_body(inverses, slab[0], s[...], (couple[0, 0], couple[1, 0]), (next_couple[0, 0], next_couple[1, 0]))
        put(raw, own)
        for t in range(4):
            put(sends.at[t], choose((chip < t) | ((chip == t) & (core == 0)), left, right))

    guarded(run)


def put_rows(ref, r, i):
    even, odd = for_rows(r, i)
    ref[:, 0] = even
    ref[:, 1] = odd


def close_kernel(
    slab, couple, next_couple, inject, near, far, s, inner, y, z, raw, rows, big, small, parts, kept
):
    me = slab[0]
    own_couple = (couple[0, 0], couple[1, 0])

    def sent(t):
        same = lax.rem(t, 2) == lax.rem(me, 2)
        return [jnp.where(same, near[t // 2, k], far[t // 2, k]) for k in range(4)]

    def run(inverses):
        def get(t):
            return [kept[t, k] for k in range(4)]

        sig_l, sig_r = tree_body(inverses, me, sent, lambda k, m: put(kept.at[k], m), get)
        own = [raw[k] for k in range(4)]
        whole, corner = close_body(
            inverses, me, own_couple, sig_l, sig_r, s[...], inner[...], y[...], z[...], own
        )
        big[...], small[...] = whole, corner
        put(parts, lesser_parts_body(me, whole, corner, y[...], inject[:, 0], own_couple, (next_couple[0, 0], next_couple[1, 0])))
        put_rows(rows, *restore(whole, inner[...], y[...], z[...]))

    guarded(run)


def lesser_kernel(slab, couple, parts, big, small, inner, y, z, inject, rows):
    r, i = lesser_body(
        slab[0],
        (couple[0, 0], couple[1, 0]),
        lambda t, k: parts[t, k],
        big[...],
        small[...],
        inner[...],
        y[...],
        z[...],
        inject[:, 0],
    )
    put_rows(rows, r, i)


def convolve_kernel(table, piece, out):
    for j in range(4):
        x = cat([piece[:, j], piece[:, 4 + j]], 0)
        o = mm(table[...], x)
        out[0, 0, :, j] = o[:64]
        out[1, 0, :, j] = o[64:]


def tables_kernel(kern, out):
    for k in range(2):
        t = []
        for c in range(2):
            x = jnp.broadcast_to(kern[k, c : c + 1, :], (64, 128))
            t.append(pltpu.roll(x, 65, 1, stride=1, stride_axis=0)[:, :64])
        out[k] = blk(t[0], t[1])


def per_device(energies, onsite, hopping, coupling, injection, kernels):
    slab = lax.axis_index("slab").astype(jnp.int32).reshape(1)

    def swapped_over(x, axis):
        return lax.all_to_all(x, axis, split_axis=0, concat_axis=0, tiled=True)

    next_couple = lax.ppermute(coupling, "slab", [(t, (t + 7) % 8) for t in range(8)])
    m256, half = (256, 256), (128, 256)
    port = (4, 64, 128)
    s, inner, y, z = call(eliminate_kernel, [m256, half, m256, half], [VM, VM], 6)(energies[:, None] - onsite, hopping)
    sends, raw = call(maps_kernel, [(4, *port), port], [SM] + [VM] * 3, 5)(slab, s, coupling, next_couple)
    near = lax.all_to_all(
        sends, "slab", split_axis=0, concat_axis=0, tiled=True, axis_index_groups=[[0, 2, 4, 6], [1, 3, 5, 7]]
    )
    far = lax.ppermute(near, "slab", [(t, t ^ 1) for t in range(8)])
    rows, big, small, parts = call(
        close_kernel,
        [(32, 2, 8, 256), half, half, (5, 64, 128)],
        [SM] + [VM] * 10,
        25,
        [pltpu.VMEM((6, 4, 64, 128), F32)],
    )(slab, coupling, next_couple, injection, near, far, s, inner, y, z, raw)

    def to_rows(x):
        return swapped_over(x.reshape(64, 8, 256), "energy")

    got_r = to_rows(rows)
    all_parts = lax.all_gather(parts, "slab")
    late_kernels, _ = lax.optimization_barrier((kernels, parts))
    reversed_kernels = jnp.pad(late_kernels[:, :, ::-1], ((0, 0), (0, 0), (0, 1)))
    (tables,) = call(tables_kernel, [(2, 128, 128)], [VM], 1)(reversed_kernels)
    (rows_l,) = call(lesser_kernel, [(32, 2, 8, 256)], [SM] + [VM] * 8, 8)(
        slab, coupling, all_parts, big, small, inner, y, z, injection
    )
    got_l = to_rows(rows_l)
    conv = call(convolve_kernel, [(2, 1, 64, 4, 256)], [VM] * 2, 2)
    return conv(tables[0], got_r)[0], conv(tables[1], got_l)[0]


def solution(mesh):
    in_specs = (
        P("energy"),
        P("slab", None),
        P(None, "slab", None, None),
        P(None, "slab", None, None),
        P("energy", "slab", None),
        P(),
    )
    out_specs = (P(None, "slab", None, "energy", None), P(None, "slab", None, "energy", None))
    return jax.shard_map(per_device, mesh=mesh, in_specs=in_specs, out_specs=out_specs, check_vma=False)
```

```python
import functools

import jax
import jax.numpy as jnp
from jax import lax
from jax.experimental import pallas as pl
from jax.experimental.pallas import tpu as pltpu
from jax.sharding import PartitionSpec as P

ETA = 0.02
F32 = jnp.float32
BF16 = jnp.bfloat16
NN = (((1,), (0,)), ((), ()))
NT = (((1,), (1,)), ((), ()))


def mmh(a, b, dims=NN):
    return lax.dot_general(a, b, dims, precision=lax.Precision.HIGHEST, preferred_element_type=F32)


def halves(x):
    high = x.astype(BF16)
    return high, (x - high.astype(F32)).astype(BF16)


def mm1(a, b, dims=NN):
    return lax.dot_general(a, b, dims, preferred_element_type=F32)


def mm3(a, b, dims=NN):
    return mm1(a[0], b[0], dims) + (mm1(a[0], b[1], dims) + mm1(a[1], b[0], dims))


def mm(a, b, dims=NN):
    return mm3(halves(a), halves(b), dims)


def cat(parts, axis):
    return jnp.concatenate(parts, axis=axis)


def blk(r, i):
    return cat([cat([r, -i], 1), cat([i, r], 1)], 0)


def pair(z):
    n = z.shape[1] // 2
    return z[:n, :n], -z[:n, n:]


def full(top):
    n = top.shape[0]
    return cat([top, cat([-top[:, n:], top[:, :n]], 1)], 0)


def eye(n):
    return (lax.broadcasted_iota(jnp.int32, (n, n), 0) == lax.broadcasted_iota(jnp.int32, (n, n), 1)).astype(F32)


def imag_eye(n):
    return blk(jnp.zeros((n, n), F32), eye(n))


def times_i(z):
    n = z.shape[0] // 2
    return cat([-z[n:], z[:n]], 0)


def lowest(values):
    return functools.reduce(jnp.minimum, values)


def scaled(low, floor):
    base = jnp.maximum(low, floor)
    shift = 1.0 + base
    gain = 4.0 / (shift * shift)
    return shift, gain, jnp.minimum(gain * low * (shift - low), gain * base)


ENOUGH = 2e-4


def corrected(mats, xs):
    rs = [eye(z.shape[0]) - mmh(z, x) for z, x in zip(mats, xs)]
    size = functools.reduce(jnp.maximum, [jnp.sum(r * r) for r in rs])
    return size, tuple(x + mm1(x.astype(BF16), r.astype(BF16)) for x, r in zip(xs, rs))


def bound(z):
    zb = z.astype(BF16)
    w = mm1(zb, zb, NT)
    return 1.0 / (1.01 * jnp.max(jnp.sum(jnp.abs(w), axis=1, keepdims=True))), w, z.T


FLOOR = 0.035


def last_steps():
    low = FLOOR
    for _ in range(4):
        shift = 1.0 + low
        gain = 4.0 / (shift * shift)
        yield shift, gain
        low *= gain


def quick(sizes):
    def inverses(mats, factor=2.0):
        eyes = [eye(z.shape[0]) for z in mats]
        parts = [halves(z) for z in mats]
        shift = 1.0 + FLOOR
        gain = 4.0 / (shift * shift)
        lows, guesses = [], []
        for z, one in zip(mats, eyes):
            inv_u, w, zt = bound(z)
            r = shift * one - w * inv_u
            guesses.append(((gain * inv_u) * mm1(zt.astype(BF16), r.astype(BF16))).astype(BF16))
            lows.append((factor * ETA * ETA) * inv_u)
        low = lowest(lows)
        rise = gain * (shift - FLOOR)
        count = sum((low < FLOOR * rise**-k).astype(jnp.int32) for k in range(1, 20))

        def step(_, guesses):
            rs = [(shift * one - mm1(p[0], x)).astype(BF16) for p, one, x in zip(parts, eyes, guesses)]
            return tuple((gain * mm1(x, r)).astype(BF16) for x, r in zip(guesses, rs))

        guesses = lax.fori_loop(0, count, step, tuple(guesses))
        products = [mm1(zh, x) + mm1(zl, x) for (zh, zl), x in zip(parts, guesses)]
        for late, (late_shift, late_gain) in enumerate(last_steps()):
            rs = [(late_shift * one - y).astype(BF16) for one, y in zip(eyes, products)]
            if late < 3:
                both = [
                    late_gain * mm1(cat([x, y.astype(BF16)], 0), r) for x, y, r in zip(guesses, products, rs)
                ]
                guesses = [v[: v.shape[1]].astype(BF16) for v in both]
                products = [v[v.shape[1] :] for v in both]
            else:
                guesses = [(late_gain * mm1(x, r)).astype(BF16) for x, r in zip(guesses, rs)]
        better = []
        for (zh, zl), one, x in zip(parts, eyes, guesses):
            rh, rl = halves(one - (mm1(zh, x) + mm1(zl, x)))
            better.append(x.astype(F32) + (mm1(x, rh) + mm1(x, rl)))
        size, better = corrected(mats, better)
        sizes.append(size)
        return better

    return inverses


def careful(mats, factor=1.0):
    n = len(mats)
    eyes = [eye(z.shape[0]) for z in mats]
    parts = [halves(z) for z in mats]
    lows, xs = [], []
    for z in mats:
        inv_u, _, zt = bound(z)
        lows.append((ETA * ETA) * inv_u)
        xs.append(zt * inv_u)

    def step(state):
        lows, xs = state
        plans = [scaled(low, 1e-3) for low in lows]
        new = []
        for k in range(n):
            xp = halves(xs[k])
            r = plans[k][0] * eyes[k] - mm3(parts[k], xp)
            new.append(plans[k][1] * mm3(xp, halves(r)))
        return tuple(p[2] for p in plans), tuple(new)

    _, xs = lax.while_loop(lambda state: lowest(state[0]) < 0.999, step, (tuple(lows), tuple(xs)))

    def again(state):
        count, size, _ = state
        return (count < 8) & jnp.logical_not(size <= ENOUGH)

    def more(state):
        count, _, xs = state
        size, xs = corrected(mats, xs)
        return count + 1, size, xs

    size, xs = corrected(mats, xs)
    return lax.while_loop(again, more, (jnp.int32(0), size, xs))[2]


def guarded(run):
    sizes = []
    run(quick(sizes))

    @pl.when(jnp.logical_not(functools.reduce(jnp.maximum, sizes) <= ENOUGH))
    def _():
        run(careful)


def rolled(x, axis):
    n = x.shape[axis]
    if axis == 0:
        return cat([x[n - 64 :], x[: n - 64]], 0)
    return cat([x[:, n - 64 :], x[:, : n - 64]], 1)


def unrolled(x, axis):
    if axis == 0:
        return cat([x[64:], x[:64]], 0)
    return cat([x[:, 64:], x[:, :64]], 1)


def eliminate_body(inverses, detune, hop):
    h0 = rolled(rolled(hop[0], 0), 1)
    h1 = rolled(rolled(hop[1], 0), 1)
    one = eye(256)
    ar = one * rolled(detune, 1) - (h0 + h0.T) * 0.5
    ai = one * ETA - (h1 - h1.T) * 0.5

    def part(rows, cols):
        return blk(ar[rows, cols], ai[rows, cols])

    b, i = slice(0, 128), slice(128, 256)
    (inner,) = inverses([part(i, i)], 1.0)
    abi = part(b, i)
    y = mm(abi, inner)
    z = mm(inner, part(i, b))
    s = part(b, b) - mm(abi, z)
    return s, inner[:128], y, z[:128]


def corners(s):
    r, i = pair(s)
    lo, hi = slice(0, 64), slice(64, 128)
    return [[blk(r[p, q], i[p, q]) for q in (lo, hi)] for p in (lo, hi)]


def lead_of(slab, c):
    return jnp.where(slab == 0, mm(c, c, NT), 0.0)


def maps_body(inverses, slab, s, couple, next_couple):
    (bb, bf), (fb, ff) = corners(s)
    c = blk(couple[0], couple[1])
    cn = blk(next_couple[0], next_couple[1])
    ff = ff + times_i(lead_of(slab, c))
    ib, if_ = inverses([bb, ff])
    b = -mm(ib, bf)
    d = -mm(fb, ib)
    phi = ff + mm(d, bf)
    br = -mm(if_, fb)
    dr = -mm(bf, if_)
    psi = bb + mm(dr, fb)
    ct = c.T
    cnt = cn.T
    left = [mm(mm(cn, ib), cnt), mm(cn, b), mm(d, cnt), phi]
    right = [mm(mm(ct, if_), c), mm(ct, br), mm(dr, c), psi]
    raw = [ib, b, d, phi]
    return [u[:64] for u in left], [u[:64] for u in right], [u[:64] for u in raw]


def compose(outer, inner, phi_inv):
    a2, b2, d2, _ = outer
    a1, b1, d1, phi1 = inner
    pq = mm(phi_inv, cat([b1, d2], 1))
    quad = mm(cat([b2, d1], 0), pq)
    n = a1.shape[0]
    return [a2 + quad[:n, n:], quad[:n, :n], quad[n:, n:], phi1 - quad[n:, :n]]


def level(inverses, slots):
    phis = inverses([outer[3] - inner[0] for outer, inner in slots])
    return [[u[:64] for u in compose(o, i, p)] for (o, i), p in zip(slots, phis)]


def constant_map(value):
    zero = jnp.zeros_like(value)
    return [value, zero, zero, imag_eye(64)]


def choose(cond, one, other):
    return [jnp.where(cond, x, y) for x, y in zip(one, other)]


def tree_body(inverses, slab, sent, put, get):
    none = constant_map(jnp.zeros((128, 128), F32))

    def wide(tops):
        return [full(u) for u in tops]

    lefts = (slab + 1) // 2

    def fetch(is_left, place):
        source = jnp.where(is_left, slab - 1 - place, slab + 1 + place)
        there = (source >= 0) & (source < 8)
        return choose(there, wide(sent(jnp.clip(source, 0, 7))), none)

    slots = []
    for k in range(4):
        is_left = k < lefts
        place = 2 * jnp.where(is_left, k, k - lefts)
        slots.append((fetch(is_left, place), fetch(is_left, place + 1)))
    for k, m in enumerate(level(inverses, slots)):
        put(k, m)

    skip = jnp.where(lefts == 1, 1, 0)
    last = choose(lax.rem(lefts, 2) == 0, wide(get(3)), none)
    slots = [(wide(get(skip)), wide(get(skip + 1))), (wide(get(skip + 2)), last)]
    for k, m in enumerate(level(inverses, slots)):
        put(4 + k, m)

    second = wide(get(5))
    left = choose(lefts == 0, none, wide(get(jnp.where(lefts == 1, 0, 4))))
    right = choose(lefts == 4, none, wide(get(jnp.where(lefts == 3, 3, jnp.where(lefts == 2, 5, 4)))))
    slots = [(left, choose(lefts >= 3, second, none)), (right, choose(lefts <= 1, second, none))]
    phis = inverses([outer[3] - inner[0] for outer, inner in slots])
    return [o[0] + mm(mm(o[1], p), o[2]) for (o, _), p in zip(slots, phis)]


def close_body(inverses, slab, couple, sig_l, sig_r, s, inner, y, z, raw):
    ib, b, d, phi = [full(u) for u in raw]
    lr, li = pair(sig_l - times_i(lead_of(slab, blk(couple[0], couple[1]))))
    rr, ri = pair(sig_r)
    zero = jnp.zeros((64, 64), F32)

    def spread(x, w):
        return cat([cat([x, zero], 1), cat([zero, w], 1)], 0)

    closed = s - blk(spread(rr, lr), spread(ri, li))
    e_inv, big = inverses([phi - sig_l, closed])
    be = mm(b, e_inv)
    gfb = mm(e_inv, d)
    gbb = ib + mm(be, d)

    def joined(k):
        return cat([cat([pair(gbb)[k], pair(be)[k]], 1), cat([pair(gfb)[k], pair(e_inv)[k]], 1)], 0)

    small = cat([joined(0), -joined(1)], 1)
    return big[:128], small


def restore(top, inner, y, z):
    ty = mm(top, y)
    zt = mm(z, full(top))
    zty = mm(zt, y)
    low = inner + zty
    r = cat([cat([top[:, :128], -ty[:, :128]], 1), cat([-zt[:, :128], low[:, :128]], 1)], 0)
    i = cat([cat([-top[:, 128:], ty[:, 128:]], 1), cat([zt[:, 128:], -low[:, 128:]], 1)], 0)
    return r, i


def for_rows(r, i):
    r, i = [unrolled(unrolled(x, 0), 1).reshape(32, 8, 256) for x in (r, i)]
    upper = lax.broadcasted_iota(jnp.int32, (32, 8, 256), 1) < 4

    def swapped(x):
        return cat([x[:, 4:], x[:, :4]], 1)

    even = jnp.where(upper, r, swapped(i))
    odd = jnp.where(upper, swapped(r), i)
    return even, odd


def right_adj(lr, li, gr, gi):
    n = lr.shape[0]
    rows = cat([cat([lr, li], 1), cat([li, -lr], 1)], 0)
    out = mm(rows, cat([gr, gi], 1), NT)
    return out[:n], out[n:]


def lesser_parts_body(slab, big, small, y, inject, couple, next_couple):
    rest = mm(cat([small, big], 0), y)
    gr, gi = cat([small[:, :128], -rest[:128, :128]], 1), cat([-small[:, 128:], rest[:128, 128:]], 1)
    fr, fi = cat([big[:, :128], -rest[128:, :128]], 1), cat([-big[:, 128:], rest[128:, 128:]], 1)
    hr, hi = 1.5 * gr - fr, 1.5 * gi - fi
    d = rolled(inject, 1)
    lr = cat([gr[:64], hr[64:]], 0) * d
    li = cat([gi[:64], hi[64:]], 0) * d
    mr, mi = right_adj(lr, li, gr, gi)
    c = blk(couple[0], couple[1])
    cn = blk(next_couple[0], next_couple[1])
    ct, cnt = c.T, cn.T
    w = mm(mm(cn, blk(-mi[:64, :64], mr[:64, :64])), cnt)
    beta = mm(cn, blk(gr[:64, 64:128], gi[:64, 64:128]))
    w = w + mm(mm(beta, times_i(lead_of(slab, c))), beta, NT)
    w = (w - w.T) * 0.5
    q = mm(mm(ct, blk(-mi[64:, 64:], mr[64:, 64:])), c)
    q = q - q.T
    left = mm(
        ct,
        cat(
            [
                blk(gr[64:128, 64:128], gi[64:128, 64:128]),
                blk(hr[64:128, 64:128], hi[64:128, 64:128]),
                blk(gr[64:128, :64], gi[64:128, :64]),
            ],
            1,
        ),
    )
    u, v, zz = left[:, :128], left[:, 128:256], left[:, 256:]
    return [m[:64] for m in (w + times_i(q), beta, u, v, zz)]


def lesser_body(slab, couple, parts, big, small, inner, y, z, inject):
    mine = times_i(lead_of(slab, blk(couple[0], couple[1])))
    sources = {}
    packed = [full(parts(t, 0)) for t in range(8)]
    for t in range(8):
        if t:
            beta = full(parts(t - 1, 1))
            both = packed[t - 1]
            w = (both - both.T) * 0.5
            sig = w + mm(mm(beta, sig), beta, NT) if t > 1 else w
            mine = jnp.where(slab == t, sig, mine)
            c = mm(mm(full(parts(t, 3)), sig), full(parts(t, 2)), NT)
            sources[t] = c - c.T - times_i((packed[t] + packed[t].T) * 0.5)
    back = jnp.zeros_like(sig)
    my_back = back
    for t in range(7, 0, -1):
        zz = full(parts(t, 4))
        back = sources[t] + mm(mm(zz, back), zz, NT)
        my_back = jnp.where(slab == t - 1, back, my_back)
    gr, gi = restore(small, inner, y, z)
    fr, fi = restore(big, inner, y, z)
    hr, hi = 1.5 * gr - fr, 1.5 * gi - fi
    d = rolled(inject, 1)
    right_r, right_i = pair(mine)
    back_r, back_i = pair(0.5 * my_back)

    def cols(xr, xi, m):
        out = mm(cat([xr, xi], 1), m)
        return out

    fm = cat([cat([right_r, right_i], 1), cat([-right_i, right_r], 1)], 0)
    bm = cat([cat([back_r, back_i], 1), cat([-back_i, back_r], 1)], 0)
    on_f = cols(hr[:, 64:128], hi[:, 64:128], fm)
    on_b = cols(gr[:, :64], gi[:, :64], bm)
    add_r = cat([on_b[:, :64], on_f[:, :64]], 1)
    add_i = cat([on_b[:, 64:], on_f[:, 64:]], 1)
    lr, li = -hi * d, hr * d
    lr = cat([lr[:, :128] + add_r, lr[:, 128:]], 1)
    li = cat([li[:, :128] + add_i, li[:, 128:]], 1)
    nr, ni = right_adj(lr, li, gr, gi)
    return nr - nr.T, ni + ni.T


VM = pl.BlockSpec(memory_space=pltpu.VMEM)
SM = pl.BlockSpec(memory_space=pltpu.SMEM)


def call(kernel, outs, specs, micros, scratch=()):
    return pl.pallas_call(
        kernel,
        out_shape=[jax.ShapeDtypeStruct(o, F32) for o in outs],
        in_specs=specs,
        out_specs=[VM] * len(outs),
        scratch_shapes=list(scratch),
        compiler_params=pltpu.CompilerParams(vmem_limit_bytes=40 * 2**20),
        cost_estimate=pl.CostEstimate(flops=int(micros * 1.1e9), bytes_accessed=1 << 20, transcendentals=0),
    )


def put(ref, values):
    for k, v in enumerate(values):
        ref[k] = v


def eliminate_kernel(detune, hop, s, inner, y, z):
    def run(inverses):
        s[...], inner[...], y[...], z[...] = eliminate_body(inverses, detune[...], (hop[0, 0], hop[1, 0]))

    guarded(run)


def maps_kernel(slab, s, couple, next_couple, sends, raw):
    chip, core = slab[0] // 2, lax.rem(slab[0], 2)

    def run(inverses):
        left, right, own = maps_body(inverses, slab[0], s[...], (couple[0, 0], couple[1, 0]), (next_couple[0, 0], next_couple[1, 0]))
        put(raw, own)
        for t in range(4):
            put(sends.at[t], choose((chip < t) | ((chip == t) & (core == 0)), left, right))

    guarded(run)


def put_rows(ref, r, i):
    even, odd = for_rows(r, i)
    ref[:, 0] = even
    ref[:, 1] = odd


def close_kernel(
    slab, couple, next_couple, inject, near, far, s, inner, y, z, raw, rows, big, small, parts, kept
):
    me = slab[0]
    own_couple = (couple[0, 0], couple[1, 0])

    def sent(t):
        same = lax.rem(t, 2) == lax.rem(me, 2)
        return [jnp.where(same, near[t // 2, k], far[t // 2, k]) for k in range(4)]

    def run(inverses):
        def get(t):
            return [kept[t, k] for k in range(4)]

        sig_l, sig_r = tree_body(inverses, me, sent, lambda k, m: put(kept.at[k], m), get)
        own = [raw[k] for k in range(4)]
        whole, corner = close_body(
            inverses, me, own_couple, sig_l, sig_r, s[...], inner[...], y[...], z[...], own
        )
        big[...], small[...] = whole, corner
        put(parts, lesser_parts_body(me, whole, corner, y[...], inject[:, 0], own_couple, (next_couple[0, 0], next_couple[1, 0])))
        put_rows(rows, *restore(whole, inner[...], y[...], z[...]))

    guarded(run)


def lesser_kernel(slab, couple, near, far, big, small, inner, y, z, inject, rows):
    me = slab[0]

    def parts(t, k):
        d = lax.rem(t // 2 - me // 2 + 4, 4)
        return jnp.where(lax.rem(me, 2) == t % 2, near[d, k], far[d, k])

    r, i = lesser_body(
        me,
        (couple[0, 0], couple[1, 0]),
        parts,
        big[...],
        small[...],
        inner[...],
        y[...],
        z[...],
        inject[:, 0],
    )
    put_rows(rows, r, i)


def convolve_kernel(table, piece, out):
    for j in range(4):
        x = cat([piece[:, j], piece[:, 4 + j]], 0)
        o = mm(table[...], x)
        out[0, 0, :, j] = o[:64]
        out[1, 0, :, j] = o[64:]


def tables_kernel(kern, out):
    for k in range(2):
        t = []
        for c in range(2):
            x = jnp.broadcast_to(kern[k, c : c + 1, :], (64, 128))
            t.append(pltpu.roll(x, 65, 1, stride=1, stride_axis=0)[:, :64])
        out[k] = blk(t[0], t[1])


def per_device(energies, onsite, hopping, coupling, injection, kernels):
    slab = lax.axis_index("slab").astype(jnp.int32).reshape(1)

    def swapped_over(x, axis):
        return lax.all_to_all(x, axis, split_axis=0, concat_axis=0, tiled=True)

    next_couple = lax.ppermute(coupling, "slab", [(t, (t + 7) % 8) for t in range(8)])
    m256, half = (256, 256), (128, 256)
    port = (4, 64, 128)
    s, inner, y, z = call(eliminate_kernel, [m256, half, m256, half], [VM, VM], 6)(energies[:, None] - onsite, hopping)
    sends, raw = call(maps_kernel, [(4, *port), port], [SM] + [VM] * 3, 5)(slab, s, coupling, next_couple)
    near = lax.all_to_all(
        sends, "slab", split_axis=0, concat_axis=0, tiled=True, axis_index_groups=[[0, 2, 4, 6], [1, 3, 5, 7]]
    )
    far = lax.ppermute(near, "slab", [(t, t ^ 1) for t in range(8)])
    rows, big, small, parts = call(
        close_kernel,
        [(32, 2, 8, 256), half, half, (5, 64, 128)],
        [SM] + [VM] * 10,
        25,
        [pltpu.VMEM((6, 4, 64, 128), F32)],
    )(slab, coupling, next_couple, injection, near, far, s, inner, y, z, raw)

    def to_rows(x):
        return swapped_over(x.reshape(64, 8, 256), "energy")

    got_r = to_rows(rows)
    near_parts = jnp.stack(
        [parts] + [lax.ppermute(parts, "slab", [(t, (t - 2 * d) % 8) for t in range(8)]) for d in (1, 2, 3)]
    )
    far_parts = lax.ppermute(near_parts, "slab", [(t, t ^ 1) for t in range(8)])
    late_kernels, _ = lax.optimization_barrier((kernels, parts))
    reversed_kernels = jnp.pad(late_kernels[:, :, ::-1], ((0, 0), (0, 0), (0, 1)))
    (tables,) = call(tables_kernel, [(2, 128, 128)], [VM], 1)(reversed_kernels)
    (rows_l,) = call(lesser_kernel, [(32, 2, 8, 256)], [SM] + [VM] * 9, 8)(
        slab, coupling, near_parts, far_parts, big, small, inner, y, z, injection
    )
    got_l = to_rows(rows_l)
    conv = call(convolve_kernel, [(2, 1, 64, 4, 256)], [VM] * 2, 2)
    return conv(tables[0], got_r)[0], conv(tables[1], got_l)[0]


def solution(mesh):
    in_specs = (
        P("energy"),
        P("slab", None),
        P(None, "slab", None, None),
        P(None, "slab", None, None),
        P("energy", "slab", None),
        P(),
    )
    out_specs = (P(None, "slab", None, "energy", None), P(None, "slab", None, "energy", None))
    return jax.shard_map(per_device, mesh=mesh, in_specs=in_specs, out_specs=out_specs, check_vma=False)
```

```python
import functools

import jax
import jax.numpy as jnp
from jax import lax
from jax.experimental import pallas as pl
from jax.experimental.pallas import tpu as pltpu
from jax.sharding import PartitionSpec as P

ETA = 0.02
F32 = jnp.float32
BF16 = jnp.bfloat16
NN = (((1,), (0,)), ((), ()))
NT = (((1,), (1,)), ((), ()))


def mmh(a, b, dims=NN):
    return lax.dot_general(a, b, dims, precision=lax.Precision.HIGHEST, preferred_element_type=F32)


def halves(x):
    high = x.astype(BF16)
    return high, (x - high.astype(F32)).astype(BF16)


def mm1(a, b, dims=NN):
    return lax.dot_general(a, b, dims, preferred_element_type=F32)


def mm3(a, b, dims=NN):
    return mm1(a[0], b[0], dims) + (mm1(a[0], b[1], dims) + mm1(a[1], b[0], dims))


def mm(a, b, dims=NN):
    return mm3(halves(a), halves(b), dims)


def cat(parts, axis):
    return jnp.concatenate(parts, axis=axis)


def blk(r, i):
    return cat([cat([r, -i], 1), cat([i, r], 1)], 0)


def pair(z):
    n = z.shape[1] // 2
    return z[:n, :n], -z[:n, n:]


def full(top):
    n = top.shape[0]
    return cat([top, cat([-top[:, n:], top[:, :n]], 1)], 0)


def eye(n):
    return (lax.broadcasted_iota(jnp.int32, (n, n), 0) == lax.broadcasted_iota(jnp.int32, (n, n), 1)).astype(F32)


def imag_eye(n):
    return blk(jnp.zeros((n, n), F32), eye(n))


def times_i(z):
    n = z.shape[0] // 2
    return cat([-z[n:], z[:n]], 0)


def lowest(values):
    return functools.reduce(jnp.minimum, values)


def scaled(low, floor):
    base = jnp.maximum(low, floor)
    shift = 1.0 + base
    gain = 4.0 / (shift * shift)
    return shift, gain, jnp.minimum(gain * low * (shift - low), gain * base)


ENOUGH = 2e-4


def corrected(mats, xs):
    rs = [eye(z.shape[0]) - mmh(z, x) for z, x in zip(mats, xs)]
    size = functools.reduce(jnp.maximum, [jnp.sum(r * r) for r in rs])
    return size, tuple(x + mm1(x.astype(BF16), r.astype(BF16)) for x, r in zip(xs, rs))


def bound(z):
    zb = z.astype(BF16)
    w = mm1(zb, zb, NT)
    return 1.0 / (1.01 * jnp.max(jnp.sum(jnp.abs(w), axis=1, keepdims=True))), w, z.T


FLOOR = 0.035


def last_steps():
    low = FLOOR
    for _ in range(4):
        shift = 1.0 + low
        gain = 4.0 / (shift * shift)
        yield shift, gain
        low *= gain


def quick(sizes):
    def inverses(mats, factor=2.0):
        eyes = [eye(z.shape[0]) for z in mats]
        parts = [halves(z) for z in mats]
        shift = 1.0 + FLOOR
        gain = 4.0 / (shift * shift)
        lows, guesses = [], []
        for z, one in zip(mats, eyes):
            inv_u, w, zt = bound(z)
            r = shift * one - w * inv_u
            guesses.append(((gain * inv_u) * mm1(zt.astype(BF16), r.astype(BF16))).astype(BF16))
            lows.append((factor * ETA * ETA) * inv_u)
        low = lowest(lows)
        rise = gain * (shift - FLOOR)
        count = sum((low < FLOOR * rise**-k).astype(jnp.int32) for k in range(1, 20))

        def step(_, guesses):
            rs = [(shift * one - mm1(p[0], x)).astype(BF16) for p, one, x in zip(parts, eyes, guesses)]
            return tuple((gain * mm1(x, r)).astype(BF16) for x, r in zip(guesses, rs))

        guesses = lax.fori_loop(0, count, step, tuple(guesses))
        products = [mm1(zh, x) + mm1(zl, x) for (zh, zl), x in zip(parts, guesses)]
        for late, (late_shift, late_gain) in enumerate(last_steps()):
            rs = [(late_shift * one - y).astype(BF16) for one, y in zip(eyes, products)]
            if late < 3:
                both = [
                    late_gain * mm1(cat([x, y.astype(BF16)], 0), r) for x, y, r in zip(guesses, products, rs)
                ]
                guesses = [v[: v.shape[1]].astype(BF16) for v in both]
                products = [v[v.shape[1] :] for v in both]
            else:
                guesses = [(late_gain * mm1(x, r)).astype(BF16) for x, r in zip(guesses, rs)]
        better = []
        for (zh, zl), one, x in zip(parts, eyes, guesses):
            r = one - (mm1(zh, x) + mm1(zl, x))
            rh, rl = halves(r)
            change = mm1(x, rh) + mm1(x, rl)
            r = r - mm3((zh, zl), halves(change))
            sizes.append(jnp.sum(r * r))
            x = x.astype(F32) + change
            better.append(x + mm1(x.astype(BF16), r.astype(BF16)))
        return better

    return inverses


def careful(mats, factor=1.0):
    n = len(mats)
    eyes = [eye(z.shape[0]) for z in mats]
    parts = [halves(z) for z in mats]
    lows, xs = [], []
    for z in mats:
        inv_u, _, zt = bound(z)
        lows.append((ETA * ETA) * inv_u)
        xs.append(zt * inv_u)

    def step(state):
        lows, xs = state
        plans = [scaled(low, 1e-3) for low in lows]
        new = []
        for k in range(n):
            xp = halves(xs[k])
            r = plans[k][0] * eyes[k] - mm3(parts[k], xp)
            new.append(plans[k][1] * mm3(xp, halves(r)))
        return tuple(p[2] for p in plans), tuple(new)

    _, xs = lax.while_loop(lambda state: lowest(state[0]) < 0.999, step, (tuple(lows), tuple(xs)))

    def again(state):
        count, size, _ = state
        return (count < 8) & jnp.logical_not(size <= ENOUGH)

    def more(state):
        count, _, xs = state
        size, xs = corrected(mats, xs)
        return count + 1, size, xs

    size, xs = corrected(mats, xs)
    return lax.while_loop(again, more, (jnp.int32(0), size, xs))[2]


def guarded(run):
    sizes = []
    run(quick(sizes))

    @pl.when(jnp.logical_not(functools.reduce(jnp.maximum, sizes) <= ENOUGH))
    def _():
        run(careful)


def rolled(x, axis):
    n = x.shape[axis]
    if axis == 0:
        return cat([x[n - 64 :], x[: n - 64]], 0)
    return cat([x[:, n - 64 :], x[:, : n - 64]], 1)


def unrolled(x, axis):
    if axis == 0:
        return cat([x[64:], x[:64]], 0)
    return cat([x[:, 64:], x[:, :64]], 1)


def eliminate_body(inverses, detune, hop):
    h0 = rolled(rolled(hop[0], 0), 1)
    h1 = rolled(rolled(hop[1], 0), 1)
    one = eye(256)
    ar = one * rolled(detune, 1) - (h0 + h0.T) * 0.5
    ai = one * ETA - (h1 - h1.T) * 0.5

    def part(rows, cols):
        return blk(ar[rows, cols], ai[rows, cols])

    b, i = slice(0, 128), slice(128, 256)
    (inner,) = inverses([part(i, i)], 1.0)
    abi = part(b, i)
    y = mm(abi, inner)
    z = mm(inner, part(i, b))
    s = part(b, b) - mm(abi, z)
    return s, inner[:128], y, z[:128]


def corners(s):
    r, i = pair(s)
    lo, hi = slice(0, 64), slice(64, 128)
    return [[blk(r[p, q], i[p, q]) for q in (lo, hi)] for p in (lo, hi)]


def lead_of(slab, c):
    return jnp.where(slab == 0, mm(c, c, NT), 0.0)


def maps_body(inverses, slab, s, couple, next_couple):
    (bb, bf), (fb, ff) = corners(s)
    c = blk(couple[0], couple[1])
    cn = blk(next_couple[0], next_couple[1])
    ff = ff + times_i(lead_of(slab, c))
    ib, if_ = inverses([bb, ff])
    b = -mm(ib, bf)
    d = -mm(fb, ib)
    phi = ff + mm(d, bf)
    br = -mm(if_, fb)
    dr = -mm(bf, if_)
    psi = bb + mm(dr, fb)
    ct = c.T
    cnt = cn.T
    left = [mm(mm(cn, ib), cnt), mm(cn, b), mm(d, cnt), phi]
    right = [mm(mm(ct, if_), c), mm(ct, br), mm(dr, c), psi]
    raw = [ib, b, d, phi]
    return [u[:64] for u in left], [u[:64] for u in right], [u[:64] for u in raw]


def compose(outer, inner, phi_inv):
    a2, b2, d2, _ = outer
    a1, b1, d1, phi1 = inner
    pq = mm(phi_inv, cat([b1, d2], 1))
    quad = mm(cat([b2, d1], 0), pq)
    n = a1.shape[0]
    return [a2 + quad[:n, n:], quad[:n, :n], quad[n:, n:], phi1 - quad[n:, :n]]


def level(inverses, slots):
    phis = inverses([outer[3] - inner[0] for outer, inner in slots])
    return [[u[:64] for u in compose(o, i, p)] for (o, i), p in zip(slots, phis)]


def constant_map(value):
    zero = jnp.zeros_like(value)
    return [value, zero, zero, imag_eye(64)]


def choose(cond, one, other):
    return [jnp.where(cond, x, y) for x, y in zip(one, other)]


def tree_body(inverses, slab, sent, put, get):
    none = [u[:64] for u in constant_map(jnp.zeros((128, 128), F32))]

    def wide(tops):
        return [full(u) for u in tops]

    lefts = (slab + 1) // 2

    def fetch(is_left, place):
        source = jnp.where(is_left, slab - 1 - place, slab + 1 + place)
        there = (source >= 0) & (source < 8)
        return wide(choose(there, sent(jnp.clip(source, 0, 7)), none))

    slots = []
    for k in range(4):
        is_left = k < lefts
        place = 2 * jnp.where(is_left, k, k - lefts)
        slots.append((fetch(is_left, place), fetch(is_left, place + 1)))
    for k, m in enumerate(level(inverses, slots)):
        put(k, m)

    skip = jnp.where(lefts == 1, 1, 0)
    last = wide(choose(lax.rem(lefts, 2) == 0, get(3), none))
    slots = [(wide(get(skip)), wide(get(skip + 1))), (wide(get(skip + 2)), last)]
    for k, m in enumerate(level(inverses, slots)):
        put(4 + k, m)

    second = get(5)
    left = choose(lefts == 0, none, get(jnp.where(lefts == 1, 0, 4)))
    right = choose(lefts == 4, none, get(jnp.where(lefts == 3, 3, jnp.where(lefts == 2, 5, 4))))
    slots = [(left, choose(lefts >= 3, second, none)), (right, choose(lefts <= 1, second, none))]
    slots = [(wide(outer), wide(inner)) for outer, inner in slots]
    phis = inverses([outer[3] - inner[0] for outer, inner in slots])
    return [o[0] + mm(mm(o[1], p), o[2]) for (o, _), p in zip(slots, phis)]


def close_body(inverses, slab, couple, sig_l, sig_r, s, inner, y, z, raw):
    ib, b, d, phi = [full(u) for u in raw]
    lr, li = pair(sig_l - times_i(lead_of(slab, blk(couple[0], couple[1]))))
    rr, ri = pair(sig_r)
    zero = jnp.zeros((64, 64), F32)

    def spread(x, w):
        return cat([cat([x, zero], 1), cat([zero, w], 1)], 0)

    closed = s - blk(spread(rr, lr), spread(ri, li))
    e_inv, big = inverses([phi - sig_l, closed])
    be = mm(b, e_inv)
    gfb = mm(e_inv, d)
    gbb = ib + mm(be, d)

    def joined(k):
        return cat([cat([pair(gbb)[k], pair(be)[k]], 1), cat([pair(gfb)[k], pair(e_inv)[k]], 1)], 0)

    small = cat([joined(0), -joined(1)], 1)
    return big[:128], small


def restore(top, inner, y, z):
    ty = mm(top, y)
    zt = mm(z, full(top))
    zty = mm(zt, y)
    low = inner + zty
    r = cat([cat([top[:, :128], -ty[:, :128]], 1), cat([-zt[:, :128], low[:, :128]], 1)], 0)
    i = cat([cat([-top[:, 128:], ty[:, 128:]], 1), cat([zt[:, 128:], -low[:, 128:]], 1)], 0)
    return r, i


def for_rows(r, i):
    r, i = [unrolled(unrolled(x, 0), 1).reshape(32, 8, 256) for x in (r, i)]
    upper = lax.broadcasted_iota(jnp.int32, (32, 8, 256), 1) < 4

    def swapped(x):
        return cat([x[:, 4:], x[:, :4]], 1)

    even = jnp.where(upper, r, swapped(i))
    odd = jnp.where(upper, swapped(r), i)
    return even, odd


def right_adj(lr, li, gr, gi):
    n = lr.shape[0]
    rows = cat([cat([lr, li], 1), cat([li, -lr], 1)], 0)
    out = mm(rows, cat([gr, gi], 1), NT)
    return out[:n], out[n:]


def lesser_parts_body(slab, big, small, y, inject, couple, next_couple):
    rest = mm(cat([small, big], 0), y)
    gr, gi = cat([small[:, :128], -rest[:128, :128]], 1), cat([-small[:, 128:], rest[:128, 128:]], 1)
    fr, fi = cat([big[:, :128], -rest[128:, :128]], 1), cat([-big[:, 128:], rest[128:, 128:]], 1)
    hr, hi = 1.5 * gr - fr, 1.5 * gi - fi
    d = rolled(inject, 1)
    lr = cat([gr[:64], hr[64:]], 0) * d
    li = cat([gi[:64], hi[64:]], 0) * d
    mr, mi = right_adj(lr, li, gr, gi)
    c = blk(couple[0], couple[1])
    cn = blk(next_couple[0], next_couple[1])
    ct, cnt = c.T, cn.T
    w = mm(mm(cn, blk(-mi[:64, :64], mr[:64, :64])), cnt)
    beta = mm(cn, blk(gr[:64, 64:128], gi[:64, 64:128]))
    w = w + mm(mm(beta, times_i(lead_of(slab, c))), beta, NT)
    w = (w - w.T) * 0.5
    q = mm(mm(ct, blk(-mi[64:, 64:], mr[64:, 64:])), c)
    q = q - q.T
    left = mm(
        ct,
        cat(
            [
                blk(gr[64:128, 64:128], gi[64:128, 64:128]),
                blk(hr[64:128, 64:128], hi[64:128, 64:128]),
                blk(gr[64:128, :64], gi[64:128, :64]),
            ],
            1,
        ),
    )
    u, v, zz = left[:, :128], left[:, 128:256], left[:, 256:]
    return [m[:64] for m in (w + times_i(q), beta, u, v, zz)]


def lesser_body(slab, couple, parts, big, small, inner, y, z, inject):
    mine = times_i(lead_of(slab, blk(couple[0], couple[1])))
    sources = {}
    packed = [full(parts(t, 0)) for t in range(8)]
    for t in range(8):
        if t:
            beta = full(parts(t - 1, 1))
            both = packed[t - 1]
            w = (both - both.T) * 0.5
            sig = w + mm(mm(beta, sig), beta, NT) if t > 1 else w
            mine = jnp.where(slab == t, sig, mine)
            c = mm(mm(full(parts(t, 3)), sig), full(parts(t, 2)), NT)
            sources[t] = c - c.T - times_i((packed[t] + packed[t].T) * 0.5)
    back = jnp.zeros_like(sig)
    my_back = back
    for t in range(7, 0, -1):
        zz = full(parts(t, 4))
        back = sources[t] + mm(mm(zz, back), zz, NT)
        my_back = jnp.where(slab == t - 1, back, my_back)
    gr, gi = restore(small, inner, y, z)
    fr, fi = restore(big, inner, y, z)
    hr, hi = 1.5 * gr - fr, 1.5 * gi - fi
    d = rolled(inject, 1)
    right_r, right_i = pair(mine)
    back_r, back_i = pair(0.5 * my_back)

    def cols(xr, xi, m):
        out = mm(cat([xr, xi], 1), m)
        return out

    fm = cat([cat([right_r, right_i], 1), cat([-right_i, right_r], 1)], 0)
    bm = cat([cat([back_r, back_i], 1), cat([-back_i, back_r], 1)], 0)
    on_f = cols(hr[:, 64:128], hi[:, 64:128], fm)
    on_b = cols(gr[:, :64], gi[:, :64], bm)
    add_r = cat([on_b[:, :64], on_f[:, :64]], 1)
    add_i = cat([on_b[:, 64:], on_f[:, 64:]], 1)
    lr, li = -hi * d, hr * d
    lr = cat([lr[:, :128] + add_r, lr[:, 128:]], 1)
    li = cat([li[:, :128] + add_i, li[:, 128:]], 1)
    nr, ni = right_adj(lr, li, gr, gi)
    return nr - nr.T, ni + ni.T


VM = pl.BlockSpec(memory_space=pltpu.VMEM)
SM = pl.BlockSpec(memory_space=pltpu.SMEM)


def call(kernel, outs, specs, micros, scratch=()):
    return pl.pallas_call(
        kernel,
        out_shape=[jax.ShapeDtypeStruct(o, F32) for o in outs],
        in_specs=specs,
        out_specs=[VM] * len(outs),
        scratch_shapes=list(scratch),
        compiler_params=pltpu.CompilerParams(vmem_limit_bytes=40 * 2**20),
        cost_estimate=pl.CostEstimate(flops=int(micros * 1.1e9), bytes_accessed=1 << 20, transcendentals=0),
    )


def put(ref, values):
    for k, v in enumerate(values):
        ref[k] = v


def eliminate_kernel(detune, hop, s, inner, y, z):
    def run(inverses):
        s[...], inner[...], y[...], z[...] = eliminate_body(inverses, detune[...], (hop[0, 0], hop[1, 0]))

    guarded(run)


def maps_kernel(slab, s, couple, next_couple, inject, sends, raw, inject_out):
    inject_out[...] = inject[:, 0]
    chip, core = slab[0] // 2, lax.rem(slab[0], 2)

    def run(inverses):
        left, right, own = maps_body(inverses, slab[0], s[...], (couple[0, 0], couple[1, 0]), (next_couple[0, 0], next_couple[1, 0]))
        put(raw, own)
        for t in range(4):
            put(sends.at[t], choose((chip < t) | ((chip == t) & (core == 0)), left, right))

    guarded(run)


def put_rows(ref, r, i):
    even, odd = for_rows(r, i)
    ref[:, 0] = even
    ref[:, 1] = odd


def close_kernel(
    slab, couple, next_couple, inject, near, far, s, inner, y, z, raw, rows, big, small, parts, kept
):
    me = slab[0]
    own_couple = (couple[0, 0], couple[1, 0])

    def sent(t):
        same = lax.rem(t, 2) == lax.rem(me, 2)
        return [jnp.where(same, near[t // 2, k], far[t // 2, k]) for k in range(4)]

    def run(inverses):
        def get(t):
            return [kept[t, k] for k in range(4)]

        sig_l, sig_r = tree_body(inverses, me, sent, lambda k, m: put(kept.at[k], m), get)
        own = [raw[k] for k in range(4)]
        whole, corner = close_body(
            inverses, me, own_couple, sig_l, sig_r, s[...], inner[...], y[...], z[...], own
        )
        big[...], small[...] = whole, corner
        put(parts, lesser_parts_body(me, whole, corner, y[...], inject[...], own_couple, (next_couple[0, 0], next_couple[1, 0])))
        put_rows(rows, *restore(whole, inner[...], y[...], z[...]))

    guarded(run)


def lesser_kernel(slab, couple, near, far, big, small, inner, y, z, inject, rows):
    me = slab[0]

    def parts(t, k):
        d = lax.rem(t // 2 - me // 2 + 4, 4)
        return jnp.where(lax.rem(me, 2) == t % 2, near[d, k], far[d, k])

    r, i = lesser_body(
        me,
        (couple[0, 0], couple[1, 0]),
        parts,
        big[...],
        small[...],
        inner[...],
        y[...],
        z[...],
        inject[...],
    )
    put_rows(rows, r, i)


def convolve_kernel(table, piece, out):
    for j in range(4):
        x = cat([piece[:, j], piece[:, 4 + j]], 0)
        o = mm(table[...], x)
        out[0, 0, :, j] = o[:64]
        out[1, 0, :, j] = o[64:]


def tables_kernel(kern, out):
    for k in range(2):
        t = []
        for c in range(2):
            x = jnp.broadcast_to(kern[k, c : c + 1, :], (64, 128))
            t.append(pltpu.roll(x, 65, 1, stride=1, stride_axis=0)[:, :64])
        out[k] = blk(t[0], t[1])


def per_device(energies, onsite, hopping, coupling, injection, kernels):
    slab = lax.axis_index("slab").astype(jnp.int32).reshape(1)

    def swapped_over(x, axis):
        return lax.all_to_all(x, axis, split_axis=0, concat_axis=0, tiled=True)

    next_couple = lax.ppermute(coupling, "slab", [(t, (t + 7) % 8) for t in range(8)])
    m256, half = (256, 256), (128, 256)
    port = (4, 64, 128)
    s, inner, y, z = call(eliminate_kernel, [m256, half, m256, half], [VM, VM], 6)(energies[:, None] - onsite, hopping)
    sends, raw, inject = call(maps_kernel, [(4, *port), port, (1, 256)], [SM] + [VM] * 4, 5)(
        slab, s, coupling, next_couple, injection
    )
    near = lax.all_to_all(
        sends, "slab", split_axis=0, concat_axis=0, tiled=True, axis_index_groups=[[0, 2, 4, 6], [1, 3, 5, 7]]
    )
    far = lax.ppermute(near, "slab", [(t, t ^ 1) for t in range(8)])
    rows, big, small, parts = call(
        close_kernel,
        [(32, 2, 8, 256), half, half, (5, 64, 128)],
        [SM] + [VM] * 10,
        25,
        [pltpu.VMEM((6, 4, 64, 128), F32)],
    )(slab, coupling, next_couple, inject, near, far, s, inner, y, z, raw)

    def to_rows(x):
        return swapped_over(x.reshape(64, 8, 256), "energy")

    got_r = to_rows(rows)
    near_parts = jnp.stack(
        [parts] + [lax.ppermute(parts, "slab", [(t, (t - 2 * d) % 8) for t in range(8)]) for d in (1, 2, 3)]
    )
    far_parts = lax.ppermute(near_parts, "slab", [(t, t ^ 1) for t in range(8)])
    late_kernels, _ = lax.optimization_barrier((kernels, parts))
    reversed_kernels = jnp.pad(late_kernels[:, :, ::-1], ((0, 0), (0, 0), (0, 1)))
    (tables,) = call(tables_kernel, [(2, 128, 128)], [VM], 1)(reversed_kernels)
    (rows_l,) = call(lesser_kernel, [(32, 2, 8, 256)], [SM] + [VM] * 9, 8)(
        slab, coupling, near_parts, far_parts, big, small, inner, y, z, inject
    )
    got_l = to_rows(rows_l)
    conv = call(convolve_kernel, [(2, 1, 64, 4, 256)], [VM] * 2, 2)
    return conv(tables[0], got_r)[0], conv(tables[1], got_l)[0]


def solution(mesh):
    in_specs = (
        P("energy"),
        P("slab", None),
        P(None, "slab", None, None),
        P(None, "slab", None, None),
        P("energy", "slab", None),
        P(),
    )
    out_specs = (P(None, "slab", None, "energy", None), P(None, "slab", None, "energy", None))
    return jax.shard_map(per_device, mesh=mesh, in_specs=in_specs, out_specs=out_specs, check_vma=False)
```

```python
import functools

import jax
import jax.numpy as jnp
from jax import lax
from jax.experimental import pallas as pl
from jax.experimental.pallas import tpu as pltpu
from jax.sharding import PartitionSpec as P

ETA = 0.02
F32 = jnp.float32
BF16 = jnp.bfloat16
NN = (((1,), (0,)), ((), ()))
NT = (((1,), (1,)), ((), ()))


def mmh(a, b, dims=NN):
    return lax.dot_general(a, b, dims, precision=lax.Precision.HIGHEST, preferred_element_type=F32)


def halves(x):
    high = x.astype(BF16)
    return high, (x - high.astype(F32)).astype(BF16)


def mm1(a, b, dims=NN):
    return lax.dot_general(a, b, dims, preferred_element_type=F32)


def mm3(a, b, dims=NN):
    return mm1(a[0], b[0], dims) + (mm1(a[0], b[1], dims) + mm1(a[1], b[0], dims))


def mm(a, b, dims=NN):
    return mm3(halves(a), halves(b), dims)


def cat(parts, axis):
    return jnp.concatenate(parts, axis=axis)


def blk(r, i):
    return cat([cat([r, -i], 1), cat([i, r], 1)], 0)


def pair(z):
    n = z.shape[1] // 2
    return z[:n, :n], -z[:n, n:]


def full(top):
    n = top.shape[0]
    return cat([top, cat([-top[:, n:], top[:, :n]], 1)], 0)


def eye(n):
    return (lax.broadcasted_iota(jnp.int32, (n, n), 0) == lax.broadcasted_iota(jnp.int32, (n, n), 1)).astype(F32)


def imag_eye(n):
    return blk(jnp.zeros((n, n), F32), eye(n))


def times_i(z):
    n = z.shape[0] // 2
    return cat([-z[n:], z[:n]], 0)


def lowest(values):
    return functools.reduce(jnp.minimum, values)


def scaled(low, floor):
    base = jnp.maximum(low, floor)
    shift = 1.0 + base
    gain = 4.0 / (shift * shift)
    return shift, gain, jnp.minimum(gain * low * (shift - low), gain * base)


ENOUGH = 2e-4


def corrected(mats, xs):
    rs = [eye(z.shape[0]) - mmh(z, x) for z, x in zip(mats, xs)]
    size = functools.reduce(jnp.maximum, [jnp.sum(r * r) for r in rs])
    return size, tuple(x + mm1(x.astype(BF16), r.astype(BF16)) for x, r in zip(xs, rs))


def bound(z):
    zb = z.astype(BF16)
    w = mm1(zb, zb, NT)
    return 1.0 / (1.01 * jnp.max(jnp.sum(jnp.abs(w), axis=1, keepdims=True))), w, z.T


FLOOR = 0.035


def last_steps():
    low = FLOOR
    for _ in range(4):
        shift = 1.0 + low
        gain = 4.0 / (shift * shift)
        yield shift, gain
        low *= gain


def quick(sizes):
    def inverses(mats, factor=2.0):
        eyes = [eye(z.shape[0]) for z in mats]
        parts = [halves(z) for z in mats]
        shift = 1.0 + FLOOR
        gain = 4.0 / (shift * shift)
        lows, guesses = [], []
        for z, one in zip(mats, eyes):
            inv_u, w, zt = bound(z)
            r = shift * one - w * inv_u
            guesses.append(((gain * inv_u) * mm1(zt.astype(BF16), r.astype(BF16))).astype(BF16))
            lows.append((factor * ETA * ETA) * inv_u)
        low = lowest(lows)
        rise = gain * (shift - FLOOR)
        count = sum((low < FLOOR * rise**-k).astype(jnp.int32) for k in range(1, 20))

        def step(shift, gain, guesses):
            rs = [(shift * one - mm1(p[0], x)).astype(BF16) for p, one, x in zip(parts, eyes, guesses)]
            return tuple((gain * mm1(x, r)).astype(BF16) for x, r in zip(guesses, rs))

        guesses = lax.fori_loop(0, count, lambda _, xs: step(shift, gain, xs), tuple(guesses))
        for late_shift, late_gain in last_steps():
            guesses = step(late_shift, late_gain, guesses)
        better = []
        for (zh, zl), one, x in zip(parts, eyes, guesses):
            rh, rl = halves(one - (mm1(zh, x) + mm1(zl, x)))
            better.append(x.astype(F32) + (mm1(x, rh) + mm1(x, rl)))
        size, better = corrected(mats, better)
        sizes.append(size)
        return better

    return inverses


def careful(mats, factor=1.0):
    n = len(mats)
    eyes = [eye(z.shape[0]) for z in mats]
    parts = [halves(z) for z in mats]
    lows, xs = [], []
    for z in mats:
        inv_u, _, zt = bound(z)
        lows.append((ETA * ETA) * inv_u)
        xs.append(zt * inv_u)

    def step(state):
        lows, xs = state
        plans = [scaled(low, 1e-3) for low in lows]
        new = []
        for k in range(n):
            xp = halves(xs[k])
            r = plans[k][0] * eyes[k] - mm3(parts[k], xp)
            new.append(plans[k][1] * mm3(xp, halves(r)))
        return tuple(p[2] for p in plans), tuple(new)

    _, xs = lax.while_loop(lambda state: lowest(state[0]) < 0.999, step, (tuple(lows), tuple(xs)))

    def again(state):
        count, size, _ = state
        return (count < 8) & jnp.logical_not(size <= ENOUGH)

    def more(state):
        count, _, xs = state
        size, xs = corrected(mats, xs)
        return count + 1, size, xs

    size, xs = corrected(mats, xs)
    return lax.while_loop(again, more, (jnp.int32(0), size, xs))[2]


def guarded(run):
    sizes = []
    run(quick(sizes))

    @pl.when(jnp.logical_not(functools.reduce(jnp.maximum, sizes) <= ENOUGH))
    def _():
        run(careful)


def rolled(x, axis):
    n = x.shape[axis]
    if axis == 0:
        return cat([x[n - 64 :], x[: n - 64]], 0)
    return cat([x[:, n - 64 :], x[:, : n - 64]], 1)


def unrolled(x, axis):
    if axis == 0:
        return cat([x[64:], x[:64]], 0)
    return cat([x[:, 64:], x[:, :64]], 1)


def eliminate_body(inverses, detune, hop):
    h0 = rolled(rolled(hop[0], 0), 1)
    h1 = rolled(rolled(hop[1], 0), 1)
    one = eye(256)
    ar = one * rolled(detune, 1) - (h0 + h0.T) * 0.5
    ai = one * ETA - (h1 - h1.T) * 0.5

    def part(rows, cols):
        return blk(ar[rows, cols], ai[rows, cols])

    b, i = slice(0, 128), slice(128, 256)
    (inner,) = inverses([part(i, i)], 1.0)
    abi = part(b, i)
    y = mm(abi, inner)
    z = mm(inner, part(i, b))
    s = part(b, b) - mm(abi, z)
    return s, inner[:128], y, z[:128]


def corners(s):
    r, i = pair(s)
    lo, hi = slice(0, 64), slice(64, 128)
    return [[blk(r[p, q], i[p, q]) for q in (lo, hi)] for p in (lo, hi)]


def lead_of(slab, c):
    return jnp.where(slab == 0, mm(c, c, NT), 0.0)


def maps_body(inverses, slab, s, couple, next_couple):
    (bb, bf), (fb, ff) = corners(s)
    c = blk(couple[0], couple[1])
    cn = blk(next_couple[0], next_couple[1])
    ff = ff + times_i(lead_of(slab, c))
    ib, if_ = inverses([bb, ff])
    b = -mm(ib, bf)
    d = -mm(fb, ib)
    phi = ff + mm(d, bf)
    br = -mm(if_, fb)
    dr = -mm(bf, if_)
    psi = bb + mm(dr, fb)
    ct = c.T
    cnt = cn.T
    left = [mm(mm(cn, ib), cnt), mm(cn, b), mm(d, cnt), phi]
    right = [mm(mm(ct, if_), c), mm(ct, br), mm(dr, c), psi]
    raw = [ib, b, d, phi]
    return [u[:64] for u in left], [u[:64] for u in right], [u[:64] for u in raw]


def compose(outer, inner, phi_inv):
    a2, b2, d2, _ = outer
    a1, b1, d1, phi1 = inner
    pq = mm(phi_inv, cat([b1, d2], 1))
    quad = mm(cat([b2, d1], 0), pq)
    n = a1.shape[0]
    return [a2 + quad[:n, n:], quad[:n, :n], quad[n:, n:], phi1 - quad[n:, :n]]


def level(inverses, slots):
    phis = inverses([outer[3] - inner[0] for outer, inner in slots])
    return [[u[:64] for u in compose(o, i, p)] for (o, i), p in zip(slots, phis)]


def constant_map(value):
    zero = jnp.zeros_like(value)
    return [value, zero, zero, imag_eye(64)]


def choose(cond, one, other):
    return [jnp.where(cond, x, y) for x, y in zip(one, other)]


def tree_body(inverses, slab, sent, put, get):
    none = constant_map(jnp.zeros((128, 128), F32))

    def wide(tops):
        return [full(u) for u in tops]

    lefts = (slab + 1) // 2

    def fetch(is_left, place):
        source = jnp.where(is_left, slab - 1 - place, slab + 1 + place)
        there = (source >= 0) & (source < 8)
        return choose(there, wide(sent(jnp.clip(source, 0, 7))), none)

    slots = []
    for k in range(4):
        is_left = k < lefts
        place = 2 * jnp.where(is_left, k, k - lefts)
        slots.append((fetch(is_left, place), fetch(is_left, place + 1)))
    for k, m in enumerate(level(inverses, slots)):
        put(k, m)

    skip = jnp.where(lefts == 1, 1, 0)
    last = choose(lax.rem(lefts, 2) == 0, wide(get(3)), none)
    slots = [(wide(get(skip)), wide(get(skip + 1))), (wide(get(skip + 2)), last)]
    for k, m in enumerate(level(inverses, slots)):
        put(4 + k, m)

    second = wide(get(5))
    left = choose(lefts == 0, none, wide(get(jnp.where(lefts == 1, 0, 4))))
    right = choose(lefts == 4, none, wide(get(jnp.where(lefts == 3, 3, jnp.where(lefts == 2, 5, 4)))))
    slots = [(left, choose(lefts >= 3, second, none)), (right, choose(lefts <= 1, second, none))]
    phis = inverses([outer[3] - inner[0] for outer, inner in slots])
    return [o[0] + mm(mm(o[1], p), o[2]) for (o, _), p in zip(slots, phis)]


def close_body(inverses, slab, couple, sig_l, sig_r, s, inner, y, z, raw):
    ib, b, d, phi = [full(u) for u in raw]
    lr, li = pair(sig_l - times_i(lead_of(slab, blk(couple[0], couple[1]))))
    rr, ri = pair(sig_r)
    zero = jnp.zeros((64, 64), F32)

    def spread(x, w):
        return cat([cat([x, zero], 1), cat([zero, w], 1)], 0)

    closed = s - blk(spread(rr, lr), spread(ri, li))
    e_inv, big = inverses([phi - sig_l, closed])
    be = mm(b, e_inv)
    gfb = mm(e_inv, d)
    gbb = ib + mm(be, d)

    def joined(k):
        return cat([cat([pair(gbb)[k], pair(be)[k]], 1), cat([pair(gfb)[k], pair(e_inv)[k]], 1)], 0)

    small = cat([joined(0), -joined(1)], 1)
    return big[:128], small


def restore(top, inner, y, z):
    ty = mm(top, y)
    zt = mm(z, full(top))
    zty = mm(zt, y)
    low = inner + zty
    r = cat([cat([top[:, :128], -ty[:, :128]], 1), cat([-zt[:, :128], low[:, :128]], 1)], 0)
    i = cat([cat([-top[:, 128:], ty[:, 128:]], 1), cat([zt[:, 128:], -low[:, 128:]], 1)], 0)
    return r, i


def for_rows(r, i):
    r, i = [unrolled(unrolled(x, 0), 1).reshape(32, 8, 256) for x in (r, i)]
    upper = lax.broadcasted_iota(jnp.int32, (32, 8, 256), 1) < 4

    def swapped(x):
        return cat([x[:, 4:], x[:, :4]], 1)

    even = jnp.where(upper, r, swapped(i))
    odd = jnp.where(upper, swapped(r), i)
    return even, odd


def right_adj(lr, li, gr, gi):
    n = lr.shape[0]
    rows = cat([cat([lr, li], 1), cat([li, -lr], 1)], 0)
    out = mm(rows, cat([gr, gi], 1), NT)
    return out[:n], out[n:]


def lesser_parts_body(slab, big, small, y, inject, couple, next_couple):
    rest = mm(cat([small, big], 0), y)
    gr, gi = cat([small[:, :128], -rest[:128, :128]], 1), cat([-small[:, 128:], rest[:128, 128:]], 1)
    fr, fi = cat([big[:, :128], -rest[128:, :128]], 1), cat([-big[:, 128:], rest[128:, 128:]], 1)
    hr, hi = 1.5 * gr - fr, 1.5 * gi - fi
    d = rolled(inject, 1)
    lr = cat([gr[:64], hr[64:]], 0) * d
    li = cat([gi[:64], hi[64:]], 0) * d
    mr, mi = right_adj(lr, li, gr, gi)
    c = blk(couple[0], couple[1])
    cn = blk(next_couple[0], next_couple[1])
    ct, cnt = c.T, cn.T
    w = mm(mm(cn, blk(-mi[:64, :64], mr[:64, :64])), cnt)
    beta = mm(cn, blk(gr[:64, 64:128], gi[:64, 64:128]))
    w = w + mm(mm(beta, times_i(lead_of(slab, c))), beta, NT)
    w = (w - w.T) * 0.5
    q = mm(mm(ct, blk(-mi[64:, 64:], mr[64:, 64:])), c)
    q = q - q.T
    left = mm(
        ct,
        cat(
            [
                blk(gr[64:128, 64:128], gi[64:128, 64:128]),
                blk(hr[64:128, 64:128], hi[64:128, 64:128]),
                blk(gr[64:128, :64], gi[64:128, :64]),
            ],
            1,
        ),
    )
    u, v, zz = left[:, :128], left[:, 128:256], left[:, 256:]
    return [m[:64] for m in (w + times_i(q), beta, u, v, zz)]


def lesser_body(slab, couple, parts, big, small, inner, y, z, inject):
    mine = times_i(lead_of(slab, blk(couple[0], couple[1])))
    sources = {}
    packed = [full(parts(t, 0)) for t in range(8)]
    for t in range(8):
        if t:
            beta = full(parts(t - 1, 1))
            both = packed[t - 1]
            w = (both - both.T) * 0.5
            sig = w + mm(mm(beta, sig), beta, NT) if t > 1 else w
            mine = jnp.where(slab == t, sig, mine)
            c = mm(mm(full(parts(t, 3)), sig), full(parts(t, 2)), NT)
            sources[t] = c - c.T - times_i((packed[t] + packed[t].T) * 0.5)
    back = jnp.zeros_like(sig)
    my_back = back
    for t in range(7, 0, -1):
        zz = full(parts(t, 4))
        back = sources[t] + mm(mm(zz, back), zz, NT)
        my_back = jnp.where(slab == t - 1, back, my_back)
    gr, gi = restore(small, inner, y, z)
    fr, fi = restore(big, inner, y, z)
    hr, hi = 1.5 * gr - fr, 1.5 * gi - fi
    d = rolled(inject, 1)
    right_r, right_i = pair(mine)
    back_r, back_i = pair(0.5 * my_back)

    def cols(xr, xi, m):
        out = mm(cat([xr, xi], 1), m)
        return out

    fm = cat([cat([right_r, right_i], 1), cat([-right_i, right_r], 1)], 0)
    bm = cat([cat([back_r, back_i], 1), cat([-back_i, back_r], 1)], 0)
    on_f = cols(hr[:, 64:128], hi[:, 64:128], fm)
    on_b = cols(gr[:, :64], gi[:, :64], bm)
    add_r = cat([on_b[:, :64], on_f[:, :64]], 1)
    add_i = cat([on_b[:, 64:], on_f[:, 64:]], 1)
    lr, li = -hi * d, hr * d
    lr = cat([lr[:, :128] + add_r, lr[:, 128:]], 1)
    li = cat([li[:, :128] + add_i, li[:, 128:]], 1)
    nr, ni = right_adj(lr, li, gr, gi)
    return nr - nr.T, ni + ni.T


VM = pl.BlockSpec(memory_space=pltpu.VMEM)
SM = pl.BlockSpec(memory_space=pltpu.SMEM)


def call(kernel, outs, specs, micros, scratch=()):
    return pl.pallas_call(
        kernel,
        out_shape=[jax.ShapeDtypeStruct(o, F32) for o in outs],
        in_specs=specs,
        out_specs=[VM] * len(outs),
        scratch_shapes=list(scratch),
        compiler_params=pltpu.CompilerParams(vmem_limit_bytes=40 * 2**20),
        cost_estimate=pl.CostEstimate(flops=int(micros * 1.1e9), bytes_accessed=1 << 20, transcendentals=0),
    )


def put(ref, values):
    for k, v in enumerate(values):
        ref[k] = v


def eliminate_kernel(detune, hop, s, inner, y, z):
    def run(inverses):
        s[...], inner[...], y[...], z[...] = eliminate_body(inverses, detune[...], (hop[0, 0], hop[1, 0]))

    guarded(run)


def maps_kernel(slab, s, couple, next_couple, sends, raw):
    chip, core = slab[0] // 2, lax.rem(slab[0], 2)

    def run(inverses):
        left, right, own = maps_body(inverses, slab[0], s[...], (couple[0, 0], couple[1, 0]), (next_couple[0, 0], next_couple[1, 0]))
        put(raw, own)
        for t in range(4):
            put(sends.at[t], choose((chip < t) | ((chip == t) & (core == 0)), left, right))

    guarded(run)


def put_rows(ref, r, i):
    even, odd = for_rows(r, i)
    ref[:, 0] = even
    ref[:, 1] = odd


def close_kernel(
    slab, couple, next_couple, inject, near, far, s, inner, y, z, raw, rows, big, small, parts, kept
):
    me = slab[0]
    own_couple = (couple[0, 0], couple[1, 0])

    def sent(t):
        same = lax.rem(t, 2) == lax.rem(me, 2)
        return [jnp.where(same, near[t // 2, k], far[t // 2, k]) for k in range(4)]

    def run(inverses):
        def get(t):
            return [kept[t, k] for k in range(4)]

        sig_l, sig_r = tree_body(inverses, me, sent, lambda k, m: put(kept.at[k], m), get)
        own = [raw[k] for k in range(4)]
        whole, corner = close_body(
            inverses, me, own_couple, sig_l, sig_r, s[...], inner[...], y[...], z[...], own
        )
        big[...], small[...] = whole, corner
        put(parts, lesser_parts_body(me, whole, corner, y[...], inject[:, 0], own_couple, (next_couple[0, 0], next_couple[1, 0])))
        put_rows(rows, *restore(whole, inner[...], y[...], z[...]))

    guarded(run)


def lesser_kernel(slab, couple, near, far, big, small, inner, y, z, inject, rows):
    me = slab[0]

    def parts(t, k):
        d = lax.rem(t // 2 - me // 2 + 4, 4)
        return jnp.where(lax.rem(me, 2) == t % 2, near[d, k], far[d, k])

    r, i = lesser_body(
        me,
        (couple[0, 0], couple[1, 0]),
        parts,
        big[...],
        small[...],
        inner[...],
        y[...],
        z[...],
        inject[:, 0],
    )
    put_rows(rows, r, i)


def convolve_kernel(table, piece, out):
    for j in range(4):
        x = cat([piece[:, j], piece[:, 4 + j]], 0)
        o = mm(table[...], x)
        out[0, 0, :, j] = o[:64]
        out[1, 0, :, j] = o[64:]


def tables_kernel(kern, out):
    for k in range(2):
        t = []
        for c in range(2):
            x = jnp.broadcast_to(kern[k, c : c + 1, :], (64, 128))
            t.append(pltpu.roll(x, 65, 1, stride=1, stride_axis=0)[:, :64])
        out[k] = blk(t[0], t[1])


def per_device(energies, onsite, hopping, coupling, injection, kernels):
    slab = lax.axis_index("slab").astype(jnp.int32).reshape(1)

    def swapped_over(x, axis):
        return lax.all_to_all(x, axis, split_axis=0, concat_axis=0, tiled=True)

    next_couple = lax.ppermute(coupling, "slab", [(t, (t + 7) % 8) for t in range(8)])
    m256, half = (256, 256), (128, 256)
    port = (4, 64, 128)
    s, inner, y, z = call(eliminate_kernel, [m256, half, m256, half], [VM, VM], 6)(energies[:, None] - onsite, hopping)
    sends, raw = call(maps_kernel, [(4, *port), port], [SM] + [VM] * 3, 5)(slab, s, coupling, next_couple)
    near = lax.all_to_all(
        sends, "slab", split_axis=0, concat_axis=0, tiled=True, axis_index_groups=[[0, 2, 4, 6], [1, 3, 5, 7]]
    )
    far = lax.ppermute(near, "slab", [(t, t ^ 1) for t in range(8)])
    rows, big, small, parts = call(
        close_kernel,
        [(32, 2, 8, 256), half, half, (5, 64, 128)],
        [SM] + [VM] * 10,
        25,
        [pltpu.VMEM((6, 4, 64, 128), F32)],
    )(slab, coupling, next_couple, injection, near, far, s, inner, y, z, raw)

    def to_rows(x):
        return swapped_over(x.reshape(64, 8, 256), "energy")

    got_r = to_rows(rows)
    near_parts = jnp.stack(
        [parts] + [lax.ppermute(parts, "slab", [(t, (t - 2 * d) % 8) for t in range(8)]) for d in (1, 2, 3)]
    )
    far_parts = lax.ppermute(near_parts, "slab", [(t, t ^ 1) for t in range(8)])
    late_kernels, _ = lax.optimization_barrier((kernels, parts))
    reversed_kernels = jnp.pad(late_kernels[:, :, ::-1], ((0, 0), (0, 0), (0, 1)))
    (tables,) = call(tables_kernel, [(2, 128, 128)], [VM], 1)(reversed_kernels)
    (rows_l,) = call(lesser_kernel, [(32, 2, 8, 256)], [SM] + [VM] * 9, 8)(
        slab, coupling, near_parts, far_parts, big, small, inner, y, z, injection
    )
    got_l = to_rows(rows_l)
    conv = call(convolve_kernel, [(2, 1, 64, 4, 256)], [VM] * 2, 2)
    return conv(tables[0], got_r)[0], conv(tables[1], got_l)[0]


def solution(mesh):
    in_specs = (
        P("energy"),
        P("slab", None),
        P(None, "slab", None, None),
        P(None, "slab", None, None),
        P("energy", "slab", None),
        P(),
    )
    out_specs = (P(None, "slab", None, "energy", None), P(None, "slab", None, "energy", None))
    return jax.shard_map(per_device, mesh=mesh, in_specs=in_specs, out_specs=out_specs, check_vma=False)
```
